32 devices in a mesh: gx: 8 (over z, core), gy: 4 (over y, x).
Axes of the slice: x: 2, y: 2, z: 4, core: 2. Of those that a mesh axis runs over, the one named last changes fastest.
Arguments:
- positions: float32 [3, 2048], P(None, ('gx', 'gy')), may hold values from -6 to 6
- block_prev: float32 [32, 3, 2048], P(None, None, ('gx', 'gy')), may hold values from -6 to 6
- block_cur: float32 [32, 3, 2048], P(None, None, ('gx', 'gy')), may hold values from -6 to 6
- neighbours: int32 [32, 2048], P(None, ('gx', 'gy')), may hold values from 0 to 319
- counts: int32 [2048], P(('gx', 'gy')), may hold values from 1 to 32
- x_lists: int32 [32, 2, 64], P(('gx', 'gy')), may hold values from 0 to 63, as said below
- y_lists: int32 [32, 2, 64], P(('gx', 'gy')), may hold values from 0 to 191, as said below
- w_radial: float32 [8, 128], replicated, may hold values from -0.375 to 0.375
- w_vector: float32 [8, 128], replicated, may hold values from -1.5 to 1.5
- w_mix: float32 [128, 128], replicated, may hold values from -0.5 to 0.5
- w_out: float32 [128], replicated, may hold values from -0.5 to 0.5
Outputs:
- new_blocks: float32 [2, 32, 3, 2048], P(None, None, None, ('gx', 'gy'))
- factors: float32 [2, 32, 32], replicated
The draws below stay inside these ranges and needn't reach their ends.
Inputs may be any that keep to these rules, and one draw needn't show every extreme that they name: `x_lists`: the two lists of a domain each hold distinct indices of the domain's own atoms. `y_lists`: the two lists of a domain each hold distinct indices into the domain's widened atoms (own atoms, then the two received gx lists).
All inputs are finite; a program needn't handle non-finite values.
Results may differ from the reference program's by a relative error of at most 0.0003.
Values sent between devices are 32-bit elements; how exact they have to be, the bound alone decides.
No kernel may reach another device: no remote copies, remote signals or barrier semaphores. Data moves between devices by JAX's collectives and lax.ppermute only.
A program may use at most 64 MiB of HBM per device.

```python
import jax
import jax.numpy as jnp
from jax import lax

VECTORS = 32
CHANNELS = 128
BASIS_SIZE = 8
SLOT_COUNT = 32
LANCZOS_STEPS = 2
ATOMS_DEV = 64
HALO_ATOMS = 64
EXTENDED = 320
DOMAINS = 32
ATOM_TOTAL = 2048
N_GX = 8
N_GY = 4


def draw_x_lists(key, part):
    subkeys = jax.random.split(jax.random.fold_in(key, 11), DOMAINS * 2)
    picked = jax.vmap(lambda subkey: jax.random.permutation(subkey, ATOMS_DEV)[:HALO_ATOMS])(subkeys)
    return picked.reshape(DOMAINS, 2, HALO_ATOMS).astype(jnp.int32)


def draw_y_lists(key, part):
    subkeys = jax.random.split(jax.random.fold_in(key, 23), DOMAINS * 2)
    picked = jax.vmap(lambda subkey: jax.random.permutation(subkey, ATOMS_DEV + 2 * HALO_ATOMS)[:HALO_ATOMS])(subkeys)
    return picked.reshape(DOMAINS, 2, HALO_ATOMS).astype(jnp.int32)


def set_ends(values, key, least, largest):
    dims = values.shape
    index_at = [jax.random.randint(jax.random.fold_in(key, axis), (), 0, dims[axis]) for axis in range(len(dims))]
    values = values.at[tuple(index_at)].set(least)
    longest = dims.index(max(dims))
    index_at[longest] = (index_at[longest] + 1) % dims[longest]
    return values.at[tuple(index_at)].set(largest)


def block_levels(key, extent, cuts, least, high):
    gain, own = 1.0, jax.random.fold_in(key, 6)
    for position, parts in cuts:
        steps = jnp.exp(jax.random.uniform(jax.random.fold_in(own, position), (parts,), jnp.float32, least / len(cuts), high / len(cuts)))
        gain = gain * jnp.repeat(steps, extent[position] // parts).reshape([-1 if axis == position else 1 for axis in range(len(extent))])
    return gain


def bell_draw(key, dims, scale, limit, cuts=(), kind=jnp.bfloat16):
    array = scale * jax.random.normal(key, dims, jnp.float32)
    if cuts:
        array = array * block_levels(key, dims, cuts, -0.22, 0.18)
    return jnp.clip(array, -limit, limit).astype(kind)


def setup_inputs(seed: int = 0) -> dict:
    arg_keys = jax.random.split(jax.random.key(seed), 12)
    return {
        "positions": bell_draw(arg_keys[0], (3, ATOM_TOTAL), 1.2, 6.0, ((1, 32),), jnp.float32),
        "block_prev": bell_draw(arg_keys[1], (VECTORS, 3, ATOM_TOTAL), 1.0, 6.0, ((2, 32),), jnp.float32),
        "block_cur": bell_draw(arg_keys[2], (VECTORS, 3, ATOM_TOTAL), 1.0, 6.0, ((2, 32),), jnp.float32),
        "neighbours": set_ends(jax.random.randint(arg_keys[3], (SLOT_COUNT, ATOM_TOTAL), 0, EXTENDED), jax.random.fold_in(arg_keys[3], 1), 0, EXTENDED - 1).astype(jnp.int32),
        "counts": set_ends(jax.random.randint(arg_keys[4], (ATOM_TOTAL,), 1, SLOT_COUNT + 1), jax.random.fold_in(arg_keys[4], 1), 1, SLOT_COUNT).astype(jnp.int32),
        "x_lists": draw_x_lists(jax.random.fold_in(arg_keys[11], 71), 0),
        "y_lists": draw_y_lists(jax.random.fold_in(arg_keys[11], 71), 0),
        "w_radial": bell_draw(arg_keys[7], (BASIS_SIZE, CHANNELS), (BASIS_SIZE * SLOT_COUNT) ** -0.5, 0.375, (), jnp.float32),
        "w_vector": bell_draw(arg_keys[8], (BASIS_SIZE, CHANNELS), (2 * BASIS_SIZE) ** -0.5, 1.5, (), jnp.float32),
        "w_mix": bell_draw(arg_keys[9], (CHANNELS, CHANNELS), CHANNELS ** -0.5, 0.5, (), jnp.float32),
        "w_out": bell_draw(arg_keys[10], (CHANNELS,), CHANNELS ** -0.5, 0.5, (), jnp.float32),
    }


EXACT_DOT = lax.Precision.HIGHEST
SOFTEN = 0.25
CUTOFF = 5.0
GAUSS_WIDTH = 2.0

def edge_terms(vector):
    squared = jnp.sum(vector * vector) + SOFTEN
    radius = jnp.sqrt(squared)
    heading = vector / radius
    envelope = jnp.maximum(1.0 - squared / (CUTOFF * CUTOFF), 0.0) ** 3
    centers = CUTOFF * (jnp.arange(BASIS_SIZE, dtype=jnp.float32) + 0.5) / BASIS_SIZE
    radial = jnp.exp(-GAUSS_WIDTH * (radius - centers) ** 2) * envelope
    return jnp.concatenate([radial, radial * heading[0], radial * heading[1], radial * heading[2]])

def weighted_terms(vector, coeffs):
    return jnp.sum(coeffs * edge_terms(vector))

def edge_jacobian(vector):
    columns = jax.vmap(lambda tangent: jax.jvp(edge_terms, (vector,), (tangent,))[1])(jnp.eye(3, dtype=vector.dtype))
    return columns.T

def edge_curvature(vector, coeffs):
    slope = jax.grad(weighted_terms)
    ignored, pullback = jax.vjp(lambda point: slope(point, coeffs), vector)
    return jax.vmap(lambda row: pullback(row)[0])(jnp.eye(3, dtype=vector.dtype))

def atom_energy(descriptor, weights):
    w_radial, w_vector, w_mix, w_out = weights
    scalar = jnp.einsum('ka,kc->ac', descriptor[0], w_radial, precision=EXACT_DOT)
    vector_part = jnp.einsum('dka,kc->dac', descriptor[1:], w_vector, precision=EXACT_DOT)
    mixed_in = scalar + lax.optimization_barrier(jnp.sum(vector_part * vector_part, axis=0))
    hidden = jax.nn.silu(jnp.dot(mixed_in, w_mix, precision=EXACT_DOT))
    return jnp.sum(jnp.dot(hidden, w_out, precision=EXACT_DOT))

def prepare(own_pos, ext_pos, neighbours, counts, weights):
    atom_count = own_pos.shape[1]
    slot_count = neighbours.shape[0]
    flat_index = neighbours.reshape(-1)
    deltas = jnp.take(ext_pos, flat_index, axis=1) - jnp.tile(own_pos, (1, slot_count))
    valid_mask = (jnp.arange(slot_count, dtype=jnp.int32)[:, None] < counts[None, :]).astype(jnp.float32).reshape(-1)
    features = jax.vmap(edge_terms, in_axes=1, out_axes=1)(deltas) * valid_mask
    descriptor = lax.optimization_barrier(jnp.sum(features.reshape(4, BASIS_SIZE, slot_count, atom_count), axis=2))
    energy_grad = jax.grad(atom_energy)
    coeffs, pullback = jax.vjp(lambda current: energy_grad(current, weights), descriptor)

    def linearized(tangent):
        return pullback(tangent)[0]
    jacobian = jax.vmap(edge_jacobian, in_axes=1, out_axes=2)(deltas) * valid_mask
    coeff_edges = jnp.tile(coeffs.reshape(4 * BASIS_SIZE, atom_count), (1, slot_count))
    curvature = jax.vmap(edge_curvature, in_axes=(1, 1), out_axes=2)(deltas, coeff_edges) * valid_mask
    return (jacobian, curvature, linearized, flat_index)

def apply_hessian(pieces, tangents, atom_count):
    jacobian, curvature, linearized, flat_index = pieces
    vectors = tangents.shape[0]
    slot_count = flat_index.shape[0] // atom_count
    own_tan = tangents[:, :, :atom_count]
    moved_by = jnp.take(tangents, flat_index, axis=2) - jnp.tile(own_tan, (1, 1, slot_count))
    moved_by = moved_by.reshape(vectors, 3, slot_count, atom_count)
    jac_edges = jacobian.reshape(4 * BASIS_SIZE, 3, slot_count, atom_count)
    curv_edges = curvature.reshape(3, 3, slot_count, atom_count)
    change = jnp.einsum('kcsa,tcsa->tka', jac_edges, moved_by, precision=EXACT_DOT)
    descr_change = change.reshape(vectors, 4, BASIS_SIZE, atom_count)
    coeff_change = jax.vmap(linearized)(descr_change).reshape(vectors, 4 * BASIS_SIZE, atom_count)
    edge_out = jnp.einsum('kcsa,tka->tcsa', jac_edges, coeff_change, precision=EXACT_DOT)
    edge_out = edge_out + jnp.einsum('cgsa,tgsa->tcsa', curv_edges, moved_by, precision=EXACT_DOT)
    result = jnp.zeros_like(tangents).at[:, :, flat_index].add(edge_out.reshape(vectors, 3, slot_count * atom_count))
    return result.at[:, :, :atom_count].add(-lax.optimization_barrier(jnp.sum(edge_out, axis=2)))

def take_rows(data, index):
    return jax.vmap(jax.vmap(lambda block, picks: jnp.take(block, picks, axis=-1)))(data, index)

def add_rows(data, index, extra):
    return jax.vmap(jax.vmap(lambda block, picks, added: block.at[..., picks].add(added)))(data, index, extra)

def extend_all(data, grid_x, grid_y):
    widened = jnp.concatenate([data, jnp.roll(take_rows(data, grid_x[:, :, 0]), 1, axis=0), jnp.roll(take_rows(data, grid_x[:, :, 1]), -1, axis=0)], axis=-1)
    return jnp.concatenate([widened, jnp.roll(take_rows(widened, grid_y[:, :, 0]), 1, axis=1), jnp.roll(take_rows(widened, grid_y[:, :, 1]), -1, axis=1)], axis=-1)

def fold_all(result, grid_x, grid_y, atom_count, halo_rows):
    widened = atom_count + 2 * halo_rows
    buffer = result[..., :widened]
    buffer = add_rows(buffer, grid_y[:, :, 0], jnp.roll(result[..., widened:widened + halo_rows], -1, axis=1))
    buffer = add_rows(buffer, grid_y[:, :, 1], jnp.roll(result[..., widened + halo_rows:], 1, axis=1))
    own_rows = buffer[..., :atom_count]
    own_rows = add_rows(own_rows, grid_x[:, :, 0], jnp.roll(buffer[..., atom_count:atom_count + halo_rows], -1, axis=0))
    own_rows = add_rows(own_rows, grid_x[:, :, 1], jnp.roll(buffer[..., atom_count + halo_rows:widened], 1, axis=0))
    return own_rows

def orthonormal(work_block, newer_block, older_block, total_rows):
    vectors = work_block.shape[0]
    work_flat = work_block.reshape(vectors, -1)
    basis_rows = jnp.concatenate([newer_block.reshape(vectors, -1), older_block.reshape(vectors, -1)], 0)
    projection = jnp.dot(basis_rows, work_flat.T, precision=EXACT_DOT) / total_rows
    residual = work_flat - jnp.dot(projection.T, basis_rows, precision=EXACT_DOT)
    gram_matrix = jnp.dot(residual, residual.T, precision=EXACT_DOT) / total_rows
    lower_factor = jnp.linalg.cholesky(gram_matrix)
    fresh_block = lax.linalg.triangular_solve(lower_factor, residual, left_side=True, lower=True)
    return (fresh_block.reshape(work_block.shape), lower_factor)

def reference(positions, block_prev, block_cur, neighbours, counts, x_lists, y_lists, w_radial, w_vector, w_mix, w_out):
    weights = (w_radial, w_vector, w_mix, w_out)
    grid_x = x_lists.reshape(N_GX, N_GY, 2, HALO_ATOMS)
    grid_y = y_lists.reshape(N_GX, N_GY, 2, HALO_ATOMS)
    pos_grid = positions.reshape(3, N_GX, N_GY, ATOMS_DEV).transpose(1, 2, 0, 3)
    slot_grid = neighbours.reshape(SLOT_COUNT, N_GX, N_GY, ATOMS_DEV).transpose(1, 2, 0, 3).reshape(DOMAINS, SLOT_COUNT, ATOMS_DEV)
    count_grid = counts.reshape(DOMAINS, ATOMS_DEV)
    ext_pos = extend_all(pos_grid, grid_x, grid_y).reshape(DOMAINS, 3, EXTENDED)
    own_pos = pos_grid.reshape(DOMAINS, 3, ATOMS_DEV)

    def one_domain(domain_data):
        own_here, ext_here, tan_here, slots_here, counts_here = domain_data
        pieces = prepare(own_here, ext_here, slots_here, counts_here, weights)
        return apply_hessian(pieces, tan_here, ATOMS_DEV)

    def hessian_of(block):
        block_grid = block.reshape(VECTORS, 3, N_GX, N_GY, ATOMS_DEV).transpose(2, 3, 0, 1, 4)
        ext_tan = extend_all(block_grid, grid_x, grid_y).reshape(DOMAINS, VECTORS, 3, EXTENDED)
        result = lax.map(one_domain, (own_pos, ext_pos, ext_tan, slot_grid, count_grid))
        result = result.reshape(N_GX, N_GY, VECTORS, 3, EXTENDED)
        own_rows = fold_all(result, grid_x, grid_y, ATOMS_DEV, HALO_ATOMS)
        return own_rows.transpose(2, 3, 0, 1, 4).reshape(VECTORS, 3, ATOM_TOTAL)
    total_rows = 3.0 * ATOM_TOTAL
    older_block = block_prev
    newer_block = block_cur
    fresh_list = []
    factor_list = []
    for lanczos_step in range(LANCZOS_STEPS):
        work_block = hessian_of(newer_block)
        fresh_block, lower_factor = orthonormal(work_block, newer_block, older_block, total_rows)
        fresh_list.append(fresh_block)
        factor_list.append(lower_factor)
        older_block = newer_block
        newer_block = fresh_block
    return (jnp.stack(fresh_list), jnp.stack(factor_list))
```

```python
import functools

import jax
import jax.numpy as jnp
from jax import lax
from jax.experimental import pallas as pl
from jax.experimental.pallas import tpu as pltpu
from jax.sharding import PartitionSpec as P

SOFTEN = 0.25
CUTOFF = 5.0
GAUSS_WIDTH = 2.0
EXACT = lax.Precision.HIGHEST
VMEM_BYTES = 48 * 1024 * 1024
NN = (((1,), (0,)), ((), ()))
NT = (((1,), (1,)), ((), ()))
TN = (((0,), (0,)), ((), ()))


def dot16(left, right, dims=NN):
    return lax.dot_general(left, right, dims, preferred_element_type=jnp.float32)


def dot32(left, right, dims=NN):
    return lax.dot_general(
        left, right, dims, precision=EXACT, preferred_element_type=jnp.float32
    )


def split(values, parts):
    pieces = []
    for _ in range(parts):
        piece = values.astype(jnp.bfloat16)
        pieces.append(piece)
        values = values - piece.astype(jnp.float32)
    return jnp.concatenate(pieces, axis=0)


def dot_split(left, right, dims=NN):
    if dims == TN:
        left = left.T
        dims = NN
    rows = left.shape[0]
    both = split(left, 2)
    high = right.astype(jnp.bfloat16)
    low = (right - high.astype(jnp.float32)).astype(jnp.bfloat16)
    first = dot16(both, high, dims)
    return first[:rows] + first[rows:] + dot16(both[:rows], low, dims)


def component(block, comp, half):
    start = comp * half
    return jnp.concatenate(
        [block[start : start + half], block[3 * half + start : 3 * half + start + half]], axis=0
    )


def unpack(packed, atoms):
    return jnp.concatenate([packed[:, :atoms], packed[:, atoms:]], axis=0)


def pick_matrix(index_row, patch_rows):
    extended = index_row.shape[1]
    rows = lax.broadcasted_iota(jnp.int32, (patch_rows, extended), 0)
    return (rows == index_row).astype(jnp.float32).astype(jnp.bfloat16)


def difference_matrix(dm_ref, nb, extended, atoms):
    half = nb.shape[0] // 2
    lanes = 2 * atoms
    paired = jnp.concatenate([nb[:half], nb[half:]], axis=1)
    rows = lax.broadcasted_iota(jnp.int32, (extended, lanes), 0)
    lane = lax.broadcasted_iota(jnp.int32, (extended, lanes), 1)
    own = (rows == jnp.where(lane < atoms, lane, lane - atoms)).astype(jnp.float32)
    for j in range(half):
        hit = (rows == paired[j : j + 1, :]).astype(jnp.float32)
        dm_ref[:, j * lanes : (j + 1) * lanes] = (hit - own).astype(jnp.bfloat16)


def fill_patch(patch_ref, sources, first, rows, atoms):
    for y, source in enumerate(sources):
        for x in range(3):
            block = source(x, first, rows)
            at = (3 * y + x) * atoms
            patch_ref[0:rows, at : at + atoms] = block[:, :atoms]
            patch_ref[rows : 2 * rows, at : at + atoms] = block[:, atoms:]


def apply_operator(parts16, dm_ref, ef_ref, ee_ref, e8_ref, p_ref, r_ref, mv_ref, eo_ref, xs_ref, sx_ref, cs_ref, atoms, moved_ready=False):
    lanes = 2 * atoms
    edges = dm_ref.shape[1]
    groups = edges // lanes
    basis = ef_ref.shape[0]
    vec3 = mv_ref.shape[0]
    half = vec3 // 6
    pairs = 2 * basis
    tiles = vec3 // 24
    lower = lax.broadcasted_iota(jnp.int32, (8, lanes), 1) < atoms

    def rows_of(tile, comp):
        per_half = half // 8
        return (tile // per_half) * 3 * half + comp * half + (tile % per_half) * 8

    if not moved_ready:
        wide = 2 * lanes
        for j in range(edges // wide):
            got = dot16(parts16, dm_ref[:, j * wide : (j + 1) * wide])
            mv_ref[:, j * wide : (j + 1) * wide] = got[:vec3] + got[vec3 : 2 * vec3]

    for tile in range(tiles):

        def gather_step(j, acc, tile=tile):
            at = pl.ds(pl.multiple_of(j * lanes, lanes), lanes)
            m = [mv_ref[rows_of(tile, c) : rows_of(tile, c) + 8, at] for c in range(3)]
            head = [e8_ref[c : c + 1, at] for c in range(3)]
            u = head[0] * m[0] + head[1] * m[1] + head[2] * m[2]
            along = [head[c] * u for c in range(3)]
            across = [m[c] - along[c] for c in range(3)]
            new = list(acc)
            for k in range(basis):
                slope = ef_ref[k : k + 1, at]
                even = ee_ref[k : k + 1, at]
                new[k] = new[k] + slope * u
                for c in range(3):
                    i = (c + 1) * basis + k
                    new[i] = new[i] + (slope * along[c] + even * across[c])
            return tuple(new)

        zero = jnp.zeros((8, lanes), jnp.float32)
        acc = lax.fori_loop(0, groups, gather_step, (zero,) * (4 * basis))
        for i in range(pairs):
            a, b = acc[i], acc[i + pairs]
            x = jnp.where(lower, a, b) + pltpu.roll(jnp.where(lower, b, a), atoms, 1)
            xs_ref[i, tile * 8 : tile * 8 + 8, :] = x
            sx_ref[i, tile * 8 : tile * 8 + 8, :] = pltpu.roll(x, atoms, 1)

    wide_lower = lax.broadcasted_iota(jnp.int32, (8 * tiles, lanes), 1) < atoms

    def mix_step(kappa, carry):
        at = pl.ds(pl.multiple_of(kappa * pairs, pairs), pairs)
        straight = p_ref[at, :]
        crossed = r_ref[at, :]
        y = jnp.zeros((8 * tiles, lanes), jnp.float32)
        for i in range(pairs):
            y = y + straight[i : i + 1, :] * xs_ref[i] + crossed[i : i + 1, :] * sx_ref[i]
        turned = pltpu.roll(y, atoms, 1)
        cs_ref[kappa] = jnp.where(wide_lower, y, turned)
        cs_ref[kappa + pairs] = jnp.where(wide_lower, turned, y)
        return carry

    lax.fori_loop(0, pairs, mix_step, 0)

    for tile in range(tiles):
        coeff = [cs_ref[i, tile * 8 : tile * 8 + 8, :] for i in range(4 * basis)]

        def spread_step(j, carry, tile=tile, coeff=coeff):
            at = pl.ds(pl.multiple_of(j * lanes, lanes), lanes)
            m = [mv_ref[rows_of(tile, c) : rows_of(tile, c) + 8, at] for c in range(3)]
            row = [e8_ref[i : i + 1, at] for i in range(8)]
            head, turn = row[0:3], row[5:8]
            u = head[0] * m[0] + head[1] * m[1] + head[2] * m[2]
            radial = jnp.zeros((8, lanes), jnp.float32)
            sums = [radial, radial, radial]
            evens = [radial, radial, radial]
            for k in range(basis):
                slope = ef_ref[k : k + 1, at]
                even = ee_ref[k : k + 1, at]
                radial = radial + slope * coeff[k]
                for c in range(3):
                    i = (c + 1) * basis + k
                    sums[c] = sums[c] + slope * coeff[i]
                    evens[c] = evens[c] + even * coeff[i]
            inner = radial + row[4] * u
            for c in range(3):
                inner = inner + head[c] * (sums[c] - evens[c]) + turn[c] * m[c]
            for c in range(3):
                out = evens[c] + head[c] * inner + row[3] * m[c] + turn[c] * u
                eo_ref[rows_of(tile, c) : rows_of(tile, c) + 8, at] = out
            return carry

        lax.fori_loop(0, groups, spread_step, 0)

    spread = dot16(split(eo_ref[...], 2), dm_ref[...], NT)
    return spread[:vec3] + spread[vec3:]


def store_patch(outs, extended_rows, pick, atoms):
    vec3 = extended_rows.shape[0]
    half3 = vec3 // 2
    both = dot16(split(extended_rows, 2), pick, NT)
    patch = both[:vec3] + both[vec3:]
    for x in range(3):
        for y in range(3):
            at = (3 * y + x) * atoms
            tile = patch[:, at : at + atoms]
            outs[x][y * half3 : (y + 1) * half3, 0:atoms] = tile[:half3]
            outs[x][y * half3 : (y + 1) * half3, atoms : 2 * atoms] = tile[half3:]


def pack_kernel(cur_ref, prev_ref, pos_ref, xl_ref, yl_ref, out_ref):
    vectors, _, atoms = cur_ref.shape
    half = vectors // 2
    for which, ref in enumerate((cur_ref, prev_ref)):
        for c in range(3):
            rows = ref[:, c, :]
            at = which * 3 * half + c * half
            out_ref[at : at + half, 0:atoms] = rows[:half]
            out_ref[at : at + half, atoms : 2 * atoms] = rows[half:]
    base = 6 * half
    out_ref[base : base + 8, :] = jnp.zeros((8, 2 * atoms), jnp.float32)
    out_ref[base : base + 3, 0:atoms] = pos_ref[...]
    halo = xl_ref.shape[1]
    out_ref[base : base + 2, atoms : atoms + halo] = xl_ref[...].astype(jnp.float32)
    out_ref[base + 2 : base + 4, atoms : atoms + halo] = yl_ref[...].astype(jnp.float32)


def index_row(sides, own3_ref, base, atoms, halo):
    even_x = sides[0] == 0
    even_y = sides[1] == 0

    def lists(ref_y, x, row):
        return ref_y[x, base + row : base + row + 1, atoms : atoms + halo]

    before_x, after_x = jnp.where(even_x, 2.0, 0.0), jnp.where(even_x, 0.0, 2.0)
    before_y, after_y = jnp.where(even_y, 2.0, 0.0), jnp.where(even_y, 0.0, 2.0)

    def pick_x(ref_y):
        low = jnp.where(even_x, lists(ref_y, 2, 0), lists(ref_y, 0, 0)) + before_x * atoms
        high = jnp.where(even_x, lists(ref_y, 0, 1), lists(ref_y, 2, 1)) + after_x * atoms
        own = lax.broadcasted_iota(jnp.int32, (1, atoms), 1).astype(jnp.float32) + atoms
        return jnp.concatenate([own, low, high], axis=1)

    refs = own3_ref
    row_y = 3.0 * atoms
    pieces = [pick_x(refs[1]) + row_y]
    tables = [pick_x(refs[0]), pick_x(refs[2])]
    for row, place, mate_has in ((2, before_y, False), (3, after_y, True)):
        use_mate = even_y == mate_has if isinstance(mate_has, bool) else mate_has
        mate_list, other_list = lists(refs[0], 1, row), lists(refs[2], 1, row)
        if mate_has:
            chosen = jnp.where(even_y, mate_list, other_list)
            table = jnp.where(even_y, tables[0], tables[1])
        else:
            chosen = jnp.where(even_y, other_list, mate_list)
            table = jnp.where(even_y, tables[1], tables[0])
        widened = table.shape[1]
        hits = lax.broadcasted_iota(jnp.int32, (widened, halo), 0) == chosen.astype(jnp.int32)
        found = dot32(jnp.broadcast_to(table, (8, widened)), hits.astype(jnp.float32))
        pieces.append(found[0:1] + place * row_y)
    return jnp.round(jnp.concatenate(pieces, axis=1)).astype(jnp.int32)


def first_kernel(
    sides, own3, mate3, other3, nb, count, w_rad, w_vec, w_mix, w_out,
    out_m, out_o, out_x, sums, cext, pext, index, ef, ee, e8, pmat, rmat,
    dm, patch, mv, eo, xs, sx, cs, f2s, hs, qs,
    *, vectors, atoms, halo,
):
    half = vectors // 2
    half3 = 3 * half
    vec3 = 6 * half
    base = 2 * half3
    lanes = 2 * atoms
    slots = nb.shape[0]
    edges = slots * atoms
    extended = cext.shape[1]
    basis, channels = w_rad.shape
    pairs = 2 * basis
    refs = (mate3, own3, other3)

    difference_matrix(dm, nb[...], extended, atoms)
    places = index_row(sides, refs, base, atoms, halo)
    index[...] = jnp.broadcast_to(places, index.shape)
    pick = pick_matrix(places, 9 * atoms)

    sources = [lambda x, first, rows, ref=ref: ref[x, first : first + rows, :] for ref in refs]
    fill_patch(patch, sources, 0, half3, atoms)
    current = split(patch[...], 2)
    fill_patch(patch, sources, half3, half3, atoms)
    previous = split(patch[...], 2)
    patch[24:32, :] = jnp.zeros((8, 9 * atoms), jnp.float32)
    for y in range(3):
        for x in range(3):
            at = (3 * y + x) * atoms
            for c in range(3):
                line = refs[y][x, base + c : base + c + 1, 0:atoms]
                patch[8 * c : 8 * c + 8, at : at + atoms] = jnp.broadcast_to(line, (8, atoms))
    place = split(patch[0:32, :], 3)
    chosen = dot16(jnp.concatenate([current, previous, place], axis=0), pick)
    cext[...] = chosen[0:vec3] + chosen[vec3 : 2 * vec3]
    pext[...] = chosen[2 * vec3 : 3 * vec3] + chosen[3 * vec3 : 4 * vec3]
    parts16 = jnp.concatenate([chosen[: 2 * vec3], chosen[4 * vec3 :]], axis=0).astype(jnp.bfloat16)

    wide = 2 * lanes
    centre = (lax.broadcasted_iota(jnp.int32, (basis, wide), 0).astype(jnp.float32) + 0.5) * (CUTOFF / basis)
    counts = count[...]
    slot_lane = lax.broadcasted_iota(jnp.int32, (1, lanes), 1)
    slot_half = jnp.where(slot_lane < atoms, 0, slots // 2)
    counts2 = jnp.concatenate([counts, counts], axis=1)
    totals = [jnp.zeros((basis, lanes), jnp.float32) for _ in range(4)]
    for j in range(edges // wide):
        at = slice(j * wide, (j + 1) * wide)
        got = dot16(parts16, dm[:, at])
        mv[:, at] = got[:vec3] + got[vec3 : 2 * vec3]
        third = 2 * vec3
        delta = got[third : third + 24] + got[third + 32 : third + 56] + got[third + 64 : third + 88]
        d = [delta[8 * c : 8 * c + 8] for c in range(3)]
        squared = d[0] * d[0] + d[1] * d[1] + d[2] * d[2] + SOFTEN
        radius = jnp.sqrt(squared)
        inverse = 1.0 / radius
        head = [d[c] * inverse for c in range(3)]
        valid = jnp.concatenate(
            [(slot_half + (2 * j + i) < counts2).astype(jnp.float32) for i in range(2)], axis=1
        )
        tau = jnp.maximum(1.0 - squared * (1.0 / (CUTOFF * CUTOFF)), 0.0)
        cut = 1.0 / (CUTOFF * CUTOFF)
        env = tau * tau * tau
        env1 = (-6.0 * cut) * radius * tau * tau
        env2 = (24.0 * cut * cut) * squared * tau - (6.0 * cut) * tau * tau
        off = radius - centre
        gauss = jnp.exp(-GAUSS_WIDTH * off * off) * valid
        gauss1 = (-2.0 * GAUSS_WIDTH) * off * gauss
        gauss2 = (4.0 * GAUSS_WIDTH * GAUSS_WIDTH * off * off - 2.0 * GAUSS_WIDTH) * gauss
        value = gauss * env
        ef[:, at] = gauss1 * env + gauss * env1
        ee[:, at] = value * inverse
        f2s[:, at] = gauss2 * env + 2.0 * gauss1 * env1 + gauss * env2
        for c in range(3):
            hs[8 * c : 8 * c + 8, at] = head[c]
        hs[24:32, at] = inverse
        terms = [value, value * head[0], value * head[1], value * head[2]]
        totals = [t + v[:, :lanes] + v[:, lanes:] for t, v in zip(totals, terms)]
    descr = [t + pltpu.roll(t, atoms, 1) for t in totals]

    lower = lax.broadcasted_iota(jnp.int32, (channels, lanes), 1) < atoms
    rad = w_rad[...]
    vec = w_vec[...]
    mix = w_mix[...]
    rad_t = rad.T
    vec_t = vec.T
    mix_t = mix.T
    out_t = jnp.broadcast_to(w_out[...], (8, channels)).T[:, 0:1]
    flow = [dot32(vec_t, descr[c + 1]) for c in range(3)]
    mixed = dot32(rad_t, descr[0]) + flow[0] * flow[0] + flow[1] * flow[1] + flow[2] * flow[2]
    hidden = dot_split(mix_t, mixed)
    gate = 1.0 / (1.0 + jnp.exp(-hidden))
    slope = gate * (1.0 + hidden * (1.0 - gate)) * out_t
    bend = gate * (1.0 - gate) * (2.0 + hidden * (1.0 - 2.0 * gate)) * out_t
    u = dot_split(mix, slope)
    alpha = dot32(rad, u)
    beta = [2.0 * dot32(vec, flow[c] * u) for c in range(3)]

    for j in range(edges // lanes):
        at = slice(j * lanes, (j + 1) * lanes)
        head = [hs[8 * c : 8 * c + 8, at] for c in range(3)]
        inverse = hs[24:32, at]
        slope_k, even_k, second = ef[:, at], ee[:, at], f2s[:, at]
        even1 = (slope_k - even_k) * inverse
        even2 = (second - 2.0 * even1) * inverse

        def over(values):
            return jnp.sum(values, axis=0, keepdims=True)

        first = over(alpha * slope_k)
        bend_r = over(alpha * second)
        turn = [over(beta[c] * even1) for c in range(3)]
        twist = [over(beta[c] * even2) for c in range(3)]
        inv1 = inverse[0:1]
        h1 = [head[c][0:1] for c in range(3)]
        radius = 1.0 / inv1
        line = h1[0] * turn[0] + h1[1] * turn[1] + h1[2] * turn[2]
        isotropic = first * inv1 + line
        radial = bend_r + (h1[0] * twist[0] + h1[1] * twist[1] + h1[2] * twist[2]) * radius - isotropic
        e8[:, at] = jnp.concatenate(h1 + [isotropic, radial] + turn, axis=0)

    lift0 = 2.0 * jnp.where(lower, flow[0], flow[2])
    lift1 = 2.0 * flow[1]
    for i in range(pairs):
        k = i % basis
        if i < basis:
            side = jnp.where(lower, jnp.broadcast_to(rad_t[:, k : k + 1], lower.shape), lift1 * vec_t[:, k : k + 1])
        else:
            side = lift0 * vec_t[:, k : k + 1]
        qs[:, i * lanes : (i + 1) * lanes] = dot_split(mix_t, side)
    both = [2.0 * dot32(vec * vec[k : k + 1, :], u) for k in range(basis)]
    low_row = lax.broadcasted_iota(jnp.int32, (1, lanes), 1) < atoms
    for i in range(pairs):
        q_i = qs[:, i * lanes : (i + 1) * lanes] * bend
        for k in range(i + 1):
            q_k = qs[:, k * lanes : (k + 1) * lanes]
            straight = jnp.sum(q_i * q_k, axis=0, keepdims=True)
            crossed = jnp.sum(q_i * pltpu.roll(q_k, atoms, 1), axis=0, keepdims=True)
            if (i < basis) == (k < basis):
                extra = both[i % basis][k % basis : k % basis + 1, :]
                straight = straight + (jnp.where(low_row, 0.0, extra) if i < basis else extra)
            pmat[i * pairs + k : i * pairs + k + 1, :] = straight
            rmat[i * pairs + k : i * pairs + k + 1, :] = crossed
            if k < i:
                pmat[k * pairs + i : k * pairs + i + 1, :] = straight
                rmat[k * pairs + i : k * pairs + i + 1, :] = pltpu.roll(crossed, atoms, 1)

    rows = apply_operator(None, dm, ef, ee, e8, pmat, rmat, mv, eo, xs, sx, cs, atoms, True)
    store_patch((out_m, out_o, out_x), rows, pick, atoms)

    basis_dot = jnp.zeros((2 * vectors, vectors), jnp.float32)
    gram = jnp.zeros((2 * vectors, 2 * vectors), jnp.float32)
    for c in range(3):
        old = jnp.concatenate([component(cext[...], c, half), component(pext[...], c, half)], axis=0)
        basis_dot = basis_dot + dot_split(old, component(rows, c, half), NT)
        own = old[:, :atoms]
        gram = gram + dot_split(own, own, NT)
    blank = jnp.zeros((2 * vectors, sums.shape[1] - 3 * vectors), jnp.float32)
    sums[...] = jnp.concatenate([gram, basis_dot, blank], axis=1)


def second_kernel(
    order, own, mate, other, far, cext, pext, index, nb, ef, ee, e8, pmat, rmat,
    out_m, out_o, out_x, sums, rown,
    dm, patch, mv, eo, xs, sx, cs, ring,
    *, vectors, atoms, total_rows,
):
    half = vectors // 2
    half3 = 3 * half
    vec3 = 6 * half
    tail = 3 * half3
    extended = cext.shape[1]
    difference_matrix(dm, nb[...], extended, atoms)
    pick = pick_matrix(index[0:1, :], 9 * atoms)
    for i, part in enumerate((own, mate, other)):
        ring[order[i]] = part[tail:, :]
    ring[order[3]] = far[...]
    total = ((ring[0] + ring[1]) + (ring[2] + ring[3])) * (1.0 / total_rows)
    sums[...] = total
    coef = total[:, 2 * vectors : 3 * vectors]

    refs = (mate, own, other)
    for x, ref in enumerate(refs):
        for y in range(3):
            at = (3 * y + x) * atoms
            block = ref[y * half3 : (y + 1) * half3, :]
            patch[0:half3, at : at + atoms] = block[:, :atoms]
            patch[half3:vec3, at : at + atoms] = block[:, atoms:]
    both = dot16(split(patch[...], 2), pick)
    work = both[:vec3] + both[vec3:]
    pieces = []
    for c in range(3):
        old = jnp.concatenate([component(cext[...], c, half), component(pext[...], c, half)], axis=0)
        pieces.append(dot_split(coef.T, old))
    lower = [p[:half] for p in pieces]
    upper = [p[half:] for p in pieces]
    resid = work - jnp.concatenate(lower + upper, axis=0)
    rown[...] = jnp.concatenate([resid[:half3, :atoms], resid[half3:, :atoms]], axis=1)
    rows = apply_operator(split(resid, 2), dm, ef, ee, e8, pmat, rmat, mv, eo, xs, sx, cs, atoms)
    store_patch((out_m, out_o, out_x), rows, pick, atoms)


def gram_kernel(rown, y0, ym, yo, out, yown, *, vectors, atoms):
    half = vectors // 2
    work = y0[...] + ym[...] + yo[...]
    yown[...] = work
    gram = jnp.zeros((2 * vectors, 2 * vectors), jnp.float32)
    for c in range(3):
        at = slice(c * half, (c + 1) * half)
        r, y = rown[at, :], work[at, :]
        stacked = jnp.concatenate(
            [r[:, :atoms], r[:, atoms:], y[:, :atoms], y[:, atoms:]], axis=0
        )
        gram = gram + dot_split(stacked, stacked, NT)
    full = jnp.concatenate([gram, jnp.zeros_like(gram)], axis=1)
    out[...] = jnp.broadcast_to(full[None], out.shape)


def cholesky(matrix):
    size = matrix.shape[0]
    rows = lax.broadcasted_iota(jnp.int32, (size, 2 * size), 0)
    lane = lax.broadcasted_iota(jnp.int32, (size, 2 * size), 1)
    unit = (lane - size == rows).astype(jnp.float32)
    work = jnp.concatenate([matrix, jnp.zeros_like(matrix)], axis=1) + unit
    done = jnp.zeros_like(work)
    for j in range(size):
        line = work[j : j + 1, :]
        pivot = work[j : j + 1, j : j + 1]
        scale = lax.rsqrt(pivot)
        scale = scale * (1.5 - 0.5 * pivot * scale * scale)
        line = line * scale
        column = work[:, j : j + 1] * scale
        done = jnp.where(rows == j, line, done)
        work = work - column * line
    upper = jnp.where(lane >= rows, done, 0.0)[:, :size]
    return upper, done[:, size:]


def final_kernel(got, sums, rown, yown, cown, blocks, factors, *, vectors, atoms, total_rows):
    half = vectors // 2
    half3 = 3 * half
    devices = got.shape[0]
    total = got[0]
    for i in range(1, devices):
        total = total + got[i]
    total = total * (1.0 / total_rows)
    v = vectors
    rr, ry, yy = total[:v, :v], total[:v, v : 2 * v], total[v : 2 * v, v : 2 * v]
    shared = sums[...]
    gram_old = shared[:, : 2 * v]
    coef1 = shared[:, 2 * v : 3 * v]
    rows = lax.broadcasted_iota(jnp.int32, (v, v), 0)
    cols = lax.broadcasted_iota(jnp.int32, (v, v), 1)
    unit = (rows == cols).astype(jnp.float32)

    upper1, inv1 = cholesky(rr)
    left = coef1 - dot32(gram_old, coef1)
    wr = rr + dot32(coef1, left, TN)
    coef_x = dot32(dot32(inv1, ry), inv1, NT)
    coef_c = dot32(wr, inv1, NT)
    cross = dot32(left[:v], inv1, NT)
    yy1 = dot32(dot32(inv1, yy), inv1, NT)
    coef2 = jnp.concatenate([coef_x, coef_c], axis=0)
    basis = jnp.concatenate(
        [
            jnp.concatenate([-unit, cross.T], axis=1),
            jnp.concatenate([cross, gram_old[:v, :v] - 2.0 * unit], axis=1),
        ],
        axis=0,
    )
    gram2 = yy1 + dot32(coef2, dot32(basis, coef2), TN)
    upper2, inv2 = cholesky(gram2)
    by_x = dot32(inv2, coef_x, NT)
    m_y = dot32(inv2, inv1)
    m_r = -dot32(by_x, inv1)
    m_c = -dot32(inv2, coef_c, NT)
    weights = jnp.concatenate([m_y, m_r, m_c], axis=1)
    factors[0] = upper1.T
    factors[1] = upper2.T
    for c in range(3):
        at = slice(c * half, (c + 1) * half)
        r, y, old = unpack(rown[at, :], atoms), unpack(yown[at, :], atoms), unpack(cown[at, :], atoms)
        blocks[0, :, c, :] = dot32(inv1, r)
        blocks[1, :, c, :] = dot32(weights, jnp.concatenate([y, r, old], axis=0))


def mates(count):
    mate = [i ^ 1 for i in range(count)]
    other = [(i - 1) % count if i % 2 == 0 else (i + 1) % count for i in range(count)]
    return mate, other


def fetch(values, axis, sources):
    return lax.ppermute(values, axis, [(s, i) for i, s in enumerate(sources)])


def vmem_call(kernel, outs, scratch=(), scalars=0, **cost):
    def call(*operands):
        spaces = [pltpu.SMEM] * scalars + [pltpu.VMEM] * (len(operands) - scalars)
        return pl.pallas_call(
            kernel,
            out_shape=outs,
            in_specs=[pl.BlockSpec(memory_space=s) for s in spaces],
            out_specs=jax.tree.map(lambda _: pl.BlockSpec(memory_space=pltpu.VMEM), outs),
            scratch_shapes=list(scratch),
            compiler_params=pltpu.CompilerParams(vmem_limit_bytes=VMEM_BYTES),
            cost_estimate=pl.CostEstimate(
                flops=cost.get("flops", 1 << 20), bytes_accessed=1 << 16, transcendentals=0
            ),
        )(*operands)

    return call


def f32(*shape):
    return jax.ShapeDtypeStruct(shape, jnp.float32)


def shards(positions, block_prev, block_cur, neighbours, counts, x_lists, y_lists, w_radial, w_vector, w_mix, w_out):
    vectors, _, atoms = block_cur.shape
    halo = x_lists.shape[2]
    slots = neighbours.shape[0]
    basis, channels = w_radial.shape
    n_x, n_y = lax.axis_size("gx"), lax.axis_size("gy")
    total_rows = 3.0 * atoms * n_x * n_y
    half3 = 3 * vectors // 2
    vec3 = 3 * vectors
    lanes = 2 * atoms
    edges = slots * atoms
    extended = atoms + 4 * halo
    pairs = 2 * basis
    mate_x, other_x = mates(n_x)
    mate_y, other_y = mates(n_y)
    at_x, at_y = lax.axis_index("gx"), lax.axis_index("gy")
    sides = jnp.stack([at_x % 2, at_y % 2]).astype(jnp.int32)
    own_rows = 2 * half3 + 8

    own = vmem_call(pack_kernel, f32(own_rows, lanes))(
        block_cur, block_prev, positions, x_lists[0], y_lists[0]
    )
    from_mate = fetch(own, "gx", mate_x)
    from_other = fetch(own, "gx", other_x)
    own3 = jnp.stack([from_mate, own, from_other])
    mate3 = fetch(own3, "gy", mate_y)
    other3 = fetch(own3, "gy", other_y)

    extent = pltpu.VMEM((extended, edges), jnp.bfloat16)
    work_scratch = [
        extent,
        pltpu.VMEM((vec3, 9 * atoms), jnp.float32),
        pltpu.VMEM((vec3, edges), jnp.float32),
        pltpu.VMEM((vec3, edges), jnp.float32),
        pltpu.VMEM((pairs, vectors, lanes), jnp.float32),
        pltpu.VMEM((pairs, vectors, lanes), jnp.float32),
        pltpu.VMEM((2 * pairs, vectors, lanes), jnp.float32),
    ]
    first = vmem_call(
        functools.partial(first_kernel, vectors=vectors, atoms=atoms, halo=halo),
        [
            f32(3 * half3, lanes),
            f32(3 * half3, lanes),
            f32(3 * half3, lanes),
            f32(2 * vectors, lanes),
            f32(vec3, extended),
            f32(vec3, extended),
            jax.ShapeDtypeStruct((8, extended), jnp.int32),
            f32(basis, edges),
            f32(basis, edges),
            f32(8, edges),
            f32(pairs * pairs, lanes),
            f32(pairs * pairs, lanes),
        ],
        work_scratch
        + [
            pltpu.VMEM((basis, edges), jnp.float32),
            pltpu.VMEM((32, edges), jnp.float32),
            pltpu.VMEM((channels, pairs * lanes), jnp.float32),
        ],
        scalars=1,
        flops=1 << 31,
    )
    part_m, part_0, part_o, local, cext, pext, index, ef, ee, e8, pmat, rmat = first(
        sides, own3, mate3, other3, neighbours, counts[None], w_radial, w_vector, w_mix, w_out[None]
    )

    back_m = fetch(part_m, "gx", mate_x)
    back_o = fetch(part_o, "gx", other_x)
    strided = [local] + [
        fetch(local, "gx", [(i + d) % n_x for i in range(n_x)]) for d in range(4, n_x, 4)
    ]
    if len(strided) == 2:
        local = strided[0] + strided[1]
    else:
        local = jnp.sum(jnp.roll(jnp.stack(strided), at_x // 4, axis=0), axis=0)
    folded = part_0 + back_m + back_o
    f_m, f_0, f_o = folded[:half3], folded[half3 : 2 * half3], folded[2 * half3 :]

    far_m = [other_y[m] for m in mate_y]
    far_o = [mate_y[o] for o in other_y]
    got_m = fetch(jnp.concatenate([f_0, f_m, local]), "gy", mate_y)
    got_o = fetch(jnp.concatenate([f_0, f_o, local]), "gy", other_y)
    if far_m == far_o:
        got_2 = fetch(jnp.concatenate([f_m, f_o, local]), "gy", far_m)
        far_mate, far_other = got_2[half3 : 2 * half3], got_2[:half3]
        sums = (local + got_m[2 * half3 :]) + (got_o[2 * half3 :] + got_2[2 * half3 :])
    else:
        far_mate = fetch(f_o, "gy", far_m)
        far_other = fetch(f_m, "gy", far_o)
        terms = [local] + [
            fetch(local, "gy", [(i + d) % n_y for i in range(n_y)]) for d in range(1, n_y)
        ]
        sums = jnp.sum(jnp.roll(jnp.stack(terms), at_y, axis=0), axis=0)
    w_m = got_m[:half3] + f_m + far_mate
    w_0 = f_0 + got_m[half3 : 2 * half3] + got_o[half3 : 2 * half3]
    w_o = got_o[:half3] + far_other + f_o
    column = jnp.concatenate([w_m, w_0, w_o, sums])

    col_m = fetch(column, "gx", mate_x)
    col_o = fetch(column, "gx", other_x)
    far = fetch(sums, "gx", [(i + 2) % n_x for i in range(n_x)])
    order = jnp.stack(
        [at_x % 4, (at_x ^ 1) % 4, (at_x - 1 + 2 * (at_x % 2)) % 4, (at_x + 2) % 4]
    ).astype(jnp.int32)

    second = vmem_call(
        functools.partial(second_kernel, vectors=vectors, atoms=atoms, total_rows=total_rows),
        [
            f32(3 * half3, lanes),
            f32(3 * half3, lanes),
            f32(3 * half3, lanes),
            f32(2 * vectors, lanes),
            f32(half3, lanes),
        ],
        work_scratch + [pltpu.VMEM((4, 2 * vectors, lanes), jnp.float32)],
        scalars=1,
        flops=1 << 30,
    )
    part_m, part_0, part_o, shared, rown = second(
        order, column, col_m, col_o, far, cext, pext, index, neighbours, ef, ee, e8, pmat, rmat
    )
    back_m = fetch(part_m, "gx", mate_x)
    back_o = fetch(part_o, "gx", other_x)
    folded = part_0 + back_m + back_o
    y_m = fetch(folded[:half3], "gy", mate_y)
    y_o = fetch(folded[2 * half3 :], "gy", other_y)

    devices = n_x * n_y
    spread, yown = vmem_call(
        functools.partial(gram_kernel, vectors=vectors, atoms=atoms),
        [f32(devices, 2 * vectors, lanes), f32(half3, lanes)],
    )(rown, folded[half3 : 2 * half3], y_m, y_o)
    got = lax.all_to_all(spread, ("gx", "gy"), 0, 0)
    blocks, factors = vmem_call(
        functools.partial(final_kernel, vectors=vectors, atoms=atoms, total_rows=total_rows),
        [f32(2, vectors, 3, atoms), f32(2, vectors, vectors)],
    )(got, shared, rown, yown, own[:half3])
    return blocks, factors


def solution(mesh):
    placed = (
        P(None, ("gx", "gy")),
        P(None, None, ("gx", "gy")),
        P(None, None, ("gx", "gy")),
        P(None, ("gx", "gy")),
        P(("gx", "gy")),
        P(("gx", "gy"), None, None),
        P(("gx", "gy"), None, None),
        P(),
        P(),
        P(),
        P(),
    )
    return jax.shard_map(
        shards,
        mesh=mesh,
        in_specs=placed,
        out_specs=(P(None, None, None, ("gx", "gy")), P()),
        check_vma=False,
    )
```

```python
import functools

import jax
import jax.numpy as jnp
from jax import lax
from jax.experimental import pallas as pl
from jax.experimental.pallas import tpu as pltpu
from jax.sharding import PartitionSpec as P

SOFTEN = 0.25
CUTOFF = 5.0
GAUSS_WIDTH = 2.0
EXACT = lax.Precision.HIGHEST
VMEM_BYTES = 48 * 1024 * 1024
NN = (((1,), (0,)), ((), ()))
NT = (((1,), (1,)), ((), ()))
TN = (((0,), (0,)), ((), ()))


def dot16(left, right, dims=NN):
    return lax.dot_general(left, right, dims, preferred_element_type=jnp.float32)


def dot32(left, right, dims=NN):
    return lax.dot_general(
        left, right, dims, precision=EXACT, preferred_element_type=jnp.float32
    )


def split(values, parts):
    pieces = []
    for _ in range(parts):
        piece = values.astype(jnp.bfloat16)
        pieces.append(piece)
        values = values - piece.astype(jnp.float32)
    return jnp.concatenate(pieces, axis=0)


def dot_split(left, right, dims=NN):
    if dims == TN:
        left = left.T
        dims = NN
    rows = left.shape[0]
    both = split(left, 2)
    high = right.astype(jnp.bfloat16)
    low = (right - high.astype(jnp.float32)).astype(jnp.bfloat16)
    first = dot16(both, high, dims)
    return first[:rows] + first[rows:] + dot16(both[:rows], low, dims)


def component(block, comp, vectors):
    return block[comp * vectors : (comp + 1) * vectors]


def unpack(packed, atoms):
    return jnp.concatenate([packed[:, :atoms], packed[:, atoms:]], axis=0)


def pack(rows):
    half = rows.shape[0] // 2
    return jnp.concatenate([rows[:half], rows[half:]], axis=1)


def pick_matrix(index_row, patch_rows):
    extended = index_row.shape[1]
    rows = lax.broadcasted_iota(jnp.int32, (patch_rows, extended), 0)
    return (rows == index_row).astype(jnp.float32).astype(jnp.bfloat16)


def select(rows, first, second):
    picks = jnp.concatenate([first, second], axis=1)
    hits = lax.broadcasted_iota(jnp.int32, (rows.shape[1], picks.shape[1]), 0) == picks
    got = dot16(split(rows, 3), hits.astype(jnp.float32).astype(jnp.bfloat16))
    count = rows.shape[0]
    return got[:count] + (got[count : 2 * count] + got[2 * count :])


def rows_and_cols(size):
    return (
        lax.broadcasted_iota(jnp.int32, (size, size), 0),
        lax.broadcasted_iota(jnp.int32, (size, size), 1),
    )


def join_triangles(lower, upper):
    rows, cols = rows_and_cols(lower.shape[0])
    return jnp.where(rows >= cols, lower, upper)


def with_diagonal(lower, source):
    size = lower.shape[0]
    rows, cols = rows_and_cols(size)
    line = jnp.sum(jnp.where(rows == cols, source, 0.0), axis=0, keepdims=True)
    upper = jnp.where(rows == 0, line, jnp.where((rows == 1) & (cols == size - 1), source[0:1, 0:1], 0.0))
    return jnp.where(rows >= cols, lower, upper)


def from_lower(joined):
    rows, cols = rows_and_cols(joined.shape[0])
    strict = jnp.where(rows > cols, joined, 0.0)
    return jnp.where(rows >= cols, joined, 0.0) + strict.T


def from_upper(joined, holder):
    size = joined.shape[0]
    rows, cols = rows_and_cols(size)
    strict = jnp.where(rows < cols, joined, 0.0)
    line = jnp.where(cols[0:1] >= 1, holder[0:1], holder[1:2, size - 1 : size])
    return strict + strict.T + jnp.where(rows == cols, line, 0.0)


def flatten(square, lanes):
    size = square.shape[0]
    rows = size * size // lanes
    return jnp.concatenate([square[i * rows : (i + 1) * rows] for i in range(lanes // size)], axis=1)


def unflatten(flat, size):
    return jnp.concatenate(
        [flat[:, i * size : (i + 1) * size] for i in range(flat.shape[1] // size)], axis=0
    )


def apply_operator(parts16, dm_ref, ef_ref, ee_ref, e8_ref, p_ref, r_ref, mv_ref, eo_ref, xs_ref, sx_ref, cs_ref, atoms, moved_ready=False):
    lanes = 2 * atoms
    edges = dm_ref.shape[1]
    groups = edges // lanes
    basis = ef_ref.shape[0]
    vec3 = mv_ref.shape[0]
    vectors = vec3 // 3
    pairs = 2 * basis
    tiles = vec3 // 24
    lower = lax.broadcasted_iota(jnp.int32, (8, lanes), 1) < atoms

    def rows_of(tile, comp):
        return comp * vectors + tile * 8

    if not moved_ready:
        wide = 2 * lanes
        for j in range(edges // wide):
            got = dot16(parts16, dm_ref[:, j * wide : (j + 1) * wide])
            mv_ref[:, j * wide : (j + 1) * wide] = got[:vec3] + got[vec3 : 2 * vec3]

    for tile in range(tiles):

        def gather_step(j, acc, tile=tile):
            at = pl.ds(pl.multiple_of(j * lanes, lanes), lanes)
            m = [mv_ref[rows_of(tile, c) : rows_of(tile, c) + 8, at] for c in range(3)]
            head = [e8_ref[c : c + 1, at] for c in range(3)]
            u = head[0] * m[0] + head[1] * m[1] + head[2] * m[2]
            along = [head[c] * u for c in range(3)]
            across = [m[c] - along[c] for c in range(3)]
            new = list(acc)
            for k in range(basis):
                slope = ef_ref[k : k + 1, at]
                even = ee_ref[k : k + 1, at]
                new[k] = new[k] + slope * u
                for c in range(3):
                    i = (c + 1) * basis + k
                    new[i] = new[i] + (slope * along[c] + even * across[c])
            return tuple(new)

        zero = jnp.zeros((8, lanes), jnp.float32)
        acc = lax.fori_loop(0, groups, gather_step, (zero,) * (4 * basis))
        for i in range(pairs):
            a, b = acc[i], acc[i + pairs]
            x = jnp.where(lower, a, b) + pltpu.roll(jnp.where(lower, b, a), atoms, 1)
            xs_ref[i, tile * 8 : tile * 8 + 8, :] = x
            sx_ref[i, tile * 8 : tile * 8 + 8, :] = pltpu.roll(x, atoms, 1)

    wide_lower = lax.broadcasted_iota(jnp.int32, (8 * tiles, lanes), 1) < atoms

    def mix_step(kappa, carry):
        at = pl.ds(pl.multiple_of(kappa * pairs, pairs), pairs)
        straight = p_ref[at, :]
        crossed = r_ref[at, :]
        y = jnp.zeros((8 * tiles, lanes), jnp.float32)
        for i in range(pairs):
            y = y + straight[i : i + 1, :] * xs_ref[i] + crossed[i : i + 1, :] * sx_ref[i]
        turned = pltpu.roll(y, atoms, 1)
        cs_ref[kappa] = jnp.where(wide_lower, y, turned)
        cs_ref[kappa + pairs] = jnp.where(wide_lower, turned, y)
        return carry

    lax.fori_loop(0, pairs, mix_step, 0)

    for tile in range(tiles):
        coeff = [cs_ref[i, tile * 8 : tile * 8 + 8, :] for i in range(4 * basis)]

        def spread_step(j, carry, tile=tile, coeff=coeff):
            at = pl.ds(pl.multiple_of(j * lanes, lanes), lanes)
            m = [mv_ref[rows_of(tile, c) : rows_of(tile, c) + 8, at] for c in range(3)]
            row = [e8_ref[i : i + 1, at] for i in range(8)]
            head, turn = row[0:3], row[5:8]
            u = head[0] * m[0] + head[1] * m[1] + head[2] * m[2]
            radial = jnp.zeros((8, lanes), jnp.float32)
            sums = [radial, radial, radial]
            evens = [radial, radial, radial]
            for k in range(basis):
                slope = ef_ref[k : k + 1, at]
                even = ee_ref[k : k + 1, at]
                radial = radial + slope * coeff[k]
                for c in range(3):
                    i = (c + 1) * basis + k
                    sums[c] = sums[c] + slope * coeff[i]
                    evens[c] = evens[c] + even * coeff[i]
            inner = radial + row[4] * u
            for c in range(3):
                inner = inner + head[c] * (sums[c] - evens[c]) + turn[c] * m[c]
            for c in range(3):
                out = evens[c] + head[c] * inner + row[3] * m[c] + turn[c] * u
                eo_ref[rows_of(tile, c) : rows_of(tile, c) + 8, at] = out
            return carry

        lax.fori_loop(0, groups, spread_step, 0)

    spread = dot16(split(eo_ref[...], 2), dm_ref[...], NT)
    return spread[:vec3] + spread[vec3:]


def store_patch(outs, extended_rows, pick, atoms):
    vec3 = extended_rows.shape[0]
    half3 = vec3 // 2
    both = dot16(split(extended_rows, 2), pick, NT)
    patch = both[:vec3] + both[vec3:]
    for x in range(3):
        for y in range(3):
            at = (3 * y + x) * atoms
            tile = patch[:, at : at + atoms]
            outs[x][y * half3 : (y + 1) * half3, 0:atoms] = tile[:half3]
            outs[x][y * half3 : (y + 1) * half3, atoms : 2 * atoms] = tile[half3:]


def select_x_kernel(sides, cur, prev, pos, lists, to_mate, to_other):
    half3 = cur.shape[0] // 2
    atoms = cur.shape[1]
    own = lax.broadcasted_iota(jnp.int32, (1, atoms), 1).astype(jnp.float32)
    rows = jnp.concatenate([cur[...], prev[...], pos[...], own, jnp.zeros((4, atoms), jnp.float32)], axis=0)
    emit(sides[0], rows, lists, to_mate, to_other, half3)


def emit(side, rows, lists, to_mate, to_other, half3):
    even = side == 0
    low, high = lists[0:1, :], lists[1:2, :]
    got = select(rows, jnp.where(even, low, high), jnp.where(even, high, low))
    halo = low.shape[1]
    for which, out in enumerate((to_mate, to_other)):
        part = got[:, which * halo : (which + 1) * halo]
        out[0:half3, :] = pack(part[0 : 2 * half3])
        out[half3 : 2 * half3, :] = pack(part[2 * half3 : 4 * half3])
        out[2 * half3 :, 0:halo] = part[4 * half3 :]
        out[2 * half3 :, halo:] = jnp.zeros_like(part[4 * half3 :])


def unpack_rows(block, half3, halo):
    return jnp.concatenate(
        [unpack(block[0:half3], halo), unpack(block[half3 : 2 * half3], halo), block[2 * half3 :, 0:halo]],
        axis=0,
    )


def beside(rows, mate, other, even, step, half3, halo):
    line = rows.shape[0] - 5
    at = (lax.broadcasted_iota(jnp.int32, (rows.shape[0], 1), 0) == line).astype(jnp.float32) * step
    mate, other = unpack_rows(mate, half3, halo), unpack_rows(other, half3, halo) + 2.0 * at
    return jnp.concatenate(
        [rows + at, jnp.where(even, other, mate), jnp.where(even, mate, other)], axis=1
    )


def select_y_kernel(sides, cur, prev, pos, from_mate, from_other, lists, to_mate, to_other, wide):
    half3 = cur.shape[0] // 2
    atoms = cur.shape[1]
    own = lax.broadcasted_iota(jnp.int32, (1, atoms), 1).astype(jnp.float32)
    rows = jnp.concatenate([cur[...], prev[...], pos[...], own, jnp.zeros((4, atoms), jnp.float32)], axis=0)
    rows = beside(rows, from_mate[...], from_other[...], sides[0] == 0, float(atoms), half3, lists.shape[1])
    wide[...] = rows
    emit(sides[1], rows, lists, to_mate, to_other, half3)


def prepare_kernel(nb, count, w_rad, w_vec, w_mix, w_out, dm, valid, rad_t, vec_t, mix_t, out_t):
    slots, atoms = nb.shape
    lanes = 2 * atoms
    difference_matrix(dm, nb[...], dm.shape[0], atoms)
    lane = lax.broadcasted_iota(jnp.int32, (8, lanes), 1)
    first = jnp.where(lane < atoms, 0, slots // 2)
    limit = jnp.concatenate([count[...], count[...]], axis=1)
    for j in range(slots // 2):
        valid[:, j * lanes : (j + 1) * lanes] = (first + j < limit).astype(jnp.float32)
    rad_t[...] = w_rad[...].T
    vec_t[...] = w_vec[...].T
    mix_t[...] = w_mix[...].T
    out_t[...] = jnp.broadcast_to(w_out[...], (8, w_out.shape[1])).T


def difference_matrix(dm_ref, nb, extended, atoms):
    half = nb.shape[0] // 2
    lanes = 2 * atoms
    paired = jnp.concatenate([nb[:half], nb[half:]], axis=1)
    rows = lax.broadcasted_iota(jnp.int32, (extended, lanes), 0)
    lane = lax.broadcasted_iota(jnp.int32, (extended, lanes), 1)
    own = (rows == jnp.where(lane < atoms, lane, lane - atoms)).astype(jnp.float32)
    for j in range(half):
        hit = (rows == paired[j : j + 1, :]).astype(jnp.float32)
        dm_ref[:, j * lanes : (j + 1) * lanes] = (hit - own).astype(jnp.bfloat16)


def gather_edges(parts16, dm, valid, mv, ef, ee, f2s, hs, vec3, lanes):
    basis, edges = ef.shape
    wide = 2 * lanes
    cut = 1.0 / (CUTOFF * CUTOFF)
    centre = (lax.broadcasted_iota(jnp.int32, (basis, wide), 0).astype(jnp.float32) + 0.5) * (CUTOFF / basis)
    totals = [jnp.zeros((basis, lanes), jnp.float32) for _ in range(4)]
    for j in range(edges // wide):
        at = slice(j * wide, (j + 1) * wide)
        got = dot16(parts16, dm[:, at])
        mv[:, at] = got[:vec3] + got[vec3 : 2 * vec3]
        third = 2 * vec3
        delta = got[third : third + 24] + got[third + 32 : third + 56] + got[third + 64 : third + 88]
        d = [delta[8 * c : 8 * c + 8] for c in range(3)]
        squared = d[0] * d[0] + d[1] * d[1] + d[2] * d[2] + SOFTEN
        radius = jnp.sqrt(squared)
        inverse = 1.0 / radius
        head = [d[c] * inverse for c in range(3)]
        tau = jnp.maximum(1.0 - squared * cut, 0.0)
        env = tau * tau * tau
        env1 = (-6.0 * cut) * radius * tau * tau
        env2 = (24.0 * cut * cut) * squared * tau - (6.0 * cut) * tau * tau
        off = radius - centre
        gauss = jnp.exp(-GAUSS_WIDTH * off * off) * valid[:, at]
        gauss1 = (-2.0 * GAUSS_WIDTH) * off * gauss
        gauss2 = (4.0 * GAUSS_WIDTH * GAUSS_WIDTH * off * off - 2.0 * GAUSS_WIDTH) * gauss
        value = gauss * env
        ef[:, at] = gauss1 * env + gauss * env1
        ee[:, at] = value * inverse
        f2s[:, at] = gauss2 * env + 2.0 * gauss1 * env1 + gauss * env2
        for c in range(3):
            hs[8 * c : 8 * c + 8, at] = head[c]
        hs[24:32, at] = inverse
        terms = [value, value * head[0], value * head[1], value * head[2]]
        totals = [t + v[:, :lanes] + v[:, lanes:] for t, v in zip(totals, terms)]
    return [t + pltpu.roll(t, lanes // 2, 1) for t in totals]


def edge_rows(alpha, beta, ef, ee, f2s, hs, e8, lanes):
    for j in range(ef.shape[1] // lanes):
        at = slice(j * lanes, (j + 1) * lanes)
        head = [hs[8 * c : 8 * c + 8, at] for c in range(3)]
        inverse = hs[24:32, at]
        slope_k, even_k, second = ef[:, at], ee[:, at], f2s[:, at]
        even1 = (slope_k - even_k) * inverse
        even2 = (second - 2.0 * even1) * inverse

        def over(values):
            return jnp.sum(values, axis=0, keepdims=True)

        first = over(alpha * slope_k)
        bend_r = over(alpha * second)
        turn = [over(beta[c] * even1) for c in range(3)]
        twist = [over(beta[c] * even2) for c in range(3)]
        inv1 = inverse[0:1]
        h1 = [head[c][0:1] for c in range(3)]
        radius = 1.0 / inv1
        line = h1[0] * turn[0] + h1[1] * turn[1] + h1[2] * turn[2]
        isotropic = first * inv1 + line
        radial = bend_r + (h1[0] * twist[0] + h1[1] * twist[1] + h1[2] * twist[2]) * radius - isotropic
        e8[:, at] = jnp.concatenate(h1 + [isotropic, radial] + turn, axis=0)


def channel_lift(flow, rad_t, vec_t, mix_t, qs, lanes, atoms):
    channels, basis = rad_t.shape
    lower = lax.broadcasted_iota(jnp.int32, (channels, lanes), 1) < atoms
    lift0 = 2.0 * jnp.where(lower, flow[0], flow[2])
    lift1 = 2.0 * flow[1]
    for i in range(2 * basis):
        k = i % basis
        if i < basis:
            side = jnp.where(lower, jnp.broadcast_to(rad_t[:, k : k + 1], lower.shape), lift1 * vec_t[:, k : k + 1])
        else:
            side = lift0 * vec_t[:, k : k + 1]
        qs[:, i * lanes : (i + 1) * lanes] = dot_split(mix_t, side)


def descriptor_curvature(vec, u, bend, qs, pmat, rmat, lanes, atoms):
    basis = vec.shape[0]
    pairs = 2 * basis
    both = [2.0 * dot32(vec * vec[k : k + 1, :], u) for k in range(basis)]
    low_row = lax.broadcasted_iota(jnp.int32, (1, lanes), 1) < atoms
    for i in range(pairs):
        q_i = qs[:, i * lanes : (i + 1) * lanes] * bend
        for k in range(i + 1):
            q_k = qs[:, k * lanes : (k + 1) * lanes]
            straight = jnp.sum(q_i * q_k, axis=0, keepdims=True)
            crossed = jnp.sum(q_i * pltpu.roll(q_k, atoms, 1), axis=0, keepdims=True)
            if (i < basis) == (k < basis):
                extra = both[i % basis][k % basis : k % basis + 1, :]
                straight = straight + (jnp.where(low_row, 0.0, extra) if i < basis else extra)
            pmat[i * pairs + k : i * pairs + k + 1, :] = straight
            rmat[i * pairs + k : i * pairs + k + 1, :] = crossed
            if k < i:
                pmat[k * pairs + i : k * pairs + i + 1, :] = straight
                rmat[k * pairs + i : k * pairs + i + 1, :] = pltpu.roll(crossed, atoms, 1)


def first_kernel(
    sides, wide, from_mate, from_other, dm, valid, w_rad, w_vec, w_mix, rad_t, vec_t, mix_t, out_t,
    out_m, out_o, out_x, sums, cext, pext, index, ef, ee, e8, pmat, rmat,
    mv, eo, xs, sx, cs, f2s, hs, qs,
    *, vectors, atoms, halo,
):
    half3 = 3 * vectors // 2
    vec3 = 2 * half3
    lanes = 2 * atoms
    rows = beside(wide[...], from_mate[...], from_other[...], sides[1] == 0, 3.0 * atoms, half3, halo)
    cext[...] = rows[:vec3]
    pext[...] = rows[vec3 : 2 * vec3]
    base = 2 * vec3
    places = jnp.round(rows[base + 3 : base + 4]).astype(jnp.int32)
    index[...] = jnp.broadcast_to(places, index.shape)
    shape = (8, rows.shape[1])
    place = jnp.concatenate(
        [jnp.broadcast_to(rows[base + c : base + c + 1], shape) for c in range(3)] + [jnp.zeros(shape, jnp.float32)],
        axis=0,
    )
    parts16 = jnp.concatenate([split(rows[:vec3], 2), split(place, 3)], axis=0)
    descr = gather_edges(parts16, dm, valid, mv, ef, ee, f2s, hs, vec3, lanes)

    rad, vec, mix = w_rad[...], w_vec[...], w_mix[...]
    radt, vect, mixt, outt = rad_t[...], vec_t[...], mix_t[...], out_t[:, 0:1]
    flow = [dot32(vect, descr[c + 1]) for c in range(3)]
    mixed = dot32(radt, descr[0]) + flow[0] * flow[0] + flow[1] * flow[1] + flow[2] * flow[2]
    hidden = dot_split(mixt, mixed)
    gate = 1.0 / (1.0 + jnp.exp(-hidden))
    slope = gate * (1.0 + hidden * (1.0 - gate)) * outt
    bend = gate * (1.0 - gate) * (2.0 + hidden * (1.0 - 2.0 * gate)) * outt
    u = dot_split(mix, slope)
    alpha = dot32(rad, u)
    beta = [2.0 * dot32(vec, flow[c] * u) for c in range(3)]
    edge_rows(alpha, beta, ef, ee, f2s, hs, e8, lanes)
    channel_lift(flow, radt, vect, mixt, qs, lanes, atoms)
    descriptor_curvature(vec, u, bend, qs, pmat, rmat, lanes, atoms)

    result = apply_operator(None, dm, ef, ee, e8, pmat, rmat, mv, eo, xs, sx, cs, atoms, True)
    store_patch((out_m, out_o, out_x), result, pick_matrix(places, 9 * atoms), atoms)

    def gram(left, right, width):
        total = jnp.zeros((vectors, vectors), jnp.float32)
        for c in range(3):
            total = total + dot_split(
                component(left, c, vectors)[:, :width], component(right, c, vectors)[:, :width], NT
            )
        return total

    old_c, old_p = rows[:vec3], rows[vec3 : 2 * vec3]
    extended = rows.shape[1]
    cw, pw = gram(old_c, result, extended), gram(old_p, result, extended)
    cc, cp, pp = gram(old_c, old_c, atoms), gram(old_c, old_p, atoms), gram(old_p, old_p, atoms)
    sums[...] = jnp.concatenate([with_diagonal(cw, pp), pw, cp, join_triangles(cc, pp)], axis=1)


def second_kernel(
    order, own, mate, other, far, cext, pext, index, dm, ef, ee, e8, pmat, rmat,
    out_m, out_o, out_x, shared, rown,
    mv, eo, xs, sx, cs, patch, ring,
    *, vectors, atoms, total_rows,
):
    half3 = 3 * vectors // 2
    vec3 = 2 * half3
    tail = 3 * half3
    pick = pick_matrix(index[0:1, :], 9 * atoms)
    for i, part in enumerate((own, mate, other)):
        ring[order[i]] = part[tail:, :]
    ring[order[3]] = far[...]
    total = ((ring[0] + ring[1]) + (ring[2] + ring[3])) * (1.0 / total_rows)
    v = vectors
    held, pw, cp, joined = (total[:, i * v : (i + 1) * v] for i in range(4))
    coef = jnp.concatenate([from_lower(held), pw], axis=0)
    cc, pp = from_lower(joined), from_upper(joined, held)
    gram_old = jnp.concatenate(
        [jnp.concatenate([cc, cp], axis=1), jnp.concatenate([cp.T, pp], axis=1)], axis=0
    )
    shared[...] = jnp.concatenate([gram_old, coef, jnp.zeros_like(coef)], axis=1)

    for x, ref in enumerate((mate, own, other)):
        for y in range(3):
            at = (3 * y + x) * atoms
            patch[:, at : at + atoms] = unpack(ref[y * half3 : (y + 1) * half3, :], atoms)
    both = dot16(split(patch[...], 2), pick)
    work = both[:vec3] + both[vec3:]
    turned = coef.T
    resid = work - jnp.concatenate(
        [
            dot_split(
                turned,
                jnp.concatenate(
                    [component(cext[...], c, vectors), component(pext[...], c, vectors)], axis=0
                ),
            )
            for c in range(3)
        ],
        axis=0,
    )
    rown[...] = pack(resid[:, :atoms])
    rows = apply_operator(split(resid, 2), dm, ef, ee, e8, pmat, rmat, mv, eo, xs, sx, cs, atoms)
    store_patch((out_m, out_o, out_x), rows, pick, atoms)


def gram_kernel(rown, y0, ym, yo, out, yown, *, vectors, atoms):
    work = y0[...] + ym[...] + yo[...]
    yown[...] = work
    r, y = unpack(rown[...], atoms), unpack(work, atoms)
    gram = jnp.zeros((2 * vectors, 2 * vectors), jnp.float32)
    for c in range(3):
        stacked = jnp.concatenate([component(r, c, vectors), component(y, c, vectors)], axis=0)
        gram = gram + dot_split(stacked, stacked, NT)
    v = vectors
    rr, ry, yy = gram[:v, :v], gram[:v, v:], gram[v:, v:]
    lanes = out.shape[2]
    sent = jnp.concatenate(
        [flatten(join_triangles(rr, yy), lanes), flatten(with_diagonal(ry, yy), lanes)], axis=0
    )
    out[...] = jnp.broadcast_to(sent[None], out.shape)


def cholesky(matrix):
    size = matrix.shape[0]
    rows = lax.broadcasted_iota(jnp.int32, (size, 2 * size), 0)
    lane = lax.broadcasted_iota(jnp.int32, (size, 2 * size), 1)
    unit = (lane - size == rows).astype(jnp.float32)
    work = jnp.concatenate([matrix, jnp.zeros_like(matrix)], axis=1) + unit
    done = jnp.zeros_like(work)
    for j in range(size):
        line = work[j : j + 1, :]
        pivot = work[j : j + 1, j : j + 1]
        scale = lax.rsqrt(pivot)
        scale = scale * (1.5 - 0.5 * pivot * scale * scale)
        line = line * scale
        column = work[:, j : j + 1] * scale
        done = jnp.where(rows == j, line, done)
        work = work - column * line
    upper = jnp.where(lane >= rows, done, 0.0)[:, :size]
    return upper, done[:, size:]


def final_kernel(got, sums, rown, yown, cown, blocks, factors, *, vectors, atoms, total_rows):
    devices = got.shape[0]
    total = got[0]
    for i in range(1, devices):
        total = total + got[i]
    total = total * (1.0 / total_rows)
    v = vectors
    count = total.shape[0] // 2
    joined, held = unflatten(total[:count], v), unflatten(total[count:], v)
    rr, ry, yy = from_lower(joined), from_lower(held), from_upper(joined, held)
    shared = sums[...]
    gram_old = shared[:, : 2 * v]
    coef1 = shared[:, 2 * v : 3 * v]
    rows = lax.broadcasted_iota(jnp.int32, (v, v), 0)
    cols = lax.broadcasted_iota(jnp.int32, (v, v), 1)
    unit = (rows == cols).astype(jnp.float32)

    upper1, inv1 = cholesky(rr)
    left = coef1 - dot32(gram_old, coef1)
    wr = rr + dot32(coef1, left, TN)
    coef_x = dot32(dot32(inv1, ry), inv1, NT)
    coef_c = dot32(wr, inv1, NT)
    cross = dot32(left[:v], inv1, NT)
    yy1 = dot32(dot32(inv1, yy), inv1, NT)
    coef2 = jnp.concatenate([coef_x, coef_c], axis=0)
    basis = jnp.concatenate(
        [
            jnp.concatenate([-unit, cross.T], axis=1),
            jnp.concatenate([cross, gram_old[:v, :v] - 2.0 * unit], axis=1),
        ],
        axis=0,
    )
    gram2 = yy1 + dot32(coef2, dot32(basis, coef2), TN)
    upper2, inv2 = cholesky(gram2)
    by_x = dot32(inv2, coef_x, NT)
    m_y = dot32(inv2, inv1)
    m_r = -dot32(by_x, inv1)
    m_c = -dot32(inv2, coef_c, NT)
    weights = jnp.concatenate([m_y, m_r, m_c], axis=1)
    factors[0] = upper1.T
    factors[1] = upper2.T
    r, y, old = unpack(rown[...], atoms), unpack(yown[...], atoms), cown[...]
    for c in range(3):
        parts = [component(part, c, vectors) for part in (y, r, old)]
        blocks[0, c] = dot32(inv1, parts[1])
        blocks[1, c] = dot32(weights, jnp.concatenate(parts, axis=0))


def mates(count):
    mate = [i ^ 1 for i in range(count)]
    other = [(i - 1) % count if i % 2 == 0 else (i + 1) % count for i in range(count)]
    return mate, other


def fetch(values, axis, sources):
    return lax.ppermute(values, axis, [(s, i) for i, s in enumerate(sources)])


def vmem_call(kernel, outs, scratch=(), scalars=0, **cost):
    def call(*operands):
        spaces = [pltpu.SMEM] * scalars + [pltpu.VMEM] * (len(operands) - scalars)
        return pl.pallas_call(
            kernel,
            out_shape=outs,
            in_specs=[pl.BlockSpec(memory_space=s) for s in spaces],
            out_specs=jax.tree.map(lambda _: pl.BlockSpec(memory_space=pltpu.VMEM), outs),
            scratch_shapes=list(scratch),
            compiler_params=pltpu.CompilerParams(vmem_limit_bytes=VMEM_BYTES),
            cost_estimate=pl.CostEstimate(
                flops=cost.get("flops", 1 << 20), bytes_accessed=1 << 16, transcendentals=0
            ),
        )(*operands)

    return call


def f32(*shape):
    return jax.ShapeDtypeStruct(shape, jnp.float32)


def shards(positions, block_prev, block_cur, neighbours, counts, x_lists, y_lists, w_radial, w_vector, w_mix, w_out):
    vectors, _, atoms = block_cur.shape
    halo = x_lists.shape[2]
    slots = neighbours.shape[0]
    basis, channels = w_radial.shape
    n_x, n_y = lax.axis_size("gx"), lax.axis_size("gy")
    total_rows = 3.0 * atoms * n_x * n_y
    half3 = 3 * vectors // 2
    vec3 = 3 * vectors
    lanes = 2 * atoms
    edges = slots * atoms
    extended = atoms + 4 * halo
    pairs = 2 * basis
    mate_x, other_x = mates(n_x)
    mate_y, other_y = mates(n_y)
    at_x, at_y = lax.axis_index("gx"), lax.axis_index("gy")
    sides = jnp.stack([at_x % 2, at_y % 2]).astype(jnp.int32)
    own_rows = 2 * half3 + 8

    cur = block_cur.transpose(1, 0, 2).reshape(vec3, atoms)
    prev = block_prev.transpose(1, 0, 2).reshape(vec3, atoms)
    slab = f32(own_rows, lanes)
    to_mate, to_other = vmem_call(select_x_kernel, [slab, slab], scalars=1)(
        sides, cur, prev, positions, x_lists[0]
    )
    mate1 = fetch(to_mate, "gx", mate_x)
    other1 = fetch(to_other, "gx", other_x)
    dm, valid, rad_t, vec_t, mix_t, out_t = vmem_call(
        prepare_kernel,
        [
            jax.ShapeDtypeStruct((extended, edges), jnp.bfloat16),
            f32(8, edges),
            f32(channels, basis),
            f32(channels, basis),
            f32(channels, channels),
            f32(channels, 8),
        ],
        flops=1 << 24,
    )(neighbours, counts[None], w_radial, w_vector, w_mix, w_out[None])
    to_mate, to_other, wide = vmem_call(
        select_y_kernel, [slab, slab, f32(2 * vec3 + 8, atoms + 2 * halo)], scalars=1
    )(sides, cur, prev, positions, mate1, other1, y_lists[0])
    mate2 = fetch(to_mate, "gy", mate_y)
    other2 = fetch(to_other, "gy", other_y)

    work_scratch = [
        pltpu.VMEM((vec3, edges), jnp.float32),
        pltpu.VMEM((vec3, edges), jnp.float32),
        pltpu.VMEM((pairs, vectors, lanes), jnp.float32),
        pltpu.VMEM((pairs, vectors, lanes), jnp.float32),
        pltpu.VMEM((2 * pairs, vectors, lanes), jnp.float32),
    ]
    first = vmem_call(
        functools.partial(first_kernel, vectors=vectors, atoms=atoms, halo=halo),
        [
            f32(3 * half3, lanes),
            f32(3 * half3, lanes),
            f32(3 * half3, lanes),
            f32(vectors, lanes),
            f32(vec3, extended),
            f32(vec3, extended),
            jax.ShapeDtypeStruct((8, extended), jnp.int32),
            f32(basis, edges),
            f32(basis, edges),
            f32(8, edges),
            f32(pairs * pairs, lanes),
            f32(pairs * pairs, lanes),
        ],
        work_scratch
        + [
            pltpu.VMEM((basis, edges), jnp.float32),
            pltpu.VMEM((32, edges), jnp.float32),
            pltpu.VMEM((channels, pairs * lanes), jnp.float32),
        ],
        scalars=1,
        flops=1 << 31,
    )
    part_m, part_0, part_o, local, cext, pext, index, ef, ee, e8, pmat, rmat = first(
        sides, wide, mate2, other2, dm, valid, w_radial, w_vector, w_mix, rad_t, vec_t, mix_t, out_t
    )

    back_m = fetch(part_m, "gx", mate_x)
    back_o = fetch(part_o, "gx", other_x)
    strided = [local] + [
        fetch(local, "gx", [(i + d) % n_x for i in range(n_x)]) for d in range(4, n_x, 4)
    ]
    if len(strided) == 2:
        local = strided[0] + strided[1]
    else:
        local = jnp.sum(jnp.roll(jnp.stack(strided), at_x // 4, axis=0), axis=0)
    folded = part_0 + back_m + back_o
    f_m, f_0, f_o = folded[:half3], folded[half3 : 2 * half3], folded[2 * half3 :]

    far_m = [other_y[m] for m in mate_y]
    far_o = [mate_y[o] for o in other_y]
    got_m = fetch(jnp.concatenate([f_0, f_m, local]), "gy", mate_y)
    got_o = fetch(jnp.concatenate([f_0, f_o, local]), "gy", other_y)
    if far_m == far_o:
        got_2 = fetch(jnp.concatenate([f_m, f_o, local]), "gy", far_m)
        far_mate, far_other = got_2[half3 : 2 * half3], got_2[:half3]
        sums = (local + got_m[2 * half3 :]) + (got_o[2 * half3 :] + got_2[2 * half3 :])
    else:
        far_mate = fetch(f_o, "gy", far_m)
        far_other = fetch(f_m, "gy", far_o)
        terms = [local] + [
            fetch(local, "gy", [(i + d) % n_y for i in range(n_y)]) for d in range(1, n_y)
        ]
        sums = jnp.sum(jnp.roll(jnp.stack(terms), at_y, axis=0), axis=0)
    w_m = got_m[:half3] + f_m + far_mate
    w_0 = f_0 + got_m[half3 : 2 * half3] + got_o[half3 : 2 * half3]
    w_o = got_o[:half3] + far_other + f_o
    column = jnp.concatenate([w_m, w_0, w_o, sums])

    col_m = fetch(column, "gx", mate_x)
    col_o = fetch(column, "gx", other_x)
    far = fetch(sums, "gx", [(i + 2) % n_x for i in range(n_x)])
    order = jnp.stack(
        [at_x % 4, (at_x ^ 1) % 4, (at_x - 1 + 2 * (at_x % 2)) % 4, (at_x + 2) % 4]
    ).astype(jnp.int32)

    second = vmem_call(
        functools.partial(second_kernel, vectors=vectors, atoms=atoms, total_rows=total_rows),
        [
            f32(3 * half3, lanes),
            f32(3 * half3, lanes),
            f32(3 * half3, lanes),
            f32(2 * vectors, lanes),
            f32(half3, lanes),
        ],
        work_scratch
        + [pltpu.VMEM((vec3, 9 * atoms), jnp.float32), pltpu.VMEM((4, vectors, lanes), jnp.float32)],
        scalars=1,
        flops=1 << 30,
    )
    part_m, part_0, part_o, shared, rown = second(
        order, column, col_m, col_o, far, cext, pext, index, dm, ef, ee, e8, pmat, rmat
    )
    back_m = fetch(part_m, "gx", mate_x)
    back_o = fetch(part_o, "gx", other_x)
    folded = part_0 + back_m + back_o
    y_m = fetch(folded[:half3], "gy", mate_y)
    y_o = fetch(folded[2 * half3 :], "gy", other_y)

    sent_rows = 2 * vectors * vectors // lanes
    spread, yown = vmem_call(
        functools.partial(gram_kernel, vectors=vectors, atoms=atoms),
        [f32(n_x * n_y, sent_rows, lanes), f32(half3, lanes)],
    )(rown, folded[half3 : 2 * half3], y_m, y_o)
    got = lax.all_to_all(spread, ("gx", "gy"), 0, 0)
    blocks, factors = vmem_call(
        functools.partial(final_kernel, vectors=vectors, atoms=atoms, total_rows=total_rows),
        [f32(2, 3, vectors, atoms), f32(2, vectors, vectors)],
    )(got, shared, rown, yown, cur)
    return blocks.transpose(0, 2, 1, 3), factors


def solution(mesh):
    placed = (
        P(None, ("gx", "gy")),
        P(None, None, ("gx", "gy")),
        P(None, None, ("gx", "gy")),
        P(None, ("gx", "gy")),
        P(("gx", "gy")),
        P(("gx", "gy"), None, None),
        P(("gx", "gy"), None, None),
        P(),
        P(),
        P(),
        P(),
    )
    return jax.shard_map(
        shards,
        mesh=mesh,
        in_specs=placed,
        out_specs=(P(None, None, None, ("gx", "gy")), P()),
        check_vma=False,
    )
```

```python
import functools

import jax
import jax.numpy as jnp
from jax import lax
from jax.experimental import pallas as pl
from jax.experimental.pallas import tpu as pltpu
from jax.sharding import PartitionSpec as P

SOFTEN = 0.25
CUTOFF = 5.0
GAUSS_WIDTH = 2.0
EXACT = lax.Precision.HIGHEST
VMEM_BYTES = 48 * 1024 * 1024
NN = (((1,), (0,)), ((), ()))
NT = (((1,), (1,)), ((), ()))
TN = (((0,), (0,)), ((), ()))


def dot16(left, right, dims=NN):
    return lax.dot_general(left, right, dims, preferred_element_type=jnp.float32)


def dot32(left, right, dims=NN):
    return lax.dot_general(
        left, right, dims, precision=EXACT, preferred_element_type=jnp.float32
    )


def split(values, parts):
    pieces = []
    for _ in range(parts):
        piece = values.astype(jnp.bfloat16)
        pieces.append(piece)
        values = values - piece.astype(jnp.float32)
    return jnp.concatenate(pieces, axis=0)


def dot_split(left, right, dims=NN):
    if dims == TN:
        left = left.T
        dims = NN
    rows = left.shape[0]
    both = split(left, 2)
    high = right.astype(jnp.bfloat16)
    low = (right - high.astype(jnp.float32)).astype(jnp.bfloat16)
    first = dot16(both, high, dims)
    return first[:rows] + first[rows:] + dot16(both[:rows], low, dims)


def component(block, comp, vectors):
    return block[comp * vectors : (comp + 1) * vectors]


def unpack(packed, atoms):
    return jnp.concatenate([packed[:, :atoms], packed[:, atoms:]], axis=0)


def pack(rows):
    half = rows.shape[0] // 2
    return jnp.concatenate([rows[:half], rows[half:]], axis=1)


def pick_matrix(index_row, patch_rows):
    extended = index_row.shape[1]
    rows = lax.broadcasted_iota(jnp.int32, (patch_rows, extended), 0)
    return (rows == index_row).astype(jnp.float32).astype(jnp.bfloat16)


def select(rows, first, second):
    picks = jnp.concatenate([first, second], axis=1)
    hits = lax.broadcasted_iota(jnp.int32, (rows.shape[1], picks.shape[1]), 0) == picks
    got = dot16(split(rows, 3), hits.astype(jnp.float32).astype(jnp.bfloat16))
    count = rows.shape[0]
    return got[:count] + (got[count : 2 * count] + got[2 * count :])


def rows_and_cols(size):
    return (
        lax.broadcasted_iota(jnp.int32, (size, size), 0),
        lax.broadcasted_iota(jnp.int32, (size, size), 1),
    )


def join_triangles(lower, upper):
    rows, cols = rows_and_cols(lower.shape[0])
    return jnp.where(rows >= cols, lower, upper)


def with_diagonal(lower, source):
    size = lower.shape[0]
    rows, cols = rows_and_cols(size)
    line = jnp.sum(jnp.where(rows == cols, source, 0.0), axis=0, keepdims=True)
    upper = jnp.where(rows == 0, line, jnp.where((rows == 1) & (cols == size - 1), source[0:1, 0:1], 0.0))
    return jnp.where(rows >= cols, lower, upper)


def from_lower(joined):
    rows, cols = rows_and_cols(joined.shape[0])
    strict = jnp.where(rows > cols, joined, 0.0)
    return jnp.where(rows >= cols, joined, 0.0) + strict.T


def from_upper(joined, holder):
    size = joined.shape[0]
    rows, cols = rows_and_cols(size)
    strict = jnp.where(rows < cols, joined, 0.0)
    line = jnp.where(cols[0:1] >= 1, holder[0:1], holder[1:2, size - 1 : size])
    return strict + strict.T + jnp.where(rows == cols, line, 0.0)


def flatten(square, lanes):
    size = square.shape[0]
    rows = size * size // lanes
    return jnp.concatenate([square[i * rows : (i + 1) * rows] for i in range(lanes // size)], axis=1)


def unflatten(flat, size):
    return jnp.concatenate(
        [flat[:, i * size : (i + 1) * size] for i in range(flat.shape[1] // size)], axis=0
    )


def apply_operator(parts16, dm_ref, ef_ref, ee_ref, e8_ref, p_ref, r_ref, mv_ref, eo_ref, xs_ref, sx_ref, cs_ref, atoms, moved_ready=False):
    lanes = 2 * atoms
    edges = dm_ref.shape[1]
    groups = edges // lanes
    basis = ef_ref.shape[0]
    vec3 = mv_ref.shape[0]
    vectors = vec3 // 3
    pairs = 2 * basis
    tiles = vec3 // 24
    lower = lax.broadcasted_iota(jnp.int32, (8, lanes), 1) < atoms

    def rows_of(tile, comp):
        return comp * vectors + tile * 8

    if not moved_ready:
        wide = 2 * lanes
        for j in range(edges // wide):
            got = dot16(parts16, dm_ref[:, j * wide : (j + 1) * wide])
            mv_ref[:, j * wide : (j + 1) * wide] = got[:vec3] + got[vec3 : 2 * vec3]

    for tile in range(tiles):

        def gather_step(j, acc, tile=tile):
            at = pl.ds(pl.multiple_of(j * lanes, lanes), lanes)
            m = [mv_ref[rows_of(tile, c) : rows_of(tile, c) + 8, at] for c in range(3)]
            head = [e8_ref[c : c + 1, at] for c in range(3)]
            u = head[0] * m[0] + head[1] * m[1] + head[2] * m[2]
            along = [head[c] * u for c in range(3)]
            across = [m[c] - along[c] for c in range(3)]
            new = list(acc)
            for k in range(basis):
                slope = ef_ref[k : k + 1, at]
                even = ee_ref[k : k + 1, at]
                new[k] = new[k] + slope * u
                for c in range(3):
                    i = (c + 1) * basis + k
                    new[i] = new[i] + (slope * along[c] + even * across[c])
            return tuple(new)

        zero = jnp.zeros((8, lanes), jnp.float32)
        acc = lax.fori_loop(0, groups, gather_step, (zero,) * (4 * basis), unroll=groups)
        for i in range(pairs):
            a, b = acc[i], acc[i + pairs]
            x = jnp.where(lower, a, b) + pltpu.roll(jnp.where(lower, b, a), atoms, 1)
            xs_ref[i, tile * 8 : tile * 8 + 8, :] = x
            sx_ref[i, tile * 8 : tile * 8 + 8, :] = pltpu.roll(x, atoms, 1)

    wide_lower = lax.broadcasted_iota(jnp.int32, (8 * tiles, lanes), 1) < atoms

    def mix_step(kappa, carry):
        at = pl.ds(pl.multiple_of(kappa * pairs, pairs), pairs)
        straight = p_ref[at, :]
        crossed = r_ref[at, :]
        y = jnp.zeros((8 * tiles, lanes), jnp.float32)
        for i in range(pairs):
            y = y + straight[i : i + 1, :] * xs_ref[i] + crossed[i : i + 1, :] * sx_ref[i]
        turned = pltpu.roll(y, atoms, 1)
        cs_ref[kappa] = jnp.where(wide_lower, y, turned)
        cs_ref[kappa + pairs] = jnp.where(wide_lower, turned, y)
        return carry

    lax.fori_loop(0, pairs, mix_step, 0, unroll=4)

    for tile in range(tiles):
        coeff = [cs_ref[i, tile * 8 : tile * 8 + 8, :] for i in range(4 * basis)]

        def spread_step(j, carry, tile=tile, coeff=coeff):
            at = pl.ds(pl.multiple_of(j * lanes, lanes), lanes)
            m = [mv_ref[rows_of(tile, c) : rows_of(tile, c) + 8, at] for c in range(3)]
            row = [e8_ref[i : i + 1, at] for i in range(8)]
            head, turn = row[0:3], row[5:8]
            u = head[0] * m[0] + head[1] * m[1] + head[2] * m[2]
            radial = row[4] * u + (turn[0] * m[0] + turn[1] * m[1] + turn[2] * m[2])
            sums, evens = [None] * 3, [None] * 3
            for k in range(basis):
                slope = ef_ref[k : k + 1, at]
                even = ee_ref[k : k + 1, at]
                radial = radial + slope * coeff[k]
                for c in range(3):
                    i = (c + 1) * basis + k
                    more, plus = slope * coeff[i], even * coeff[i]
                    sums[c] = more if k == 0 else sums[c] + more
                    evens[c] = plus if k == 0 else evens[c] + plus
            for c in range(3):
                radial = radial + head[c] * (sums[c] - evens[c])
            for c in range(3):
                out = evens[c] + head[c] * radial + (row[3] * m[c] + turn[c] * u)
                eo_ref[rows_of(tile, c) : rows_of(tile, c) + 8, at] = out
            return carry

        lax.fori_loop(0, groups, spread_step, 0, unroll=groups)

    spread = dot16(split(eo_ref[...], 2), dm_ref[...], NT)
    return spread[:vec3] + spread[vec3:]


def stacked_sums(parts):
    row = lax.broadcasted_iota(jnp.int32, parts[0].shape, 0)

    def moved(values, by):
        return values + pltpu.roll(values, by % 8, 0)

    upper = row < 4
    fours = [
        jnp.where(upper, parts[i], parts[i + 4]) + pltpu.roll(jnp.where(upper, parts[i + 4], parts[i]), 4, 0)
        for i in range(4)
    ]
    twos = [jnp.where(row % 4 < 2, moved(fours[i], -2), moved(fours[i + 2], 2)) for i in range(2)]
    return jnp.where(row % 2 < 1, moved(twos[0], -1), moved(twos[1], 1))


def store_patch(outs, extended_rows, pick, atoms):
    vec3 = extended_rows.shape[0]
    half3 = vec3 // 2
    both = dot16(split(extended_rows, 2), pick, NT)
    patch = both[:vec3] + both[vec3:]
    for x in range(3):
        for y in range(3):
            at = (3 * y + x) * atoms
            tile = patch[:, at : at + atoms]
            outs[x][y * half3 : (y + 1) * half3, 0:atoms] = tile[:half3]
            outs[x][y * half3 : (y + 1) * half3, atoms : 2 * atoms] = tile[half3:]


def select_x_kernel(sides, table, to_mate, to_other):
    rows = table[: table.shape[0] - 8, :]
    lists = table[table.shape[0] - 8 :, :].astype(jnp.int32)
    emit(sides[0], rows, lists[0:2], to_mate, to_other, (rows.shape[0] - 8) // 4)


def emit(side, rows, lists, to_mate, to_other, half3):
    even = side == 0
    low, high = lists[0:1, :], lists[1:2, :]
    got = select(rows, jnp.where(even, low, high), jnp.where(even, high, low))
    halo = low.shape[1]
    for which, out in enumerate((to_mate, to_other)):
        part = got[:, which * halo : (which + 1) * halo]
        out[0:half3, :] = pack(part[0 : 2 * half3])
        out[half3 : 2 * half3, :] = pack(part[2 * half3 : 4 * half3])
        out[2 * half3 :, 0:halo] = part[4 * half3 :]
        out[2 * half3 :, halo:] = jnp.zeros_like(part[4 * half3 :])


def unpack_rows(block, half3, halo):
    return jnp.concatenate(
        [unpack(block[0:half3], halo), unpack(block[half3 : 2 * half3], halo), block[2 * half3 :, 0:halo]],
        axis=0,
    )


def beside(rows, mate, other, even, step, half3, halo):
    line = rows.shape[0] - 5
    at = (lax.broadcasted_iota(jnp.int32, (rows.shape[0], 1), 0) == line).astype(jnp.float32) * step
    mate, other = unpack_rows(mate, half3, halo), unpack_rows(other, half3, halo) + 2.0 * at
    return jnp.concatenate(
        [rows + at, jnp.where(even, other, mate), jnp.where(even, mate, other)], axis=1
    )


def select_y_kernel(sides, table, from_mate, from_other, to_mate, to_other, wide):
    atoms = table.shape[1]
    rows = table[: table.shape[0] - 8, :]
    lists = table[table.shape[0] - 8 :, :].astype(jnp.int32)
    half3 = (rows.shape[0] - 8) // 4
    got = beside(rows, from_mate[...], from_other[...], sides[0] == 0, float(atoms), half3, atoms)
    wide[...] = got
    emit(sides[1], got, lists[2:4], to_mate, to_other, half3)


def prepare_kernel(table, dm, valid, rad, vec, mix, rad_t, vec_t, mix_t, out_t, *, slots, atoms):
    lanes = 2 * atoms
    basis, channels = rad.shape
    starts = [0, channels, channels + basis, channels + 2 * basis, channels + 2 * basis + 8]
    w_mix, w_rad, w_vec = (table[starts[i] : starts[i + 1], :] for i in range(3))
    w_out = table[starts[3] : starts[4], :]
    ints = table[starts[4] :, 0:atoms].astype(jnp.int32)
    nb, count = ints[:slots], ints[slots : slots + 1]
    difference_matrix(dm, nb, dm.shape[0], atoms)
    lane = lax.broadcasted_iota(jnp.int32, (8, lanes), 1)
    first = jnp.where(lane < atoms, 0, slots // 2)
    limit = jnp.concatenate([count, count], axis=1)
    for j in range(slots // 2):
        valid[:, j * lanes : (j + 1) * lanes] = (first + j < limit).astype(jnp.float32)
    rad[...] = w_rad
    vec[...] = w_vec
    mix[...] = w_mix
    rad_t[...] = w_rad.T
    vec_t[...] = w_vec.T
    mix_t[...] = w_mix.T
    out_t[...] = w_out.T


def difference_matrix(dm_ref, nb, extended, atoms):
    half = nb.shape[0] // 2
    lanes = 2 * atoms
    paired = jnp.concatenate([nb[:half], nb[half:]], axis=1)
    rows = lax.broadcasted_iota(jnp.int32, (extended, lanes), 0)
    lane = lax.broadcasted_iota(jnp.int32, (extended, lanes), 1)
    own = (rows == jnp.where(lane < atoms, lane, lane - atoms)).astype(jnp.float32)
    for j in range(half):
        hit = (rows == paired[j : j + 1, :]).astype(jnp.float32)
        dm_ref[:, j * lanes : (j + 1) * lanes] = (hit - own).astype(jnp.bfloat16)


def gather_edges(parts16, dm, valid, mv, ef, ee, f2s, hs, vec3, lanes):
    basis, edges = ef.shape
    wide = 2 * lanes
    cut = 1.0 / (CUTOFF * CUTOFF)
    centre = (lax.broadcasted_iota(jnp.int32, (basis, wide), 0).astype(jnp.float32) + 0.5) * (CUTOFF / basis)
    totals = [jnp.zeros((basis, lanes), jnp.float32) for _ in range(4)]
    for j in range(edges // wide):
        at = slice(j * wide, (j + 1) * wide)
        got = dot16(parts16, dm[:, at])
        mv[:, at] = got[:vec3] + got[vec3 : 2 * vec3]
        third = 2 * vec3
        delta = got[third : third + 24] + got[third + 32 : third + 56] + got[third + 64 : third + 88]
        d = [delta[8 * c : 8 * c + 8] for c in range(3)]
        squared = d[0] * d[0] + d[1] * d[1] + d[2] * d[2] + SOFTEN
        radius = jnp.sqrt(squared)
        inverse = 1.0 / radius
        head = [d[c] * inverse for c in range(3)]
        tau = jnp.maximum(1.0 - squared * cut, 0.0)
        env = tau * tau * tau
        env1 = (-6.0 * cut) * radius * tau * tau
        env2 = (24.0 * cut * cut) * squared * tau - (6.0 * cut) * tau * tau
        off = radius - centre
        gauss = jnp.exp(-GAUSS_WIDTH * off * off) * valid[:, at]
        gauss1 = (-2.0 * GAUSS_WIDTH) * off * gauss
        gauss2 = (4.0 * GAUSS_WIDTH * GAUSS_WIDTH * off * off - 2.0 * GAUSS_WIDTH) * gauss
        value = gauss * env
        ef[:, at] = gauss1 * env + gauss * env1
        ee[:, at] = value * inverse
        f2s[:, at] = gauss2 * env + 2.0 * gauss1 * env1 + gauss * env2
        for c in range(3):
            hs[8 * c : 8 * c + 8, at] = head[c]
        hs[24:32, at] = inverse
        terms = [value, value * head[0], value * head[1], value * head[2]]
        totals = [t + v[:, :lanes] + v[:, lanes:] for t, v in zip(totals, terms)]
    return [t + pltpu.roll(t, lanes // 2, 1) for t in totals]


def edge_rows(alpha, beta, ef, ee, f2s, hs, e8, lanes):
    for j in range(ef.shape[1] // lanes):
        at = slice(j * lanes, (j + 1) * lanes)
        head = [hs[8 * c : 8 * c + 8, at] for c in range(3)]
        inverse = hs[24:32, at]
        slope_k, even_k, second = ef[:, at], ee[:, at], f2s[:, at]
        even1 = (slope_k - even_k) * inverse
        even2 = (second - 2.0 * even1) * inverse

        sums = stacked_sums(
            [alpha * slope_k, alpha * second]
            + [beta[c] * even1 for c in range(3)]
            + [beta[c] * even2 for c in range(3)]
        )
        first, bend_r = sums[0:1], sums[1:2]
        turn = [sums[2 + c : 3 + c] for c in range(3)]
        twist = [sums[5 + c : 6 + c] for c in range(3)]
        inv1 = inverse[0:1]
        h1 = [head[c][0:1] for c in range(3)]
        radius = 1.0 / inv1
        line = h1[0] * turn[0] + h1[1] * turn[1] + h1[2] * turn[2]
        isotropic = first * inv1 + line
        radial = bend_r + (h1[0] * twist[0] + h1[1] * twist[1] + h1[2] * twist[2]) * radius - isotropic
        e8[:, at] = jnp.concatenate(h1 + [isotropic, radial] + turn, axis=0)


def channel_lift(flow, rad_t, vec_t, mix_t, qs, qr, lanes, atoms):
    channels, basis = rad_t.shape
    lower = lax.broadcasted_iota(jnp.int32, (channels, lanes), 1) < atoms
    lift0 = 2.0 * jnp.where(lower, flow[0], flow[2])
    lift1 = 2.0 * flow[1]
    for i in range(2 * basis):
        k = i % basis
        if i < basis:
            side = jnp.where(lower, jnp.broadcast_to(rad_t[:, k : k + 1], lower.shape), lift1 * vec_t[:, k : k + 1])
        else:
            side = lift0 * vec_t[:, k : k + 1]
        lifted = dot_split(mix_t, side)
        qs[:, i * lanes : (i + 1) * lanes] = lifted
        qr[:, i * lanes : (i + 1) * lanes] = pltpu.roll(lifted, atoms, 1)


def descriptor_curvature(vec, u, bend, qs, qr, bd, both, pmat, rmat, lanes, atoms):
    basis = vec.shape[0]
    pairs = 2 * basis
    channels = bend.shape[0]
    bd[...] = bend
    low_row = lax.broadcasted_iota(jnp.int32, (basis, lanes), 1) < atoms
    for k in range(basis):
        both[k] = 2.0 * dot32(vec * vec[k : k + 1, :], u)

    def block(i, column):
        accs = None
        for tile in range(channels // 8):
            rows = slice(8 * tile, 8 * tile + 8)
            weight = bd[rows, :]
            left = [
                qs[rows, pl.ds(pl.multiple_of((i + d) * lanes, lanes), lanes)] * weight for d in range(2)
            ]
            columns = [slice((column + k) * lanes, (column + k + 1) * lanes) for k in range(basis)]
            right = [ref[rows, at] for ref in (qs, qr) for at in columns]
            terms = [l * r for l in left for r in right]
            accs = terms if accs is None else [a + t for a, t in zip(accs, terms)]
        return [stacked_sums(accs[q * basis : (q + 1) * basis]) for q in range(4)]

    def put(i, column, tiles):
        for d in range(2):
            at = pl.ds(pl.multiple_of((i + d) * pairs + column, basis), basis)
            pmat[at, :] = tiles[2 * d]
            rmat[at, :] = tiles[2 * d + 1]

    def upper_step(step, carry):
        i = 2 * step
        tiles = block(i, 0)
        for d in range(2):
            tiles[2 * d] = tiles[2 * d] + jnp.where(low_row, 0.0, both[i + d])
        put(i, 0, tiles)
        return carry

    def lower_step(step, carry):
        i = 2 * step + basis
        tiles = block(i, 0)
        put(i, 0, tiles)
        for d in range(2):
            pmat[pl.ds(i + d, basis, pairs), :] = tiles[2 * d]
            rmat[pl.ds(i + d, basis, pairs), :] = pltpu.roll(tiles[2 * d + 1], atoms, 1)
        tiles = block(i, basis)
        for d in range(2):
            tiles[2 * d] = tiles[2 * d] + both[i + d - basis]
        put(i, basis, tiles)
        return carry

    lax.fori_loop(0, basis // 2, upper_step, 0)
    lax.fori_loop(0, basis // 2, lower_step, 0)


def first_kernel(
    sides, wide, from_mate, from_other, dm, valid, w_rad, w_vec, w_mix, rad_t, vec_t, mix_t, out_t,
    out_m, out_o, out_x, sums, cext, pext, index, ef, ee, e8, pmat, rmat,
    mv, eo, xs, sx, cs, f2s, hs, qs, qr, bd, both,
    *, vectors, atoms, halo,
):
    half3 = 3 * vectors // 2
    vec3 = 2 * half3
    lanes = 2 * atoms
    rows = beside(wide[...], from_mate[...], from_other[...], sides[1] == 0, 3.0 * atoms, half3, halo)
    cext[...] = rows[:vec3]
    pext[...] = rows[vec3 : 2 * vec3]
    base = 2 * vec3
    places = jnp.round(rows[base + 3 : base + 4]).astype(jnp.int32)
    index[...] = jnp.broadcast_to(places, index.shape)
    shape = (8, rows.shape[1])
    place = jnp.concatenate(
        [jnp.broadcast_to(rows[base + c : base + c + 1], shape) for c in range(3)] + [jnp.zeros(shape, jnp.float32)],
        axis=0,
    )
    parts16 = jnp.concatenate([split(rows[:vec3], 2), split(place, 3)], axis=0)
    descr = gather_edges(parts16, dm, valid, mv, ef, ee, f2s, hs, vec3, lanes)

    rad, vec, mix = w_rad[...], w_vec[...], w_mix[...]
    radt, vect, mixt, outt = rad_t[...], vec_t[...], mix_t[...], out_t[:, 0:1]
    flow = [dot32(vect, descr[c + 1]) for c in range(3)]
    mixed = dot32(radt, descr[0]) + flow[0] * flow[0] + flow[1] * flow[1] + flow[2] * flow[2]
    hidden = dot_split(mixt, mixed)
    gate = 1.0 / (1.0 + jnp.exp(-hidden))
    slope = gate * (1.0 + hidden * (1.0 - gate)) * outt
    bend = gate * (1.0 - gate) * (2.0 + hidden * (1.0 - 2.0 * gate)) * outt
    u = dot_split(mix, slope)
    alpha = dot32(rad, u)
    beta = [2.0 * dot32(vec, flow[c] * u) for c in range(3)]
    edge_rows(alpha, beta, ef, ee, f2s, hs, e8, lanes)
    channel_lift(flow, radt, vect, mixt, qs, qr, lanes, atoms)
    descriptor_curvature(vec, u, bend, qs, qr, bd, both, pmat, rmat, lanes, atoms)

    result = apply_operator(None, dm, ef, ee, e8, pmat, rmat, mv, eo, xs, sx, cs, atoms, True)
    store_patch((out_m, out_o, out_x), result, pick_matrix(places, 9 * atoms), atoms)

    def gram(left, right, width):
        total = jnp.zeros((vectors, vectors), jnp.float32)
        for c in range(3):
            total = total + dot_split(
                component(left, c, vectors)[:, :width], component(right, c, vectors)[:, :width], NT
            )
        return total

    old_c, old_p = rows[:vec3], rows[vec3 : 2 * vec3]
    extended = rows.shape[1]
    cw, pw = gram(old_c, result, extended), gram(old_p, result, extended)
    cc, cp, pp = gram(old_c, old_c, atoms), gram(old_c, old_p, atoms), gram(old_p, old_p, atoms)
    sums[...] = jnp.concatenate([with_diagonal(cw, pp), pw, cp, join_triangles(cc, pp)], axis=1)


def second_kernel(
    order, own, mate, other, far, cext, pext, index, dm, ef, ee, e8, pmat, rmat,
    out_m, out_o, out_x, shared, rown,
    mv, eo, xs, sx, cs, patch, ring,
    *, vectors, atoms, total_rows,
):
    half3 = 3 * vectors // 2
    vec3 = 2 * half3
    tail = 3 * half3
    pick = pick_matrix(index[0:1, :], 9 * atoms)
    for i, part in enumerate((own, mate, other)):
        ring[order[i]] = part[tail:, :]
    ring[order[3]] = far[...]
    total = ((ring[0] + ring[1]) + (ring[2] + ring[3])) * (1.0 / total_rows)
    v = vectors
    held, pw, cp, joined = (total[:, i * v : (i + 1) * v] for i in range(4))
    coef = jnp.concatenate([from_lower(held), pw], axis=0)
    cc, pp = from_lower(joined), from_upper(joined, held)
    gram_old = jnp.concatenate(
        [jnp.concatenate([cc, cp], axis=1), jnp.concatenate([cp.T, pp], axis=1)], axis=0
    )
    shared[...] = jnp.concatenate([gram_old, coef, jnp.zeros_like(coef)], axis=1)

    for x, ref in enumerate((mate, own, other)):
        for y in range(3):
            at = (3 * y + x) * atoms
            patch[:, at : at + atoms] = unpack(ref[y * half3 : (y + 1) * half3, :], atoms)
    both = dot16(split(patch[...], 2), pick)
    work = both[:vec3] + both[vec3:]
    turned = coef.T
    resid = work - jnp.concatenate(
        [
            dot_split(
                turned,
                jnp.concatenate(
                    [component(cext[...], c, vectors), component(pext[...], c, vectors)], axis=0
                ),
            )
            for c in range(3)
        ],
        axis=0,
    )
    rown[...] = pack(resid[:, :atoms])
    rows = apply_operator(split(resid, 2), dm, ef, ee, e8, pmat, rmat, mv, eo, xs, sx, cs, atoms)
    store_patch((out_m, out_o, out_x), rows, pick, atoms)


def gram_kernel(rown, y0, ym, yo, out, yown, *, vectors, atoms):
    work = y0[...] + ym[...] + yo[...]
    yown[...] = work
    r, y = unpack(rown[...], atoms), unpack(work, atoms)
    gram = jnp.zeros((2 * vectors, 2 * vectors), jnp.float32)
    for c in range(3):
        stacked = jnp.concatenate([component(r, c, vectors), component(y, c, vectors)], axis=0)
        gram = gram + dot_split(stacked, stacked, NT)
    v = vectors
    rr, ry, yy = gram[:v, :v], gram[:v, v:], gram[v:, v:]
    lanes = out.shape[2]
    sent = jnp.concatenate(
        [flatten(join_triangles(rr, yy), lanes), flatten(with_diagonal(ry, yy), lanes)], axis=0
    )
    out[...] = jnp.broadcast_to(sent[None], out.shape)


def cholesky(matrix, *extra):
    size = matrix.shape[0]
    rows, cols = rows_and_cols(size)
    unit = (rows == cols).astype(jnp.float32)
    work = jnp.concatenate([matrix, unit, *extra], axis=1)
    columns = [jnp.broadcast_to(matrix[:, k : k + 1], work.shape) for k in range(size)]
    lines = []
    for j in range(0, size, 2):
        first, second = columns[j], columns[j + 1]
        a, b, d = first[j : j + 1], first[j + 1 : j + 2], second[j + 1 : j + 2]
        det = a * d - b * b
        inverse = 1.0 / det
        ai, bi, di = a * inverse, b * inverse, d * inverse
        keep = (j + 2) // 8 * 8
        for k in range(j + 2, size):
            low = columns[k]
            x0, x1 = low[j : j + 1], low[j + 1 : j + 2]
            low = low[keep:] - (first[keep:] * (di * x0 - bi * x1) + second[keep:] * (ai * x1 - bi * x0))
            columns[k] = jnp.concatenate([columns[k][:keep], low], axis=0) if keep else low
        r0, r1 = work[j : j + 1], work[j + 1 : j + 2]
        work = work - (first * (di * r0 - bi * r1) + second * (ai * r1 - bi * r0))
        lines += [r0 * root_inverse(a), (r1 - (b / a) * r0) * root_inverse(det / a)]
    done = jnp.concatenate(lines, axis=0)
    upper = jnp.where(cols >= rows, done[:, :size], 0.0)
    return [upper] + [done[:, i * size : (i + 1) * size] for i in range(1, 2 + len(extra))]


def root_inverse(value):
    guess = lax.rsqrt(value)
    return guess * (1.5 - 0.5 * value * guess * guess)


def final_kernel(got, sums, rown, yown, cown, blocks, factors, *, vectors, atoms, total_rows):
    devices = got.shape[0]
    v = vectors
    total = got[0]
    for i in range(1, devices):
        total = total + got[i]
    total = total * (1.0 / total_rows)
    count = total.shape[0] // 2
    joined, held = unflatten(total[:count], v), unflatten(total[count:], v)
    rr, ry, yy = from_lower(joined), from_lower(held), from_upper(joined, held)
    shared = sums[...]
    gram_old, coef1 = shared[:, : 2 * v], shared[:, 2 * v : 3 * v]
    rows, cols = rows_and_cols(v)
    unit = (rows == cols).astype(jnp.float32)
    left = coef1 - dot32(gram_old, coef1)
    wr = rr + dot32(coef1, left, TN)
    fixed = yy + dot32(wr, dot32(gram_old[:v, :v] - 2.0 * unit, wr), TN)

    upper1, inv1, along, cross = cholesky(rr, ry, left[:v].T)
    mixed = dot32(cross, wr)
    gram2 = fixed + dot32(
        jnp.concatenate([along, mixed], axis=0), jnp.concatenate([mixed - along, along], axis=0), TN
    )
    upper2, inv2 = cholesky(gram2)
    factors[0] = upper1.T
    factors[1] = jnp.where(rows >= cols, dot32(inv1, upper2, NT), 0.0)
    r, y, old = unpack(rown[...], atoms), unpack(yown[...], atoms), cown[0 : 3 * vectors, :]
    back = dot32(along, inv1, TN)
    weights = jnp.concatenate([-back, -wr.T], axis=1)
    for c in range(3):
        parts = [component(part, c, vectors) for part in (r, old)]
        blocks[0, c] = dot32(inv1, parts[0])
        rest = component(y, c, vectors) + dot32(weights, jnp.concatenate(parts, axis=0))
        blocks[1, c] = dot32(inv2, rest)


def mates(count):
    mate = [i ^ 1 for i in range(count)]
    other = [(i - 1) % count if i % 2 == 0 else (i + 1) % count for i in range(count)]
    return mate, other


def fetch(values, axis, sources):
    return lax.ppermute(values, axis, [(s, i) for i, s in enumerate(sources)])


def vmem_call(kernel, outs, scratch=(), scalars=0, flops=1 << 20):
    def call(*operands):
        spaces = [pltpu.SMEM] * scalars + [pltpu.VMEM] * (len(operands) - scalars)
        return pl.pallas_call(
            kernel,
            out_shape=outs,
            in_specs=[pl.BlockSpec(memory_space=s) for s in spaces],
            out_specs=jax.tree.map(lambda _: pl.BlockSpec(memory_space=pltpu.VMEM), outs),
            scratch_shapes=list(scratch),
            compiler_params=pltpu.CompilerParams(vmem_limit_bytes=VMEM_BYTES),
            cost_estimate=pl.CostEstimate(flops=flops, bytes_accessed=1 << 16, transcendentals=0),
        )(*operands)

    return call


def laid(shape, pieces):
    total = None
    for row, piece in pieces:
        rows, lanes = piece.shape
        edges = ((row, shape[0] - row - rows), (0, shape[1] - lanes))
        placed = jnp.pad(piece, edges).astype(jnp.float32)
        total = placed if total is None else total + placed
    return total


def f32(*shape):
    return jax.ShapeDtypeStruct(shape, jnp.float32)


def shards(positions, block_prev, block_cur, neighbours, counts, x_lists, y_lists, w_radial, w_vector, w_mix, w_out):
    vectors, _, atoms = block_cur.shape
    halo = x_lists.shape[2]
    slots = neighbours.shape[0]
    basis, channels = w_radial.shape
    n_x, n_y = lax.axis_size("gx"), lax.axis_size("gy")
    total_rows = 3.0 * atoms * n_x * n_y
    half3 = 3 * vectors // 2
    vec3 = 3 * vectors
    lanes = 2 * atoms
    edges = slots * atoms
    extended = atoms + 4 * halo
    pairs = 2 * basis
    mate_x, other_x = mates(n_x)
    mate_y, other_y = mates(n_y)
    at_x, at_y = lax.axis_index("gx"), lax.axis_index("gy")
    sides = jnp.stack([at_x % 2, at_y % 2]).astype(jnp.int32)
    own_rows = 2 * half3 + 8

    cur = block_cur.transpose(1, 0, 2).reshape(vec3, atoms)
    prev = block_prev.transpose(1, 0, 2).reshape(vec3, atoms)
    slab = f32(own_rows, lanes)
    all_rows = 2 * vec3 + 8

    counting = lax.broadcasted_iota(jnp.float32, (1, atoms), 1)
    table = laid(
        (all_rows + 8, atoms),
        [
            (0, cur),
            (vec3, prev),
            (2 * vec3, positions),
            (2 * vec3 + 3, counting),
            (all_rows, x_lists[0]),
            (all_rows + 2, y_lists[0]),
        ],
    )
    to_mate, to_other = vmem_call(select_x_kernel, [slab, slab], scalars=1)(sides, table)
    mate1 = fetch(to_mate, "gx", mate_x)
    other1 = fetch(to_other, "gx", other_x)
    after = channels + 2 * basis + 8
    fixed = laid(
        (after + slots + 8, channels),
        [
            (0, w_mix),
            (channels, w_radial),
            (channels + basis, w_vector),
            (channels + 2 * basis, w_out[None]),
            (after, neighbours),
            (after + slots, counts[None]),
        ],
    )
    rad_shape, mix_shape, turned_shape = f32(basis, channels), f32(channels, channels), f32(channels, basis)
    dm, valid, rad, vec, mix, rad_t, vec_t, mix_t, out_t = vmem_call(
        functools.partial(prepare_kernel, slots=slots, atoms=atoms),
        [
            jax.ShapeDtypeStruct((extended, edges), jnp.bfloat16),
            f32(8, edges),
            rad_shape,
            rad_shape,
            mix_shape,
            turned_shape,
            turned_shape,
            mix_shape,
            f32(channels, 8),
        ],
        flops=1 << 24,
    )(fixed)
    to_mate, to_other, wide = vmem_call(
        select_y_kernel, [slab, slab, f32(all_rows, atoms + 2 * halo)], scalars=1
    )(sides, table, mate1, other1)
    mate2 = fetch(to_mate, "gy", mate_y)
    other2 = fetch(to_other, "gy", other_y)

    work_scratch = [
        pltpu.VMEM((vec3, edges), jnp.float32),
        pltpu.VMEM((vec3, edges), jnp.float32),
        pltpu.VMEM((pairs, vectors, lanes), jnp.float32),
        pltpu.VMEM((pairs, vectors, lanes), jnp.float32),
        pltpu.VMEM((2 * pairs, vectors, lanes), jnp.float32),
    ]
    first = vmem_call(
        functools.partial(first_kernel, vectors=vectors, atoms=atoms, halo=halo),
        [
            f32(3 * half3, lanes),
            f32(3 * half3, lanes),
            f32(3 * half3, lanes),
            f32(vectors, lanes),
            f32(vec3, extended),
            f32(vec3, extended),
            jax.ShapeDtypeStruct((8, extended), jnp.int32),
            f32(basis, edges),
            f32(basis, edges),
            f32(8, edges),
            f32(pairs * pairs, lanes),
            f32(pairs * pairs, lanes),
        ],
        work_scratch
        + [
            pltpu.VMEM((basis, edges), jnp.float32),
            pltpu.VMEM((32, edges), jnp.float32),
            pltpu.VMEM((channels, pairs * lanes), jnp.float32),
            pltpu.VMEM((channels, pairs * lanes), jnp.float32),
            pltpu.VMEM((channels, lanes), jnp.float32),
            pltpu.VMEM((basis, basis, lanes), jnp.float32),
        ],
        scalars=1,
        flops=1 << 31,
    )
    part_m, part_0, part_o, local, cext, pext, index, ef, ee, e8, pmat, rmat = first(
        sides, wide, mate2, other2, dm, valid, rad, vec, mix, rad_t, vec_t, mix_t, out_t
    )

    back_m = fetch(part_m, "gx", mate_x)
    back_o = fetch(part_o, "gx", other_x)
    strided = [local] + [
        fetch(local, "gx", [(i + d) % n_x for i in range(n_x)]) for d in range(4, n_x, 4)
    ]
    if len(strided) == 2:
        local = strided[0] + strided[1]
    else:
        local = jnp.sum(jnp.roll(jnp.stack(strided), at_x // 4, axis=0), axis=0)
    folded = part_0 + back_m + back_o
    f_m, f_0, f_o = folded[:half3], folded[half3 : 2 * half3], folded[2 * half3 :]

    far_m = [other_y[m] for m in mate_y]
    far_o = [mate_y[o] for o in other_y]
    got_m = fetch(jnp.concatenate([f_0, f_m, local]), "gy", mate_y)
    got_o = fetch(jnp.concatenate([f_0, f_o, local]), "gy", other_y)
    if far_m == far_o:
        got_2 = fetch(jnp.concatenate([f_m, f_o, local]), "gy", far_m)
        far_mate, far_other = got_2[half3 : 2 * half3], got_2[:half3]
        sums = (local + got_m[2 * half3 :]) + (got_o[2 * half3 :] + got_2[2 * half3 :])
    else:
        far_mate = fetch(f_o, "gy", far_m)
        far_other = fetch(f_m, "gy", far_o)
        terms = [local] + [
            fetch(local, "gy", [(i + d) % n_y for i in range(n_y)]) for d in range(1, n_y)
        ]
        sums = jnp.sum(jnp.roll(jnp.stack(terms), at_y, axis=0), axis=0)
    w_m = got_m[:half3] + f_m + far_mate
    w_0 = f_0 + got_m[half3 : 2 * half3] + got_o[half3 : 2 * half3]
    w_o = got_o[:half3] + far_other + f_o
    column = jnp.concatenate([w_m, w_0, w_o, sums])

    col_m = fetch(column, "gx", mate_x)
    col_o = fetch(column, "gx", other_x)
    far = fetch(sums, "gx", [(i + 2) % n_x for i in range(n_x)])
    order = jnp.stack(
        [at_x % 4, (at_x ^ 1) % 4, (at_x - 1 + 2 * (at_x % 2)) % 4, (at_x + 2) % 4]
    ).astype(jnp.int32)

    second = vmem_call(
        functools.partial(second_kernel, vectors=vectors, atoms=atoms, total_rows=total_rows),
        [
            f32(3 * half3, lanes),
            f32(3 * half3, lanes),
            f32(3 * half3, lanes),
            f32(2 * vectors, lanes),
            f32(half3, lanes),
        ],
        work_scratch
        + [pltpu.VMEM((vec3, 9 * atoms), jnp.float32), pltpu.VMEM((4, vectors, lanes), jnp.float32)],
        scalars=1,
        flops=1 << 30,
    )
    part_m, part_0, part_o, shared, rown = second(
        order, column, col_m, col_o, far, cext, pext, index, dm, ef, ee, e8, pmat, rmat
    )
    back_m = fetch(part_m, "gx", mate_x)
    back_o = fetch(part_o, "gx", other_x)
    folded = part_0 + back_m + back_o
    y_m = fetch(folded[:half3], "gy", mate_y)
    y_o = fetch(folded[2 * half3 :], "gy", other_y)

    sent_rows = 2 * vectors * vectors // lanes
    spread, yown = vmem_call(
        functools.partial(gram_kernel, vectors=vectors, atoms=atoms),
        [f32(n_x * n_y, sent_rows, lanes), f32(half3, lanes)],
    )(rown, folded[half3 : 2 * half3], y_m, y_o)
    got = lax.all_to_all(spread, ("gx", "gy"), 0, 0)
    blocks, factors = vmem_call(
        functools.partial(final_kernel, vectors=vectors, atoms=atoms, total_rows=total_rows),
        [f32(2, 3, vectors, atoms), f32(2, vectors, vectors)],
    )(got, shared, rown, yown, table)
    return blocks.transpose(0, 2, 1, 3), factors


def solution(mesh):
    placed = (
        P(None, ("gx", "gy")),
        P(None, None, ("gx", "gy")),
        P(None, None, ("gx", "gy")),
        P(None, ("gx", "gy")),
        P(("gx", "gy")),
        P(("gx", "gy"), None, None),
        P(("gx", "gy"), None, None),
        P(),
        P(),
        P(),
        P(),
    )
    return jax.shard_map(
        shards,
        mesh=mesh,
        in_specs=placed,
        out_specs=(P(None, None, None, ("gx", "gy")), P()),
        check_vma=False,
    )
```

```python
import functools

import jax
import jax.numpy as jnp
from jax import lax
from jax.experimental import pallas as pl
from jax.experimental.pallas import tpu as pltpu
from jax.sharding import PartitionSpec as P

SOFTEN = 0.25
CUTOFF = 5.0
GAUSS_WIDTH = 2.0
EXACT = lax.Precision.HIGHEST
VMEM_BYTES = 48 * 1024 * 1024
NN = (((1,), (0,)), ((), ()))
NT = (((1,), (1,)), ((), ()))
TN = (((0,), (0,)), ((), ()))


def dot16(left, right, dims=NN):
    return lax.dot_general(left, right, dims, preferred_element_type=jnp.float32)


def dot32(left, right, dims=NN):
    return lax.dot_general(
        left, right, dims, precision=EXACT, preferred_element_type=jnp.float32
    )


def split(values, parts):
    pieces = []
    for _ in range(parts):
        piece = values.astype(jnp.bfloat16)
        pieces.append(piece)
        values = values - piece.astype(jnp.float32)
    return jnp.concatenate(pieces, axis=0)


def dot_split(left, right, dims=NN):
    if dims == TN:
        left = left.T
        dims = NN
    rows = left.shape[0]
    both = split(left, 2)
    high = right.astype(jnp.bfloat16)
    low = (right - high.astype(jnp.float32)).astype(jnp.bfloat16)
    first = dot16(both, high, dims)
    return first[:rows] + first[rows:] + dot16(both[:rows], low, dims)


def component(block, comp, vectors):
    return block[comp * vectors : (comp + 1) * vectors]


def unpack(packed, atoms):
    return jnp.concatenate([packed[:, :atoms], packed[:, atoms:]], axis=0)


def pack(rows):
    half = rows.shape[0] // 2
    return jnp.concatenate([rows[:half], rows[half:]], axis=1)


def pick_matrix(index_row, patch_rows):
    extended = index_row.shape[1]
    rows = lax.broadcasted_iota(jnp.int32, (patch_rows, extended), 0)
    return (rows == index_row).astype(jnp.float32).astype(jnp.bfloat16)


def select(rows, *names):
    picks = jnp.concatenate(names, axis=1)
    hits = lax.broadcasted_iota(jnp.int32, (rows.shape[1], picks.shape[1]), 0) == picks
    got = dot16(split(rows, 3), hits.astype(jnp.float32).astype(jnp.bfloat16))
    count = rows.shape[0]
    return got[:count] + (got[count : 2 * count] + got[2 * count :])


def rows_and_cols(size):
    return (
        lax.broadcasted_iota(jnp.int32, (size, size), 0),
        lax.broadcasted_iota(jnp.int32, (size, size), 1),
    )


def join_triangles(lower, upper):
    rows, cols = rows_and_cols(lower.shape[0])
    return jnp.where(rows >= cols, lower, upper)


def with_diagonal(lower, source):
    size = lower.shape[0]
    rows, cols = rows_and_cols(size)
    line = jnp.sum(jnp.where(rows == cols, source, 0.0), axis=0, keepdims=True)
    upper = jnp.where(rows == 0, line, jnp.where((rows == 1) & (cols == size - 1), source[0:1, 0:1], 0.0))
    return jnp.where(rows >= cols, lower, upper)


def from_lower(joined):
    rows, cols = rows_and_cols(joined.shape[0])
    strict = jnp.where(rows > cols, joined, 0.0)
    return jnp.where(rows >= cols, joined, 0.0) + strict.T


def from_upper(joined, holder):
    size = joined.shape[0]
    rows, cols = rows_and_cols(size)
    strict = jnp.where(rows < cols, joined, 0.0)
    line = jnp.where(cols[0:1] >= 1, holder[0:1], holder[1:2, size - 1 : size])
    return strict + strict.T + jnp.where(rows == cols, line, 0.0)


def flatten(square, lanes):
    size = square.shape[0]
    rows = size * size // lanes
    return jnp.concatenate([square[i * rows : (i + 1) * rows] for i in range(lanes // size)], axis=1)


def unflatten(flat, size):
    return jnp.concatenate(
        [flat[:, i * size : (i + 1) * size] for i in range(flat.shape[1] // size)], axis=0
    )


def rows_of(tile, comp, vectors):
    return slice(comp * vectors + tile * 8, comp * vectors + tile * 8 + 8)


def contract(mv_ref, ef_ref, ee_ref, head_of, xs_ref, sx_ref, atoms):
    lanes = 2 * atoms
    basis, edges = ef_ref.shape
    vectors = mv_ref.shape[0] // 3
    pairs = 2 * basis
    lower = lax.broadcasted_iota(jnp.int32, (8, lanes), 1) < atoms
    for tile in range(vectors // 8):
        acc = [jnp.zeros((8, lanes), jnp.float32)] * (4 * basis)
        for j in range(edges // lanes):
            at = slice(j * lanes, (j + 1) * lanes)
            m = [mv_ref[rows_of(tile, c, vectors), at] for c in range(3)]
            head = [head_of(c, at) for c in range(3)]
            u = head[0] * m[0] + head[1] * m[1] + head[2] * m[2]
            along = [head[c] * u for c in range(3)]
            across = [m[c] - along[c] for c in range(3)]
            for k in range(basis):
                slope = ef_ref[k : k + 1, at]
                even = ee_ref[k : k + 1, at]
                acc[k] = acc[k] + slope * u
                for c in range(3):
                    i = (c + 1) * basis + k
                    acc[i] = acc[i] + (slope * along[c] + even * across[c])
        for i in range(pairs):
            a, b = acc[i], acc[i + pairs]
            x = jnp.where(lower, a, b) + pltpu.roll(jnp.where(lower, b, a), atoms, 1)
            xs_ref[i, tile * 8 : tile * 8 + 8, :] = x
            sx_ref[i, tile * 8 : tile * 8 + 8, :] = pltpu.roll(x, atoms, 1)


def spread(dm_ref, ef_ref, ee_ref, e8_ref, p_ref, r_ref, mv_ref, eo_ref, xs_ref, sx_ref, cs_ref, atoms):
    lanes = 2 * atoms
    basis, edges = ef_ref.shape
    groups = edges // lanes
    vec3 = mv_ref.shape[0]
    vectors = vec3 // 3
    pairs = 2 * basis
    tiles = vectors // 8
    wide_lower = lax.broadcasted_iota(jnp.int32, (8 * tiles, lanes), 1) < atoms

    def mix_step(kappa, carry):
        at = pl.ds(pl.multiple_of(kappa * pairs, pairs), pairs)
        straight = p_ref[at, :]
        crossed = r_ref[at, :]
        y = jnp.zeros((8 * tiles, lanes), jnp.float32)
        for i in range(pairs):
            y = y + straight[i : i + 1, :] * xs_ref[i] + crossed[i : i + 1, :] * sx_ref[i]
        turned = pltpu.roll(y, atoms, 1)
        cs_ref[kappa] = jnp.where(wide_lower, y, turned)
        cs_ref[kappa + pairs] = jnp.where(wide_lower, turned, y)
        return carry

    lax.fori_loop(0, pairs, mix_step, 0, unroll=4)

    for tile in range(tiles):
        coeff = [cs_ref[i, tile * 8 : tile * 8 + 8, :] for i in range(4 * basis)]

        def spread_step(j, carry, tile=tile, coeff=coeff):
            at = pl.ds(pl.multiple_of(j * lanes, lanes), lanes)
            m = [mv_ref[rows_of(tile, c, vectors), at] for c in range(3)]
            row = [e8_ref[i : i + 1, at] for i in range(8)]
            head, turn = row[0:3], row[5:8]
            u = head[0] * m[0] + head[1] * m[1] + head[2] * m[2]
            radial = row[4] * u + (turn[0] * m[0] + turn[1] * m[1] + turn[2] * m[2])
            sums, evens = [None] * 3, [None] * 3
            for k in range(basis):
                slope = ef_ref[k : k + 1, at]
                even = ee_ref[k : k + 1, at]
                radial = radial + slope * coeff[k]
                for c in range(3):
                    i = (c + 1) * basis + k
                    more, plus = slope * coeff[i], even * coeff[i]
                    sums[c] = more if k == 0 else sums[c] + more
                    evens[c] = plus if k == 0 else evens[c] + plus
            for c in range(3):
                radial = radial + head[c] * (sums[c] - evens[c])
            for c in range(3):
                out = evens[c] + head[c] * radial + (row[3] * m[c] + turn[c] * u)
                eo_ref[rows_of(tile, c, vectors), at] = out
            return carry

        lax.fori_loop(0, groups, spread_step, 0, unroll=groups)

    both = dot16(split(eo_ref[...], 2), dm_ref[...], NT)
    return both[:vec3] + both[vec3:]


def stacked_sums(parts):
    row = lax.broadcasted_iota(jnp.int32, parts[0].shape, 0)

    def moved(values, by):
        return values + pltpu.roll(values, by % 8, 0)

    upper = row < 4
    fours = [
        jnp.where(upper, parts[i], parts[i + 4]) + pltpu.roll(jnp.where(upper, parts[i + 4], parts[i]), 4, 0)
        for i in range(4)
    ]
    twos = [jnp.where(row % 4 < 2, moved(fours[i], -2), moved(fours[i + 2], 2)) for i in range(2)]
    return jnp.where(row % 2 < 1, moved(twos[0], -1), moved(twos[1], 1))


def store_patch(outs, extended_rows, pick, atoms):
    vec3 = extended_rows.shape[0]
    half3 = vec3 // 2
    both = dot16(split(extended_rows, 2), pick, NT)
    patch = both[:vec3] + both[vec3:]
    for x in range(3):
        for y in range(3):
            at = (3 * y + x) * atoms
            tile = patch[:, at : at + atoms]
            outs[x][y * half3 : (y + 1) * half3, 0:atoms] = tile[:half3]
            outs[x][y * half3 : (y + 1) * half3, atoms : 2 * atoms] = tile[half3:]


def emit(even, rows, lists, to_mate, to_other):
    low, high = lists
    got = select(rows, jnp.where(even, low, high), jnp.where(even, high, low))
    halo = low.shape[1]
    vec3 = (rows.shape[0] - 8) // 2
    for which, out in enumerate((to_mate, to_other)):
        part = got[:, which * halo : (which + 1) * halo]
        out[0:vec3, :] = jnp.concatenate([part[0:vec3], part[vec3 : 2 * vec3]], axis=1)
        out[vec3:, :] = jnp.concatenate([part[2 * vec3 :], jnp.zeros_like(part[2 * vec3 :])], axis=1)


def unpack_rows(block, width):
    vec3 = block.shape[0] - 8
    return jnp.concatenate([block[:vec3, 0:width], block[:vec3, width : 2 * width], block[vec3:, 0:width]], axis=0)


def table_rows(table, atoms):
    rows = unpack_rows(table, atoms)
    count = rows.shape[0]
    number = lax.broadcasted_iota(jnp.int32, (8, atoms), 1).astype(jnp.float32)
    line = lax.broadcasted_iota(jnp.int32, (8, atoms), 0)
    last = jnp.where(line < 3, rows[count - 8 :], jnp.where(line == 3, number, 0.0))
    return jnp.concatenate([rows[: count - 8], last], axis=0)


def table_lists(table, line, halo):
    base = table.shape[0] - 8 + line
    rows = table[base : base + 2, 0:halo].astype(jnp.int32)
    return rows[0:1], rows[1:2]


def beside(rows, mate, other, even, step):
    line = rows.shape[0] - 5
    at = (lax.broadcasted_iota(jnp.int32, (rows.shape[0], 1), 0) == line).astype(jnp.float32) * step
    other = other + 2.0 * at
    return jnp.concatenate(
        [rows + at, jnp.where(even, other, mate), jnp.where(even, mate, other)], axis=1
    )


def select_kernel(sides, table, from_mate, from_other, to_mate, to_other, wide, *, atoms, halo):
    even = sides[0] == 0
    picked = []
    for ref, flip in ((from_mate[...], False), (from_other[...], True)):
        low, high = table_lists(ref, 3, halo)
        names = jnp.where(even, low, high) if flip else jnp.where(even, high, low)
        picked.append(select(table_rows(ref, atoms), names))
    got = beside(table_rows(table[...], atoms), *picked, even, float(atoms))
    wide[...] = got
    emit(sides[1] == 0, got, table_lists(table[...], 5, halo), to_mate, to_other)


def prepare_kernel(table, dm, valid, rad, vec, mix, rad_t, vec_t, mix_t, out_t, *, slots, atoms):
    lanes = 2 * atoms
    basis, channels = rad.shape
    starts = [0, channels, channels + basis, channels + 2 * basis, channels + 2 * basis + 8]
    w_mix, w_rad, w_vec = (table[starts[i] : starts[i + 1], :] for i in range(3))
    w_out = table[starts[3] : starts[4], :]
    ints = table[starts[4] :, 0:atoms].astype(jnp.int32)
    nb, count = ints[:slots], ints[slots : slots + 1]
    difference_matrix(dm, nb, dm.shape[0], atoms)
    lane = lax.broadcasted_iota(jnp.int32, (8, lanes), 1)
    first = jnp.where(lane < atoms, 0, slots // 2)
    limit = jnp.concatenate([count, count], axis=1)
    for j in range(slots // 2):
        valid[:, j * lanes : (j + 1) * lanes] = (first + j < limit).astype(jnp.float32)
    rad[...] = w_rad
    vec[...] = w_vec
    mix[...] = w_mix
    rad_t[...] = w_rad.T
    vec_t[...] = w_vec.T
    mix_t[...] = w_mix.T
    out_t[...] = w_out.T


def difference_matrix(dm_ref, nb, extended, atoms):
    half = nb.shape[0] // 2
    lanes = 2 * atoms
    paired = jnp.concatenate([nb[:half], nb[half:]], axis=1)
    rows = lax.broadcasted_iota(jnp.int32, (extended, lanes), 0)
    lane = lax.broadcasted_iota(jnp.int32, (extended, lanes), 1)
    own = (rows == jnp.where(lane < atoms, lane, lane - atoms)).astype(jnp.float32)
    for j in range(half):
        hit = (rows == paired[j : j + 1, :]).astype(jnp.float32)
        dm_ref[:, j * lanes : (j + 1) * lanes] = (hit - own).astype(jnp.bfloat16)


def gather_edges(parts16, dm, valid, mv, ef, ee, f2s, hs, vec3, lanes):
    basis, edges = ef.shape
    wide = 2 * lanes
    cut = 1.0 / (CUTOFF * CUTOFF)
    centre = (lax.broadcasted_iota(jnp.int32, (basis, wide), 0).astype(jnp.float32) + 0.5) * (CUTOFF / basis)
    totals = [jnp.zeros((basis, lanes), jnp.float32) for _ in range(4)]
    for j in range(edges // wide):
        at = slice(j * wide, (j + 1) * wide)
        got = dot16(parts16, dm[:, at])
        mv[:, at] = got[:vec3] + got[vec3 : 2 * vec3]
        third = 2 * vec3
        delta = got[third : third + 24] + got[third + 32 : third + 56] + got[third + 64 : third + 88]
        d = [delta[8 * c : 8 * c + 8] for c in range(3)]
        squared = d[0] * d[0] + d[1] * d[1] + d[2] * d[2] + SOFTEN
        radius = jnp.sqrt(squared)
        inverse = 1.0 / radius
        head = [d[c] * inverse for c in range(3)]
        tau = jnp.maximum(1.0 - squared * cut, 0.0)
        env = tau * tau * tau
        env1 = (-6.0 * cut) * radius * tau * tau
        env2 = (24.0 * cut * cut) * squared * tau - (6.0 * cut) * tau * tau
        off = radius - centre
        gauss = jnp.exp(-GAUSS_WIDTH * off * off) * valid[:, at]
        gauss1 = (-2.0 * GAUSS_WIDTH) * off * gauss
        gauss2 = (4.0 * GAUSS_WIDTH * GAUSS_WIDTH * off * off - 2.0 * GAUSS_WIDTH) * gauss
        value = gauss * env
        ef[:, at] = gauss1 * env + gauss * env1
        ee[:, at] = value * inverse
        f2s[:, at] = gauss2 * env + 2.0 * gauss1 * env1 + gauss * env2
        for c in range(3):
            hs[8 * c : 8 * c + 8, at] = head[c]
        hs[24:32, at] = inverse
        terms = [value, value * head[0], value * head[1], value * head[2]]
        totals = [t + v[:, :lanes] + v[:, lanes:] for t, v in zip(totals, terms)]
    return [t + pltpu.roll(t, lanes // 2, 1) for t in totals]


def edge_rows(alpha, beta, ef, ee, f2s, hs, e8, lanes):
    for j in range(ef.shape[1] // lanes):
        at = slice(j * lanes, (j + 1) * lanes)
        head = [hs[8 * c : 8 * c + 8, at] for c in range(3)]
        inverse = hs[24:32, at]
        slope_k, even_k, second = ef[:, at], ee[:, at], f2s[:, at]
        even1 = (slope_k - even_k) * inverse
        even2 = (second - 2.0 * even1) * inverse

        sums = stacked_sums(
            [alpha * slope_k, alpha * second]
            + [beta[c] * even1 for c in range(3)]
            + [beta[c] * even2 for c in range(3)]
        )
        first, bend_r = sums[0:1], sums[1:2]
        turn = [sums[2 + c : 3 + c] for c in range(3)]
        twist = [sums[5 + c : 6 + c] for c in range(3)]
        inv1 = inverse[0:1]
        h1 = [head[c][0:1] for c in range(3)]
        radius = 1.0 / inv1
        line = h1[0] * turn[0] + h1[1] * turn[1] + h1[2] * turn[2]
        isotropic = first * inv1 + line
        radial = bend_r + (h1[0] * twist[0] + h1[1] * twist[1] + h1[2] * twist[2]) * radius - isotropic
        e8[:, at] = jnp.concatenate(h1 + [isotropic, radial] + turn, axis=0)


def channel_lift(flow, rad_t, vec_t, mix_t, qs, qr, lanes, atoms):
    channels, basis = rad_t.shape
    lower = lax.broadcasted_iota(jnp.int32, (channels, lanes), 1) < atoms
    lift0 = 2.0 * jnp.where(lower, flow[0], flow[2])
    lift1 = 2.0 * flow[1]
    for i in range(2 * basis):
        k = i % basis
        if i < basis:
            side = jnp.where(lower, jnp.broadcast_to(rad_t[:, k : k + 1], lower.shape), lift1 * vec_t[:, k : k + 1])
        else:
            side = lift0 * vec_t[:, k : k + 1]
        lifted = dot_split(mix_t, side)
        qs[:, i * lanes : (i + 1) * lanes] = lifted
        qr[:, i * lanes : (i + 1) * lanes] = pltpu.roll(lifted, atoms, 1)


def descriptor_curvature(vec, u, bend, qs, qr, bd, both, pmat, rmat, lanes, atoms):
    basis = vec.shape[0]
    pairs = 2 * basis
    channels = bend.shape[0]
    bd[...] = bend
    low_row = lax.broadcasted_iota(jnp.int32, (basis, lanes), 1) < atoms
    for k in range(basis):
        both[k] = 2.0 * dot32(vec * vec[k : k + 1, :], u)

    def block(i, column):
        accs = None
        for tile in range(channels // 8):
            rows = slice(8 * tile, 8 * tile + 8)
            weight = bd[rows, :]
            left = [
                qs[rows, pl.ds(pl.multiple_of((i + d) * lanes, lanes), lanes)] * weight for d in range(2)
            ]
            columns = [slice((column + k) * lanes, (column + k + 1) * lanes) for k in range(basis)]
            right = [ref[rows, at] for ref in (qs, qr) for at in columns]
            terms = [l * r for l in left for r in right]
            accs = terms if accs is None else [a + t for a, t in zip(accs, terms)]
        return [stacked_sums(accs[q * basis : (q + 1) * basis]) for q in range(4)]

    def put(i, column, tiles):
        for d in range(2):
            at = pl.ds(pl.multiple_of((i + d) * pairs + column, basis), basis)
            pmat[at, :] = tiles[2 * d]
            rmat[at, :] = tiles[2 * d + 1]

    def upper_step(step, carry):
        i = 2 * step
        tiles = block(i, 0)
        for d in range(2):
            tiles[2 * d] = tiles[2 * d] + jnp.where(low_row, 0.0, both[i + d])
        put(i, 0, tiles)
        return carry

    def lower_step(step, carry):
        i = 2 * step + basis
        tiles = block(i, 0)
        put(i, 0, tiles)
        for d in range(2):
            pmat[pl.ds(i + d, basis, pairs), :] = tiles[2 * d]
            rmat[pl.ds(i + d, basis, pairs), :] = pltpu.roll(tiles[2 * d + 1], atoms, 1)
        tiles = block(i, basis)
        for d in range(2):
            tiles[2 * d] = tiles[2 * d] + both[i + d - basis]
        put(i, basis, tiles)
        return carry

    lax.fori_loop(0, basis // 2, upper_step, 0)
    lax.fori_loop(0, basis // 2, lower_step, 0)


def first_kernel(
    sides, wide, from_mate, from_other, dm, valid, w_rad, w_vec, w_mix, rad_t, vec_t, mix_t, out_t,
    out_m, out_o, out_x, partial, cext, pext, index, ef, ee, e8, pmat, rmat,
    mv, eo, xs, sx, cs, f2s, hs, qs, qr, bd, both,
    *, vectors, atoms, halo,
):
    half3 = 3 * vectors // 2
    vec3 = 2 * half3
    lanes = 2 * atoms
    rows = beside(
        wide[...],
        unpack_rows(from_mate[...], halo),
        unpack_rows(from_other[...], halo),
        sides[1] == 0,
        3.0 * atoms,
    )
    cext[...] = rows[:vec3]
    pext[...] = rows[vec3 : 2 * vec3]
    base = 2 * vec3
    places = jnp.round(rows[base + 3 : base + 4]).astype(jnp.int32)
    index[...] = jnp.broadcast_to(places, index.shape)
    shape = (8, rows.shape[1])
    place = jnp.concatenate(
        [jnp.broadcast_to(rows[base + c : base + c + 1], shape) for c in range(3)] + [jnp.zeros(shape, jnp.float32)],
        axis=0,
    )
    parts16 = jnp.concatenate([split(rows[:vec3], 2), split(place, 3)], axis=0)
    descr = gather_edges(parts16, dm, valid, mv, ef, ee, f2s, hs, vec3, lanes)

    rad, vec, mix = w_rad[...], w_vec[...], w_mix[...]
    radt, vect, mixt, outt = rad_t[...], vec_t[...], mix_t[...], out_t[:, 0:1]
    flow = [dot32(vect, descr[c + 1]) for c in range(3)]
    mixed = dot32(radt, descr[0]) + flow[0] * flow[0] + flow[1] * flow[1] + flow[2] * flow[2]
    hidden = dot_split(mixt, mixed)
    gate = 1.0 / (1.0 + jnp.exp(-hidden))
    slope = gate * (1.0 + hidden * (1.0 - gate)) * outt
    bend = gate * (1.0 - gate) * (2.0 + hidden * (1.0 - 2.0 * gate)) * outt
    u = dot_split(mix, slope)
    alpha = dot32(rad, u)
    beta = [2.0 * dot32(vec, flow[c] * u) for c in range(3)]
    edge_rows(alpha, beta, ef, ee, f2s, hs, e8, lanes)
    contract(mv, ef, ee, lambda c, at: hs[8 * c : 8 * c + 8, at], xs, sx, atoms)
    channel_lift(flow, radt, vect, mixt, qs, qr, lanes, atoms)
    descriptor_curvature(vec, u, bend, qs, qr, bd, both, pmat, rmat, lanes, atoms)

    result = spread(dm, ef, ee, e8, pmat, rmat, mv, eo, xs, sx, cs, atoms)
    partial[...] = result
    store_patch((out_m, out_o, out_x), result, pick_matrix(places, 9 * atoms), atoms)


def product(left, right, vectors):
    total = jnp.zeros((vectors, vectors), jnp.float32)
    for c in range(3):
        total = total + dot_split(component(left, c, vectors), component(right, c, vectors), NT)
    return total


def sums_kernel(cext, pext, partial, out, *, vectors, atoms):
    old_c, old_p, new = cext[...], pext[...], partial[...]
    cw, pw = product(old_c, new, vectors), product(old_p, new, vectors)
    own_c, own_p = old_c[:, :atoms], old_p[:, :atoms]
    cc, cp, pp = (product(*pair, vectors) for pair in ((own_c, own_c), (own_c, own_p), (own_p, own_p)))
    out[...] = jnp.concatenate([with_diagonal(cw, pp), pw, cp, join_triangles(cc, pp)], axis=1)


def pair_kernel(resid, partial, out, *, vectors, atoms):
    r = resid[...]
    own = r[:, :atoms]
    lanes = out.shape[1]
    rr, ry = product(own, own, vectors), product(r, partial[...], vectors)
    out[...] = jnp.concatenate([flatten(rr, lanes), flatten(ry, lanes)], axis=0)


def second_kernel(order, own, mate, other, *rest, vectors, atoms, total_rows, chips):
    far, rest = rest[: chips - 2], rest[chips - 2 :]
    cext, pext, index, dm, ef, ee, e8, pmat, rmat, out_m, out_o, out_x, shared, rown, rext, partial = rest[:16]
    mv, eo, xs, sx, cs, patch, ring = rest[16:]
    half3 = 3 * vectors // 2
    vec3 = 2 * half3
    tail = 3 * half3
    pick = pick_matrix(index[0:1, :], 9 * atoms)
    ring[order[0]] = own[tail:, :]
    ring[order[1]] = other[tail:, :]
    for i, part in enumerate(far):
        ring[order[2 + i]] = part[...]
    total = ring[0]
    for i in range(1, chips):
        total = total + ring[i]
    total = total * (1.0 / total_rows)
    v = vectors
    held, pw, cp, joined = (total[:, i * v : (i + 1) * v] for i in range(4))
    coef = jnp.concatenate([from_lower(held), pw], axis=0)
    cc, pp = from_lower(joined), from_upper(joined, held)
    gram_old = jnp.concatenate(
        [jnp.concatenate([cc, cp], axis=1), jnp.concatenate([cp.T, pp], axis=1)], axis=0
    )
    shared[...] = jnp.concatenate([gram_old, coef, jnp.zeros_like(coef)], axis=1)

    for x, ref in enumerate((mate, own, other)):
        for y in range(3):
            at = (3 * y + x) * atoms
            patch[:, at : at + atoms] = unpack(ref[y * half3 : (y + 1) * half3, :], atoms)
    both = dot16(split(patch[...], 2), pick)
    work = both[:vec3] + both[vec3:]
    turned = coef.T
    resid = work - jnp.concatenate(
        [
            dot_split(
                turned,
                jnp.concatenate(
                    [component(cext[...], c, vectors), component(pext[...], c, vectors)], axis=0
                ),
            )
            for c in range(3)
        ],
        axis=0,
    )
    rown[...] = pack(resid[:, :atoms])
    rext[...] = resid
    parts16 = split(resid, 2)
    wide = 4 * atoms
    for j in range(dm.shape[1] // wide):
        at = slice(j * wide, (j + 1) * wide)
        got = dot16(parts16, dm[:, at])
        mv[:, at] = got[:vec3] + got[vec3:]
    contract(mv, ef, ee, lambda c, at: e8[c : c + 1, at], xs, sx, atoms)
    rows = spread(dm, ef, ee, e8, pmat, rmat, mv, eo, xs, sx, cs, atoms)
    partial[...] = rows
    store_patch((out_m, out_o, out_x), rows, pick, atoms)


def send_sums(pairs, yy, out):
    count, lanes = pairs.shape[0] // 2, pairs.shape[1]
    size = yy.shape[0]
    rr, ry = unflatten(pairs[:count], size), unflatten(pairs[count:], size)
    sent = jnp.concatenate(
        [flatten(join_triangles(rr, yy), lanes), flatten(with_diagonal(ry, yy), lanes)], axis=0
    )
    out[...] = jnp.broadcast_to(sent[None], out.shape)


def gram_kernel(pairs, y0, ym, yo, out, yown, *, vectors, atoms):
    work = y0[...] + ym[...] + yo[...]
    yown[...] = work
    y = unpack(work, atoms)
    send_sums(pairs[...], product(y, y, vectors), out)


def column_gram_kernel(order, own, mate, other, far, out, yown, held, *, vectors, atoms):
    half3 = 3 * vectors // 2

    def part(ref, which):
        return ref[which * half3 : (which + 1) * half3, :]

    m, zero, o = 0, 1, 2
    mine = part(own, zero) + part(mate, m) + part(other, o)
    yown[...] = mine
    held[order[0]] = mine
    held[order[1]] = part(mate, zero) + part(own, m) + part(far, o)
    held[order[2]] = part(other, zero) + part(far, m) + part(own, o)
    held[order[3]] = part(far, zero) + part(other, m) + part(mate, o)
    y = jnp.concatenate([unpack(held[i], atoms) for i in range(4)], axis=1)
    tail = 3 * half3
    pairs = (own[tail:, :] + mate[tail:, :]) + (other[tail:, :] + far[tail:, :])
    send_sums(pairs, product(y, y, vectors), out)


def cholesky(matrix, *extra):
    size = matrix.shape[0]
    rows, cols = rows_and_cols(size)
    unit = (rows == cols).astype(jnp.float32)
    work = jnp.concatenate([matrix, unit, *extra], axis=1)
    columns = [jnp.broadcast_to(matrix[:, k : k + 1], work.shape) for k in range(size)]
    lines = []
    for j in range(0, size, 2):
        first, second = columns[j], columns[j + 1]
        a, b, d = first[j : j + 1], first[j + 1 : j + 2], second[j + 1 : j + 2]
        det = a * d - b * b
        inverse = 1.0 / det
        ai, bi, di = a * inverse, b * inverse, d * inverse
        keep = (j + 2) // 8 * 8
        for k in range(j + 2, size):
            low = columns[k]
            x0, x1 = low[j : j + 1], low[j + 1 : j + 2]
            low = low[keep:] - (first[keep:] * (di * x0 - bi * x1) + second[keep:] * (ai * x1 - bi * x0))
            columns[k] = jnp.concatenate([columns[k][:keep], low], axis=0) if keep else low
        r0, r1 = work[j : j + 1], work[j + 1 : j + 2]
        work = work - (first * (di * r0 - bi * r1) + second * (ai * r1 - bi * r0))
        lines += [r0 * root_inverse(a), (r1 - (b / a) * r0) * root_inverse(det / a)]
    done = jnp.concatenate(lines, axis=0)
    upper = jnp.where(cols >= rows, done[:, :size], 0.0)
    return [upper] + [done[:, i * size : (i + 1) * size] for i in range(1, 2 + len(extra))]


def root_inverse(value):
    guess = lax.rsqrt(value)
    return guess * (1.5 - 0.5 * value * guess * guess)


def final_kernel(got, sums, rown, yown, cown, blocks, factors, *, vectors, atoms, total_rows):
    devices = got.shape[0]
    v = vectors
    total = got[0]
    for i in range(1, devices):
        total = total + got[i]
    total = total * (1.0 / total_rows)
    count = total.shape[0] // 2
    joined, held = unflatten(total[:count], v), unflatten(total[count:], v)
    rr, ry, yy = from_lower(joined), from_lower(held), from_upper(joined, held)
    shared = sums[...]
    gram_old, coef1 = shared[:, : 2 * v], shared[:, 2 * v : 3 * v]
    rows, cols = rows_and_cols(v)
    unit = (rows == cols).astype(jnp.float32)
    left = coef1 - dot32(gram_old, coef1)
    wr = rr + dot32(coef1, left, TN)
    fixed = yy + dot32(wr, dot32(gram_old[:v, :v] - 2.0 * unit, wr), TN)

    upper1, inv1, along, cross = cholesky(rr, ry, left[:v].T)
    mixed = dot32(cross, wr)
    gram2 = fixed + dot32(
        jnp.concatenate([along, mixed], axis=0), jnp.concatenate([mixed - along, along], axis=0), TN
    )
    upper2, inv2 = cholesky(gram2)
    factors[0] = upper1.T
    factors[1] = jnp.where(rows >= cols, dot32(inv1, upper2, NT), 0.0)
    r, y, old = unpack(rown[...], atoms), unpack(yown[...], atoms), cown[0 : 3 * vectors, 0:atoms]
    back = dot32(along, inv1, TN)
    weights = jnp.concatenate([-back, -wr.T], axis=1)
    for c in range(3):
        parts = [component(part, c, vectors) for part in (r, old)]
        blocks[0, c] = dot32(inv1, parts[0])
        rest = component(y, c, vectors) + dot32(weights, jnp.concatenate(parts, axis=0))
        blocks[1, c] = dot32(inv2, rest)


def mates(count):
    mate = [i ^ 1 for i in range(count)]
    other = [(i - 1) % count if i % 2 == 0 else (i + 1) % count for i in range(count)]
    return mate, other


def fetch(values, axis, sources):
    return lax.ppermute(values, axis, [(s, i) for i, s in enumerate(sources)])


def vmem_call(kernel, outs, scratch=(), scalars=0, flops=1 << 20):
    def call(*operands):
        spaces = [pltpu.SMEM] * scalars + [pltpu.VMEM] * (len(operands) - scalars)
        return pl.pallas_call(
            kernel,
            out_shape=outs,
            in_specs=[pl.BlockSpec(memory_space=s) for s in spaces],
            out_specs=jax.tree.map(lambda _: pl.BlockSpec(memory_space=pltpu.VMEM), outs),
            scratch_shapes=list(scratch),
            compiler_params=pltpu.CompilerParams(vmem_limit_bytes=VMEM_BYTES),
            cost_estimate=pl.CostEstimate(flops=flops, bytes_accessed=1 << 16, transcendentals=0),
        )(*operands)

    return call


def laid(shape, pieces):
    total = None
    for row, lane, piece in pieces:
        rows, lanes = piece.shape
        edges = ((row, shape[0] - row - rows), (lane, shape[1] - lane - lanes))
        placed = jnp.pad(piece, edges).astype(jnp.float32)
        total = placed if total is None else total + placed
    return total


def f32(*shape):
    return jax.ShapeDtypeStruct(shape, jnp.float32)


def shards(positions, block_prev, block_cur, neighbours, counts, x_lists, y_lists, w_radial, w_vector, w_mix, w_out):
    vectors, _, atoms = block_cur.shape
    halo = x_lists.shape[2]
    slots = neighbours.shape[0]
    basis, channels = w_radial.shape
    n_x, n_y = lax.axis_size("gx"), lax.axis_size("gy")
    total_rows = 3.0 * atoms * n_x * n_y
    half3 = 3 * vectors // 2
    vec3 = 3 * vectors
    lanes = 2 * atoms
    edges = slots * atoms
    extended = atoms + 4 * halo
    pairs = 2 * basis
    mate_x, other_x = mates(n_x)
    mate_y, other_y = mates(n_y)
    at_x, at_y = lax.axis_index("gx"), lax.axis_index("gy")
    sides = jnp.stack([at_x % 2, at_y % 2]).astype(jnp.int32)
    own_rows = vec3 + 8

    cur = block_cur.transpose(1, 0, 2).reshape(vec3, atoms)
    prev = block_prev.transpose(1, 0, 2).reshape(vec3, atoms)
    slab = f32(own_rows, lanes)
    all_rows = 2 * vec3 + 8

    table = laid(
        (own_rows, lanes),
        [
            (0, 0, cur),
            (0, atoms, prev),
            (vec3, 0, positions),
            (vec3 + 3, 0, x_lists[0]),
            (vec3 + 5, 0, y_lists[0]),
        ],
    )
    mate1 = fetch(table, "gx", mate_x)
    other1 = fetch(table, "gx", other_x)
    after = channels + 2 * basis + 8
    fixed = laid(
        (after + slots + 8, channels),
        [
            (0, 0, w_mix),
            (channels, 0, w_radial),
            (channels + basis, 0, w_vector),
            (channels + 2 * basis, 0, w_out[None]),
            (after, 0, neighbours),
            (after + slots, 0, counts[None]),
        ],
    )
    rad_shape, mix_shape, turned_shape = f32(basis, channels), f32(channels, channels), f32(channels, basis)
    dm, valid, rad, vec, mix, rad_t, vec_t, mix_t, out_t = vmem_call(
        functools.partial(prepare_kernel, slots=slots, atoms=atoms),
        [
            jax.ShapeDtypeStruct((extended, edges), jnp.bfloat16),
            f32(8, edges),
            rad_shape,
            rad_shape,
            mix_shape,
            turned_shape,
            turned_shape,
            mix_shape,
            f32(channels, 8),
        ],
        flops=1 << 24,
    )(fixed)
    to_mate, to_other, wide = vmem_call(
        functools.partial(select_kernel, atoms=atoms, halo=halo),
        [slab, slab, f32(all_rows, atoms + 2 * halo)],
        scalars=1,
    )(sides, table, mate1, other1)
    mate2 = fetch(to_mate, "gy", mate_y)
    other2 = fetch(to_other, "gy", other_y)

    work_scratch = [
        pltpu.VMEM((vec3, edges), jnp.float32),
        pltpu.VMEM((vec3, edges), jnp.float32),
        pltpu.VMEM((pairs, vectors, lanes), jnp.float32),
        pltpu.VMEM((pairs, vectors, lanes), jnp.float32),
        pltpu.VMEM((2 * pairs, vectors, lanes), jnp.float32),
    ]
    first = vmem_call(
        functools.partial(first_kernel, vectors=vectors, atoms=atoms, halo=halo),
        [
            f32(3 * half3, lanes),
            f32(3 * half3, lanes),
            f32(3 * half3, lanes),
            f32(vec3, extended),
            f32(vec3, extended),
            f32(vec3, extended),
            jax.ShapeDtypeStruct((8, extended), jnp.int32),
            f32(basis, edges),
            f32(basis, edges),
            f32(8, edges),
            f32(pairs * pairs, lanes),
            f32(pairs * pairs, lanes),
        ],
        work_scratch
        + [
            pltpu.VMEM((basis, edges), jnp.float32),
            pltpu.VMEM((32, edges), jnp.float32),
            pltpu.VMEM((channels, pairs * lanes), jnp.float32),
            pltpu.VMEM((channels, pairs * lanes), jnp.float32),
            pltpu.VMEM((channels, lanes), jnp.float32),
            pltpu.VMEM((basis, basis, lanes), jnp.float32),
        ],
        scalars=1,
        flops=1 << 31,
    )
    part_m, part_0, part_o, partial, cext, pext, index, ef, ee, e8, pmat, rmat = first(
        sides, wide, mate2, other2, dm, valid, rad, vec, mix, rad_t, vec_t, mix_t, out_t
    )

    back_m = fetch(part_m, "gx", mate_x)
    back_o = fetch(part_o, "gx", other_x)
    local = vmem_call(
        functools.partial(sums_kernel, vectors=vectors, atoms=atoms), f32(vectors, lanes), flops=1 << 25
    )(cext, pext, partial)
    local = local + fetch(local, "gx", mate_x)
    folded = part_0 + back_m + back_o
    f_m, f_0, f_o = folded[:half3], folded[half3 : 2 * half3], folded[2 * half3 :]

    far_m = [other_y[m] for m in mate_y]
    far_o = [mate_y[o] for o in other_y]
    got_m = fetch(jnp.concatenate([f_0, f_m, local]), "gy", mate_y)
    got_o = fetch(jnp.concatenate([f_0, f_o, local]), "gy", other_y)
    if far_m == far_o:
        got_2 = fetch(jnp.concatenate([f_m, f_o, local]), "gy", far_m)
        far_mate, far_other = got_2[half3 : 2 * half3], got_2[:half3]
        sums = (local + got_m[2 * half3 :]) + (got_o[2 * half3 :] + got_2[2 * half3 :])
    else:
        far_mate = fetch(f_o, "gy", far_m)
        far_other = fetch(f_m, "gy", far_o)
        terms = [local] + [
            fetch(local, "gy", [(i + d) % n_y for i in range(n_y)]) for d in range(1, n_y)
        ]
        sums = jnp.sum(jnp.roll(jnp.stack(terms), at_y, axis=0), axis=0)
    w_m = got_m[:half3] + f_m + far_mate
    w_0 = f_0 + got_m[half3 : 2 * half3] + got_o[half3 : 2 * half3]
    w_o = got_o[:half3] + far_other + f_o
    column = jnp.concatenate([w_m, w_0, w_o, sums])

    col_m = fetch(column, "gx", mate_x)
    col_o = fetch(column, "gx", other_x)
    pairs_x = n_x // 2
    steps = [d for d in range(1, pairs_x - 1)]
    far = [
        fetch(sums, "gx", [(i + 2 * d) % n_x if i % 2 == 0 else (i - 2 * d) % n_x for i in range(n_x)])
        for d in steps
    ]
    chip, way = at_x // 2, 1 - 2 * (at_x % 2)
    order = jnp.stack([(chip + d * way) % pairs_x for d in [0, -1] + steps]).astype(jnp.int32)

    second = vmem_call(
        functools.partial(second_kernel, vectors=vectors, atoms=atoms, total_rows=total_rows, chips=pairs_x),
        [
            f32(3 * half3, lanes),
            f32(3 * half3, lanes),
            f32(3 * half3, lanes),
            f32(2 * vectors, lanes),
            f32(half3, lanes),
            f32(vec3, extended),
            f32(vec3, extended),
        ],
        work_scratch
        + [pltpu.VMEM((vec3, 9 * atoms), jnp.float32), pltpu.VMEM((pairs_x, vectors, lanes), jnp.float32)],
        scalars=1,
        flops=1 << 30,
    )
    part_m, part_0, part_o, shared, rown, rext, partial = second(
        order, column, col_m, col_o, *far, cext, pext, index, dm, ef, ee, e8, pmat, rmat
    )
    back_m = fetch(part_m, "gx", mate_x)
    back_o = fetch(part_o, "gx", other_x)
    sent_rows = 2 * vectors * vectors // lanes
    pairs_rr = vmem_call(
        functools.partial(pair_kernel, vectors=vectors, atoms=atoms), f32(sent_rows, lanes), flops=1 << 25
    )(rext, partial)
    folded = part_0 + back_m + back_o
    if far_m == far_o:
        share = jnp.concatenate([folded, pairs_rr])
        got_m = fetch(share, "gy", mate_y)
        got_o = fetch(share, "gy", other_y)
        got_2 = fetch(share, "gy", far_m)
        order = jnp.stack([at_y, at_y ^ 1, (at_y - 1 + 2 * (at_y % 2)) % 4, (at_y + 2) % 4])
        spread_sums, yown = vmem_call(
            functools.partial(column_gram_kernel, vectors=vectors, atoms=atoms),
            [f32(n_x, sent_rows, lanes), f32(half3, lanes)],
            [pltpu.VMEM((4, half3, lanes), jnp.float32)],
            scalars=1,
        )(order.astype(jnp.int32), share, got_m, got_o, got_2)
        got = lax.all_to_all(spread_sums, "gx", 0, 0)
    else:
        y_m = fetch(folded[:half3], "gy", mate_y)
        y_o = fetch(folded[2 * half3 :], "gy", other_y)
        spread_sums, yown = vmem_call(
            functools.partial(gram_kernel, vectors=vectors, atoms=atoms),
            [f32(n_x * n_y, sent_rows, lanes), f32(half3, lanes)],
        )(pairs_rr, folded[half3 : 2 * half3], y_m, y_o)
        got = lax.all_to_all(spread_sums, ("gx", "gy"), 0, 0)
    blocks, factors = vmem_call(
        functools.partial(final_kernel, vectors=vectors, atoms=atoms, total_rows=total_rows),
        [f32(2, 3, vectors, atoms), f32(2, vectors, vectors)],
    )(got, shared, rown, yown, table)
    return blocks.transpose(0, 2, 1, 3), factors


def solution(mesh):
    placed = (
        P(None, ("gx", "gy")),
        P(None, None, ("gx", "gy")),
        P(None, None, ("gx", "gy")),
        P(None, ("gx", "gy")),
        P(("gx", "gy")),
        P(("gx", "gy"), None, None),
        P(("gx", "gy"), None, None),
        P(),
        P(),
        P(),
        P(),
    )
    return jax.shard_map(
        shards,
        mesh=mesh,
        in_specs=placed,
        out_specs=(P(None, None, None, ("gx", "gy")), P()),
        check_vma=False,
    )
```

```python
import functools

import jax
import jax.numpy as jnp
from jax import lax
from jax.experimental import pallas as pl
from jax.experimental.pallas import tpu as pltpu
from jax.sharding import PartitionSpec as P

SOFTEN = 0.25
CUTOFF = 5.0
GAUSS_WIDTH = 2.0
EXACT = lax.Precision.HIGHEST
VMEM_BYTES = 48 * 1024 * 1024
NN = (((1,), (0,)), ((), ()))
NT = (((1,), (1,)), ((), ()))
TN = (((0,), (0,)), ((), ()))


def dot16(left, right, dims=NN):
    return lax.dot_general(left, right, dims, preferred_element_type=jnp.float32)


def dot32(left, right, dims=NN):
    return lax.dot_general(
        left, right, dims, precision=EXACT, preferred_element_type=jnp.float32
    )


def split(values, parts):
    pieces = []
    for _ in range(parts):
        piece = values.astype(jnp.bfloat16)
        pieces.append(piece)
        values = values - piece.astype(jnp.float32)
    return jnp.concatenate(pieces, axis=0)


def dot_split(left, right, dims=NN):
    if dims == TN:
        left = left.T
        dims = NN
    rows = left.shape[0]
    both = split(left, 2)
    high = right.astype(jnp.bfloat16)
    low = (right - high.astype(jnp.float32)).astype(jnp.bfloat16)
    first = dot16(both, high, dims)
    return first[:rows] + first[rows:] + dot16(both[:rows], low, dims)


def component(block, comp, vectors):
    return block[comp * vectors : (comp + 1) * vectors]


def unpack(packed, atoms):
    return jnp.concatenate([packed[:, :atoms], packed[:, atoms:]], axis=0)


def pack(rows):
    half = rows.shape[0] // 2
    return jnp.concatenate([rows[:half], rows[half:]], axis=1)


def pick_matrix(index_row, patch_rows):
    extended = index_row.shape[1]
    rows = lax.broadcasted_iota(jnp.int32, (patch_rows, extended), 0)
    return (rows == index_row).astype(jnp.float32).astype(jnp.bfloat16)


def select(rows, *names):
    picks = jnp.concatenate(names, axis=1)
    hits = lax.broadcasted_iota(jnp.int32, (rows.shape[1], picks.shape[1]), 0) == picks
    got = dot16(split(rows, 3), hits.astype(jnp.float32).astype(jnp.bfloat16))
    count = rows.shape[0]
    return got[:count] + (got[count : 2 * count] + got[2 * count :])


def rows_and_cols(size):
    return (
        lax.broadcasted_iota(jnp.int32, (size, size), 0),
        lax.broadcasted_iota(jnp.int32, (size, size), 1),
    )


def join_triangles(lower, upper):
    rows, cols = rows_and_cols(lower.shape[0])
    return jnp.where(rows >= cols, lower, upper)


def with_diagonal(lower, source):
    size = lower.shape[0]
    rows, cols = rows_and_cols(size)
    line = jnp.sum(jnp.where(rows == cols, source, 0.0), axis=0, keepdims=True)
    upper = jnp.where(rows == 0, line, jnp.where((rows == 1) & (cols == size - 1), source[0:1, 0:1], 0.0))
    return jnp.where(rows >= cols, lower, upper)


def from_lower(joined):
    rows, cols = rows_and_cols(joined.shape[0])
    strict = jnp.where(rows > cols, joined, 0.0)
    return jnp.where(rows >= cols, joined, 0.0) + strict.T


def from_upper(joined, holder):
    size = joined.shape[0]
    rows, cols = rows_and_cols(size)
    strict = jnp.where(rows < cols, joined, 0.0)
    line = jnp.where(cols[0:1] >= 1, holder[0:1], holder[1:2, size - 1 : size])
    return strict + strict.T + jnp.where(rows == cols, line, 0.0)


def flatten(square, lanes):
    size = square.shape[0]
    rows = size * size // lanes
    return jnp.concatenate([square[i * rows : (i + 1) * rows] for i in range(lanes // size)], axis=1)


def unflatten(flat, size):
    return jnp.concatenate(
        [flat[:, i * size : (i + 1) * size] for i in range(flat.shape[1] // size)], axis=0
    )


def rows_of(tile, comp, vectors):
    return slice(comp * vectors + tile * 8, comp * vectors + tile * 8 + 8)


def contract(mv_ref, ef_ref, ee_ref, head_of, xs_ref, sx_ref, atoms):
    lanes = 2 * atoms
    basis, edges = ef_ref.shape
    vectors = mv_ref.shape[0] // 3
    pairs = 2 * basis
    lower = lax.broadcasted_iota(jnp.int32, (8, lanes), 1) < atoms
    for tile in range(vectors // 8):
        acc = [jnp.zeros((8, lanes), jnp.float32)] * (4 * basis)
        for j in range(edges // lanes):
            at = slice(j * lanes, (j + 1) * lanes)
            m = [mv_ref[rows_of(tile, c, vectors), at] for c in range(3)]
            head = [head_of(c, at) for c in range(3)]
            u = head[0] * m[0] + head[1] * m[1] + head[2] * m[2]
            along = [head[c] * u for c in range(3)]
            across = [m[c] - along[c] for c in range(3)]
            for k in range(basis):
                slope = ef_ref[k : k + 1, at]
                even = ee_ref[k : k + 1, at]
                acc[k] = acc[k] + slope * u
                for c in range(3):
                    i = (c + 1) * basis + k
                    acc[i] = acc[i] + (slope * along[c] + even * across[c])
        for i in range(pairs):
            a, b = acc[i], acc[i + pairs]
            x = jnp.where(lower, a, b) + pltpu.roll(jnp.where(lower, b, a), atoms, 1)
            xs_ref[i, tile * 8 : tile * 8 + 8, :] = x
            sx_ref[i, tile * 8 : tile * 8 + 8, :] = pltpu.roll(x, atoms, 1)


def spread(dm_ref, ef_ref, ee_ref, e8_ref, p_ref, r_ref, mv_ref, eo_ref, xs_ref, sx_ref, cs_ref, atoms):
    lanes = 2 * atoms
    basis, edges = ef_ref.shape
    groups = edges // lanes
    vec3 = mv_ref.shape[0]
    vectors = vec3 // 3
    pairs = 2 * basis
    tiles = vectors // 8
    wide_lower = lax.broadcasted_iota(jnp.int32, (8 * tiles, lanes), 1) < atoms

    def mix_step(kappa, carry):
        at = pl.ds(pl.multiple_of(kappa * pairs, pairs), pairs)
        straight = p_ref[at, :]
        crossed = r_ref[at, :]
        y = jnp.zeros((8 * tiles, lanes), jnp.float32)
        for i in range(pairs):
            y = y + straight[i : i + 1, :] * xs_ref[i] + crossed[i : i + 1, :] * sx_ref[i]
        turned = pltpu.roll(y, atoms, 1)
        cs_ref[kappa] = jnp.where(wide_lower, y, turned)
        cs_ref[kappa + pairs] = jnp.where(wide_lower, turned, y)
        return carry

    lax.fori_loop(0, pairs, mix_step, 0, unroll=8)

    total = None
    step = max(groups // 4, 1)
    for first in range(0, groups, step):
        for tile in range(tiles):
            coeff = [cs_ref[i, tile * 8 : tile * 8 + 8, :] for i in range(4 * basis)]
            for j in range(first, first + step):
                at = slice(j * lanes, (j + 1) * lanes)
                m = [mv_ref[rows_of(tile, c, vectors), at] for c in range(3)]
                row = [e8_ref[i : i + 1, at] for i in range(8)]
                head, turn = row[0:3], row[5:8]
                u = head[0] * m[0] + head[1] * m[1] + head[2] * m[2]
                radial = row[4] * u + (turn[0] * m[0] + turn[1] * m[1] + turn[2] * m[2])
                sums, evens = [None] * 3, [None] * 3
                for k in range(basis):
                    slope = ef_ref[k : k + 1, at]
                    even = ee_ref[k : k + 1, at]
                    radial = radial + slope * coeff[k]
                    for c in range(3):
                        i = (c + 1) * basis + k
                        more, plus = slope * coeff[i], even * coeff[i]
                        sums[c] = more if k == 0 else sums[c] + more
                        evens[c] = plus if k == 0 else evens[c] + plus
                for c in range(3):
                    radial = radial + head[c] * (sums[c] - evens[c])
                for c in range(3):
                    eo_ref[rows_of(tile, c, vectors), at] = (
                        evens[c] + head[c] * radial + (row[3] * m[c] + turn[c] * u)
                    )
        at = slice(first * lanes, (first + step) * lanes)
        both = dot16(split(eo_ref[:, at], 2), dm_ref[:, at], NT)
        part = both[:vec3] + both[vec3:]
        total = part if total is None else total + part
    return total


def stacked_sums(parts):
    row = lax.broadcasted_iota(jnp.int32, parts[0].shape, 0)

    def moved(values, by):
        return values + pltpu.roll(values, by % 8, 0)

    upper = row < 4
    fours = [
        jnp.where(upper, parts[i], parts[i + 4]) + pltpu.roll(jnp.where(upper, parts[i + 4], parts[i]), 4, 0)
        for i in range(4)
    ]
    twos = [jnp.where(row % 4 < 2, moved(fours[i], -2), moved(fours[i + 2], 2)) for i in range(2)]
    return jnp.where(row % 2 < 1, moved(twos[0], -1), moved(twos[1], 1))


def store_patch(outs, extended_rows, pick, atoms):
    vec3 = extended_rows.shape[0]
    half3 = vec3 // 2
    both = dot16(split(extended_rows, 2), pick, NT)
    patch = both[:vec3] + both[vec3:]
    for x in range(3):
        for y in range(3):
            at = (3 * y + x) * atoms
            tile = patch[:, at : at + atoms]
            outs[x][y * half3 : (y + 1) * half3, 0:atoms] = tile[:half3]
            outs[x][y * half3 : (y + 1) * half3, atoms : 2 * atoms] = tile[half3:]


def emit(even, rows, lists, to_mate, to_other):
    low, high = lists
    got = select(rows, jnp.where(even, low, high), jnp.where(even, high, low))
    halo = low.shape[1]
    vec3 = (rows.shape[0] - 8) // 2
    for which, out in enumerate((to_mate, to_other)):
        part = got[:, which * halo : (which + 1) * halo]
        out[0:vec3, :] = jnp.concatenate([part[0:vec3], part[vec3 : 2 * vec3]], axis=1)
        out[vec3:, :] = jnp.concatenate([part[2 * vec3 :], jnp.zeros_like(part[2 * vec3 :])], axis=1)


def unpack_rows(block, width):
    vec3 = block.shape[0] - 8
    return jnp.concatenate([block[:vec3, 0:width], block[:vec3, width : 2 * width], block[vec3:, 0:width]], axis=0)


def table_rows(table, atoms):
    rows = unpack_rows(table, atoms)
    count = rows.shape[0]
    number = lax.broadcasted_iota(jnp.int32, (8, atoms), 1).astype(jnp.float32)
    line = lax.broadcasted_iota(jnp.int32, (8, atoms), 0)
    last = jnp.where(line < 3, rows[count - 8 :], jnp.where(line == 3, number, 0.0))
    return jnp.concatenate([rows[: count - 8], last], axis=0)


def table_lists(table, line, halo):
    base = table.shape[0] - 8 + line
    rows = table[base : base + 2, 0:halo].astype(jnp.int32)
    return rows[0:1], rows[1:2]


def beside(rows, mate, other, even, step):
    line = rows.shape[0] - 5
    at = (lax.broadcasted_iota(jnp.int32, (rows.shape[0], 1), 0) == line).astype(jnp.float32) * step
    other = other + 2.0 * at
    return jnp.concatenate(
        [rows + at, jnp.where(even, other, mate), jnp.where(even, mate, other)], axis=1
    )


def select_kernel(sides, table, from_mate, from_other, to_mate, to_other, wide, *, atoms, halo):
    even = sides[0] == 0
    picked = []
    for ref, flip in ((from_mate[...], False), (from_other[...], True)):
        low, high = table_lists(ref, 3, halo)
        names = jnp.where(even, low, high) if flip else jnp.where(even, high, low)
        picked.append(select(table_rows(ref, atoms), names))
    got = beside(table_rows(table[...], atoms), *picked, even, float(atoms))
    wide[...] = got
    emit(sides[1] == 0, got, table_lists(table[...], 5, halo), to_mate, to_other)


def prepare_kernel(table, dm, valid, rad, vec, mix, rad_t, vec_t, mix_t, out_t, *, slots, atoms):
    lanes = 2 * atoms
    basis, channels = rad.shape
    starts = [0, channels, channels + basis, channels + 2 * basis, channels + 2 * basis + 8]
    w_mix, w_rad, w_vec = (table[starts[i] : starts[i + 1], :] for i in range(3))
    w_out = table[starts[3] : starts[4], :]
    ints = table[starts[4] :, 0:atoms].astype(jnp.int32)
    nb, count = ints[:slots], ints[slots : slots + 1]
    difference_matrix(dm, nb, dm.shape[0], atoms)
    lane = lax.broadcasted_iota(jnp.int32, (8, lanes), 1)
    first = jnp.where(lane < atoms, 0, slots // 2)
    limit = jnp.concatenate([count, count], axis=1)
    for j in range(slots // 2):
        valid[:, j * lanes : (j + 1) * lanes] = (first + j < limit).astype(jnp.float32)
    rad[...] = w_rad
    vec[...] = w_vec
    mix[...] = w_mix
    rad_t[...] = w_rad.T
    vec_t[...] = w_vec.T
    mix_t[...] = w_mix.T
    out_t[...] = w_out.T


def difference_matrix(dm_ref, nb, extended, atoms):
    half = nb.shape[0] // 2
    lanes = 2 * atoms
    paired = jnp.concatenate([nb[:half], nb[half:]], axis=1)
    rows = lax.broadcasted_iota(jnp.int32, (extended, lanes), 0)
    lane = lax.broadcasted_iota(jnp.int32, (extended, lanes), 1)
    own = (rows == jnp.where(lane < atoms, lane, lane - atoms)).astype(jnp.float32)
    for j in range(half):
        hit = (rows == paired[j : j + 1, :]).astype(jnp.float32)
        dm_ref[:, j * lanes : (j + 1) * lanes] = (hit - own).astype(jnp.bfloat16)


def gather_edges(parts16, dm, valid, mv, ef, ee, f2s, hs, vec3, lanes):
    basis, edges = ef.shape
    wide = 2 * lanes
    cut = 1.0 / (CUTOFF * CUTOFF)
    centre = (lax.broadcasted_iota(jnp.int32, (basis, wide), 0).astype(jnp.float32) + 0.5) * (CUTOFF / basis)
    totals = [jnp.zeros((basis, lanes), jnp.float32) for _ in range(4)]
    for j in range(edges // wide):
        at = slice(j * wide, (j + 1) * wide)
        got = dot16(parts16, dm[:, at])
        mv[:, at] = got[:vec3] + got[vec3 : 2 * vec3]
        third = 2 * vec3
        delta = got[third : third + 24] + got[third + 32 : third + 56] + got[third + 64 : third + 88]
        d = [delta[8 * c : 8 * c + 8] for c in range(3)]
        squared = d[0] * d[0] + d[1] * d[1] + d[2] * d[2] + SOFTEN
        radius = jnp.sqrt(squared)
        inverse = 1.0 / radius
        head = [d[c] * inverse for c in range(3)]
        tau = jnp.maximum(1.0 - squared * cut, 0.0)
        env = tau * tau * tau
        env1 = (-6.0 * cut) * radius * tau * tau
        env2 = (24.0 * cut * cut) * squared * tau - (6.0 * cut) * tau * tau
        off = radius - centre
        gauss = jnp.exp(-GAUSS_WIDTH * off * off) * valid[:, at]
        gauss1 = (-2.0 * GAUSS_WIDTH) * off * gauss
        gauss2 = (4.0 * GAUSS_WIDTH * GAUSS_WIDTH * off * off - 2.0 * GAUSS_WIDTH) * gauss
        value = gauss * env
        ef[:, at] = gauss1 * env + gauss * env1
        ee[:, at] = value * inverse
        f2s[:, at] = gauss2 * env + 2.0 * gauss1 * env1 + gauss * env2
        for c in range(3):
            hs[8 * c : 8 * c + 8, at] = head[c]
        hs[24:32, at] = inverse
        terms = [value, value * head[0], value * head[1], value * head[2]]
        totals = [t + v[:, :lanes] + v[:, lanes:] for t, v in zip(totals, terms)]
    return [t + pltpu.roll(t, lanes // 2, 1) for t in totals]


def edge_rows(alpha, beta, ef, ee, f2s, hs, e8, lanes):
    for j in range(ef.shape[1] // lanes):
        at = slice(j * lanes, (j + 1) * lanes)
        head = [hs[8 * c : 8 * c + 8, at] for c in range(3)]
        inverse = hs[24:32, at]
        slope_k, even_k, second = ef[:, at], ee[:, at], f2s[:, at]
        even1 = (slope_k - even_k) * inverse
        even2 = (second - 2.0 * even1) * inverse

        sums = stacked_sums(
            [alpha * slope_k, alpha * second]
            + [beta[c] * even1 for c in range(3)]
            + [beta[c] * even2 for c in range(3)]
        )
        first, bend_r = sums[0:1], sums[1:2]
        turn = [sums[2 + c : 3 + c] for c in range(3)]
        twist = [sums[5 + c : 6 + c] for c in range(3)]
        inv1 = inverse[0:1]
        h1 = [head[c][0:1] for c in range(3)]
        radius = 1.0 / inv1
        line = h1[0] * turn[0] + h1[1] * turn[1] + h1[2] * turn[2]
        isotropic = first * inv1 + line
        radial = bend_r + (h1[0] * twist[0] + h1[1] * twist[1] + h1[2] * twist[2]) * radius - isotropic
        e8[:, at] = jnp.concatenate(h1 + [isotropic, radial] + turn, axis=0)


def channel_lift(flow, rad_t, vec_t, mix_t, qs, qr, lanes, atoms):
    channels, basis = rad_t.shape
    lower = lax.broadcasted_iota(jnp.int32, (channels, lanes), 1) < atoms
    lift0 = 2.0 * jnp.where(lower, flow[0], flow[2])
    lift1 = 2.0 * flow[1]
    for i in range(2 * basis):
        k = i % basis
        if i < basis:
            side = jnp.where(lower, jnp.broadcast_to(rad_t[:, k : k + 1], lower.shape), lift1 * vec_t[:, k : k + 1])
        else:
            side = lift0 * vec_t[:, k : k + 1]
        lifted = dot_split(mix_t, side)
        qs[:, i * lanes : (i + 1) * lanes] = lifted
        qr[:, i * lanes : (i + 1) * lanes] = pltpu.roll(lifted, atoms, 1)


def descriptor_curvature(vec, u, bend, qs, qr, bd, both, pmat, rmat, lanes, atoms):
    basis = vec.shape[0]
    pairs = 2 * basis
    channels = bend.shape[0]
    bd[...] = bend
    low_row = lax.broadcasted_iota(jnp.int32, (basis, lanes), 1) < atoms
    for k in range(basis):
        both[k] = 2.0 * dot32(vec * vec[k : k + 1, :], u)

    def block(i, column):
        accs = None
        for tile in range(channels // 8):
            rows = slice(8 * tile, 8 * tile + 8)
            weight = bd[rows, :]
            left = [
                qs[rows, pl.ds(pl.multiple_of((i + d) * lanes, lanes), lanes)] * weight for d in range(2)
            ]
            columns = [slice((column + k) * lanes, (column + k + 1) * lanes) for k in range(basis)]
            right = [ref[rows, at] for ref in (qs, qr) for at in columns]
            terms = [l * r for l in left for r in right]
            accs = terms if accs is None else [a + t for a, t in zip(accs, terms)]
        return [stacked_sums(accs[q * basis : (q + 1) * basis]) for q in range(4)]

    def put(i, column, tiles):
        for d in range(2):
            at = pl.ds(pl.multiple_of((i + d) * pairs + column, basis), basis)
            pmat[at, :] = tiles[2 * d]
            rmat[at, :] = tiles[2 * d + 1]

    def upper_step(step, carry):
        i = 2 * step
        tiles = block(i, 0)
        for d in range(2):
            tiles[2 * d] = tiles[2 * d] + jnp.where(low_row, 0.0, both[i + d])
        put(i, 0, tiles)
        return carry

    def lower_step(step, carry):
        i = 2 * step + basis
        tiles = block(i, 0)
        put(i, 0, tiles)
        for d in range(2):
            pmat[pl.ds(i + d, basis, pairs), :] = tiles[2 * d]
            rmat[pl.ds(i + d, basis, pairs), :] = pltpu.roll(tiles[2 * d + 1], atoms, 1)
        tiles = block(i, basis)
        for d in range(2):
            tiles[2 * d] = tiles[2 * d] + both[i + d - basis]
        put(i, basis, tiles)
        return carry

    lax.fori_loop(0, basis // 2, upper_step, 0, unroll=True)
    lax.fori_loop(0, basis // 2, lower_step, 0, unroll=True)


def first_kernel(
    sides, wide, from_mate, from_other, dm, valid, w_rad, w_vec, w_mix, rad_t, vec_t, mix_t, out_t,
    out_m, out_o, out_x, partial, cext, pext, index, ef, ee, e8, pmat, rmat,
    mv, eo, xs, sx, cs, f2s, hs, qs, qr, bd, both,
    *, vectors, atoms, halo,
):
    half3 = 3 * vectors // 2
    vec3 = 2 * half3
    lanes = 2 * atoms
    rows = beside(
        wide[...],
        unpack_rows(from_mate[...], halo),
        unpack_rows(from_other[...], halo),
        sides[1] == 0,
        3.0 * atoms,
    )
    cext[...] = rows[:vec3]
    pext[...] = rows[vec3 : 2 * vec3]
    base = 2 * vec3
    places = jnp.round(rows[base + 3 : base + 4]).astype(jnp.int32)
    index[...] = jnp.broadcast_to(places, index.shape)
    shape = (8, rows.shape[1])
    place = jnp.concatenate(
        [jnp.broadcast_to(rows[base + c : base + c + 1], shape) for c in range(3)] + [jnp.zeros(shape, jnp.float32)],
        axis=0,
    )
    parts16 = jnp.concatenate([split(rows[:vec3], 2), split(place, 3)], axis=0)
    descr = gather_edges(parts16, dm, valid, mv, ef, ee, f2s, hs, vec3, lanes)

    rad, vec, mix = w_rad[...], w_vec[...], w_mix[...]
    radt, vect, mixt, outt = rad_t[...], vec_t[...], mix_t[...], out_t[:, 0:1]
    flow = [dot32(vect, descr[c + 1]) for c in range(3)]
    mixed = dot32(radt, descr[0]) + flow[0] * flow[0] + flow[1] * flow[1] + flow[2] * flow[2]
    hidden = dot_split(mixt, mixed)
    gate = 1.0 / (1.0 + jnp.exp(-hidden))
    slope = gate * (1.0 + hidden * (1.0 - gate)) * outt
    bend = gate * (1.0 - gate) * (2.0 + hidden * (1.0 - 2.0 * gate)) * outt
    u = dot_split(mix, slope)
    alpha = dot32(rad, u)
    beta = [2.0 * dot32(vec, flow[c] * u) for c in range(3)]
    edge_rows(alpha, beta, ef, ee, f2s, hs, e8, lanes)
    contract(mv, ef, ee, lambda c, at: hs[8 * c : 8 * c + 8, at], xs, sx, atoms)
    channel_lift(flow, radt, vect, mixt, qs, qr, lanes, atoms)
    descriptor_curvature(vec, u, bend, qs, qr, bd, both, pmat, rmat, lanes, atoms)

    result = spread(dm, ef, ee, e8, pmat, rmat, mv, eo, xs, sx, cs, atoms)
    partial[...] = result
    store_patch((out_m, out_o, out_x), result, pick_matrix(places, 9 * atoms), atoms)


def product(left, right, vectors):
    total = jnp.zeros((vectors, vectors), jnp.float32)
    for c in range(3):
        total = total + dot_split(component(left, c, vectors), component(right, c, vectors), NT)
    return total


def sums_kernel(cext, pext, partial, out, *, vectors, atoms):
    old_c, old_p, new = cext[...], pext[...], partial[...]
    cw, pw = product(old_c, new, vectors), product(old_p, new, vectors)
    own_c, own_p = old_c[:, :atoms], old_p[:, :atoms]
    cc, cp, pp = (product(*pair, vectors) for pair in ((own_c, own_c), (own_c, own_p), (own_p, own_p)))
    out[...] = jnp.concatenate([with_diagonal(cw, pp), pw, cp, join_triangles(cc, pp)], axis=1)


def pair_kernel(resid, partial, out, *, vectors, atoms):
    r = resid[...]
    own = r[:, :atoms]
    lanes = out.shape[1]
    rr, ry = product(own, own, vectors), product(r, partial[...], vectors)
    out[...] = jnp.concatenate([flatten(rr, lanes), flatten(ry, lanes)], axis=0)


def second_kernel(order, own, mate, other, *rest, vectors, atoms, total_rows, chips):
    far, rest = rest[: chips - 2], rest[chips - 2 :]
    cext, pext, index, dm, ef, ee, e8, pmat, rmat, out_m, out_o, out_x, shared, rown, rext, partial = rest[:16]
    mv, eo, xs, sx, cs, patch, ring = rest[16:]
    half3 = 3 * vectors // 2
    vec3 = 2 * half3
    tail = 3 * half3
    pick = pick_matrix(index[0:1, :], 9 * atoms)
    ring[order[0]] = own[tail:, :]
    ring[order[1]] = other[tail:, :]
    for i, part in enumerate(far):
        ring[order[2 + i]] = part[...]
    total = ring[0]
    for i in range(1, chips):
        total = total + ring[i]
    total = total * (1.0 / total_rows)
    v = vectors
    held, pw, cp, joined = (total[:, i * v : (i + 1) * v] for i in range(4))
    coef = jnp.concatenate([from_lower(held), pw], axis=0)
    cc, pp = from_lower(joined), from_upper(joined, held)
    gram_old = jnp.concatenate(
        [jnp.concatenate([cc, cp], axis=1), jnp.concatenate([cp.T, pp], axis=1)], axis=0
    )
    shared[...] = jnp.concatenate([gram_old, coef, jnp.zeros_like(coef)], axis=1)

    for x, ref in enumerate((mate, own, other)):
        for y in range(3):
            at = (3 * y + x) * atoms
            patch[:, at : at + atoms] = unpack(ref[y * half3 : (y + 1) * half3, :], atoms)
    both = dot16(split(patch[...], 2), pick)
    work = both[:vec3] + both[vec3:]
    turned = coef.T
    resid = work - jnp.concatenate(
        [
            dot_split(
                turned,
                jnp.concatenate(
                    [component(cext[...], c, vectors), component(pext[...], c, vectors)], axis=0
                ),
            )
            for c in range(3)
        ],
        axis=0,
    )
    rown[...] = pack(resid[:, :atoms])
    rext[...] = resid
    parts16 = split(resid, 2)
    wide = 4 * atoms
    for j in range(dm.shape[1] // wide):
        at = slice(j * wide, (j + 1) * wide)
        got = dot16(parts16, dm[:, at])
        mv[:, at] = got[:vec3] + got[vec3:]
    contract(mv, ef, ee, lambda c, at: e8[c : c + 1, at], xs, sx, atoms)
    rows = spread(dm, ef, ee, e8, pmat, rmat, mv, eo, xs, sx, cs, atoms)
    partial[...] = rows
    store_patch((out_m, out_o, out_x), rows, pick, atoms)


def send_sums(pairs, yy, out):
    count, lanes = pairs.shape[0] // 2, pairs.shape[1]
    size = yy.shape[0]
    rr, ry = unflatten(pairs[:count], size), unflatten(pairs[count:], size)
    sent = jnp.concatenate(
        [flatten(join_triangles(rr, yy), lanes), flatten(with_diagonal(ry, yy), lanes)], axis=0
    )
    out[...] = jnp.broadcast_to(sent[None], out.shape)


def gram_kernel(pairs, y0, ym, yo, out, yown, *, vectors, atoms):
    work = y0[...] + ym[...] + yo[...]
    yown[...] = work
    y = unpack(work, atoms)
    send_sums(pairs[...], product(y, y, vectors), out)


def column_gram_kernel(order, own, mate, other, far, out, yown, held, *, vectors, atoms):
    half3 = 3 * vectors // 2

    def part(ref, which):
        return ref[which * half3 : (which + 1) * half3, :]

    m, zero, o = 0, 1, 2
    mine = part(own, zero) + part(mate, m) + part(other, o)
    yown[...] = mine
    held[order[0]] = mine
    held[order[1]] = part(mate, zero) + part(own, m) + part(far, o)
    held[order[2]] = part(other, zero) + part(far, m) + part(own, o)
    held[order[3]] = part(far, zero) + part(other, m) + part(mate, o)
    y = jnp.concatenate([unpack(held[i], atoms) for i in range(4)], axis=1)
    tail = 3 * half3
    pairs = (own[tail:, :] + mate[tail:, :]) + (other[tail:, :] + far[tail:, :])
    send_sums(pairs, product(y, y, vectors), out)


def cholesky(matrix, *extra):
    size = matrix.shape[0]
    rows, cols = rows_and_cols(size)
    unit = (rows == cols).astype(jnp.float32)
    work = jnp.concatenate([matrix, unit, *extra], axis=1)
    columns = [jnp.broadcast_to(matrix[:, k : k + 1], work.shape) for k in range(size)]
    lines = []
    for j in range(0, size, 2):
        first, second = columns[j], columns[j + 1]
        a, b, d = first[j : j + 1], first[j + 1 : j + 2], second[j + 1 : j + 2]
        det = a * d - b * b
        inverse = 1.0 / det
        ai, bi, di = a * inverse, b * inverse, d * inverse
        keep = (j + 2) // 8 * 8
        for k in range(j + 2, size):
            low = columns[k]
            x0, x1 = low[j : j + 1], low[j + 1 : j + 2]
            low = low[keep:] - (first[keep:] * (di * x0 - bi * x1) + second[keep:] * (ai * x1 - bi * x0))
            columns[k] = jnp.concatenate([columns[k][:keep], low], axis=0) if keep else low
        r0, r1 = work[j : j + 1], work[j + 1 : j + 2]
        work = work - (first * (di * r0 - bi * r1) + second * (ai * r1 - bi * r0))
        lines += [r0 * root_inverse(a), (r1 - (b / a) * r0) * root_inverse(det / a)]
    done = jnp.concatenate(lines, axis=0)
    upper = jnp.where(cols >= rows, done[:, :size], 0.0)
    return [upper] + [done[:, i * size : (i + 1) * size] for i in range(1, 2 + len(extra))]


def root_inverse(value):
    guess = lax.rsqrt(value)
    return guess * (1.5 - 0.5 * value * guess * guess)


def final_kernel(got, sums, rown, yown, cown, blocks, factors, *, vectors, atoms, total_rows):
    devices = got.shape[0]
    v = vectors
    total = got[0]
    for i in range(1, devices):
        total = total + got[i]
    total = total * (1.0 / total_rows)
    count = total.shape[0] // 2
    joined, held = unflatten(total[:count], v), unflatten(total[count:], v)
    rr, ry, yy = from_lower(joined), from_lower(held), from_upper(joined, held)
    shared = sums[...]
    gram_old, coef1 = shared[:, : 2 * v], shared[:, 2 * v : 3 * v]
    rows, cols = rows_and_cols(v)
    unit = (rows == cols).astype(jnp.float32)
    left = coef1 - dot32(gram_old, coef1)
    wr = rr + dot32(coef1, left, TN)
    fixed = yy + dot32(wr, dot32(gram_old[:v, :v] - 2.0 * unit, wr), TN)

    upper1, inv1, along, cross = cholesky(rr, ry, left[:v].T)
    mixed = dot32(cross, wr)
    gram2 = fixed + dot32(
        jnp.concatenate([along, mixed], axis=0), jnp.concatenate([mixed - along, along], axis=0), TN
    )
    upper2, inv2 = cholesky(gram2)
    factors[0] = upper1.T
    factors[1] = jnp.where(rows >= cols, dot32(inv1, upper2, NT), 0.0)
    r, y, old = unpack(rown[...], atoms), unpack(yown[...], atoms), cown[0 : 3 * vectors, 0:atoms]
    back = dot32(along, inv1, TN)
    weights = jnp.concatenate([-back, -wr.T], axis=1)
    for c in range(3):
        parts = [component(part, c, vectors) for part in (r, old)]
        blocks[0, c] = dot32(inv1, parts[0])
        rest = component(y, c, vectors) + dot32(weights, jnp.concatenate(parts, axis=0))
        blocks[1, c] = dot32(inv2, rest)


def mates(count):
    mate = [i ^ 1 for i in range(count)]
    other = [(i - 1) % count if i % 2 == 0 else (i + 1) % count for i in range(count)]
    return mate, other


def fetch(values, axis, sources):
    return lax.ppermute(values, axis, [(s, i) for i, s in enumerate(sources)])


def vmem_call(kernel, outs, scratch=(), scalars=0, flops=1 << 20):
    def call(*operands):
        spaces = [pltpu.SMEM] * scalars + [pltpu.VMEM] * (len(operands) - scalars)
        return pl.pallas_call(
            kernel,
            out_shape=outs,
            in_specs=[pl.BlockSpec(memory_space=s) for s in spaces],
            out_specs=jax.tree.map(lambda _: pl.BlockSpec(memory_space=pltpu.VMEM), outs),
            scratch_shapes=list(scratch),
            compiler_params=pltpu.CompilerParams(vmem_limit_bytes=VMEM_BYTES),
            cost_estimate=pl.CostEstimate(flops=flops, bytes_accessed=1 << 16, transcendentals=0),
        )(*operands)

    return call


def laid(shape, pieces):
    total = None
    for row, lane, piece in pieces:
        rows, lanes = piece.shape
        edges = ((row, shape[0] - row - rows), (lane, shape[1] - lane - lanes))
        placed = jnp.pad(piece, edges).astype(jnp.float32)
        total = placed if total is None else total + placed
    return total


def f32(*shape):
    return jax.ShapeDtypeStruct(shape, jnp.float32)


def shards(positions, block_prev, block_cur, neighbours, counts, x_lists, y_lists, w_radial, w_vector, w_mix, w_out):
    vectors, _, atoms = block_cur.shape
    halo = x_lists.shape[2]
    slots = neighbours.shape[0]
    basis, channels = w_radial.shape
    n_x, n_y = lax.axis_size("gx"), lax.axis_size("gy")
    total_rows = 3.0 * atoms * n_x * n_y
    half3 = 3 * vectors // 2
    vec3 = 3 * vectors
    lanes = 2 * atoms
    edges = slots * atoms
    extended = atoms + 4 * halo
    pairs = 2 * basis
    mate_x, other_x = mates(n_x)
    mate_y, other_y = mates(n_y)
    at_x, at_y = lax.axis_index("gx"), lax.axis_index("gy")
    sides = jnp.stack([at_x % 2, at_y % 2]).astype(jnp.int32)
    own_rows = vec3 + 8

    cur = block_cur.transpose(1, 0, 2).reshape(vec3, atoms)
    prev = block_prev.transpose(1, 0, 2).reshape(vec3, atoms)
    slab = f32(own_rows, lanes)
    all_rows = 2 * vec3 + 8

    table = laid(
        (own_rows, lanes),
        [
            (0, 0, cur),
            (0, atoms, prev),
            (vec3, 0, positions),
            (vec3 + 3, 0, x_lists[0]),
            (vec3 + 5, 0, y_lists[0]),
        ],
    )
    mate1 = fetch(table, "gx", mate_x)
    other1 = fetch(table, "gx", other_x)
    after = channels + 2 * basis + 8
    fixed = laid(
        (after + slots + 8, channels),
        [
            (0, 0, w_mix),
            (channels, 0, w_radial),
            (channels + basis, 0, w_vector),
            (channels + 2 * basis, 0, w_out[None]),
            (after, 0, neighbours),
            (after + slots, 0, counts[None]),
        ],
    )
    rad_shape, mix_shape, turned_shape = f32(basis, channels), f32(channels, channels), f32(channels, basis)
    dm, valid, rad, vec, mix, rad_t, vec_t, mix_t, out_t = vmem_call(
        functools.partial(prepare_kernel, slots=slots, atoms=atoms),
        [
            jax.ShapeDtypeStruct((extended, edges), jnp.bfloat16),
            f32(8, edges),
            rad_shape,
            rad_shape,
            mix_shape,
            turned_shape,
            turned_shape,
            mix_shape,
            f32(channels, 8),
        ],
        flops=1 << 24,
    )(fixed)
    to_mate, to_other, wide = vmem_call(
        functools.partial(select_kernel, atoms=atoms, halo=halo),
        [slab, slab, f32(all_rows, atoms + 2 * halo)],
        scalars=1,
    )(sides, table, mate1, other1)
    mate2 = fetch(to_mate, "gy", mate_y)
    other2 = fetch(to_other, "gy", other_y)

    work_scratch = [
        pltpu.VMEM((vec3, edges), jnp.float32),
        pltpu.VMEM((vec3, edges), jnp.float32),
        pltpu.VMEM((pairs, vectors, lanes), jnp.float32),
        pltpu.VMEM((pairs, vectors, lanes), jnp.float32),
        pltpu.VMEM((2 * pairs, vectors, lanes), jnp.float32),
    ]
    first = vmem_call(
        functools.partial(first_kernel, vectors=vectors, atoms=atoms, halo=halo),
        [
            f32(3 * half3, lanes),
            f32(3 * half3, lanes),
            f32(3 * half3, lanes),
            f32(vec3, extended),
            f32(vec3, extended),
            f32(vec3, extended),
            jax.ShapeDtypeStruct((8, extended), jnp.int32),
            f32(basis, edges),
            f32(basis, edges),
            f32(8, edges),
            f32(pairs * pairs, lanes),
            f32(pairs * pairs, lanes),
        ],
        work_scratch
        + [
            pltpu.VMEM((basis, edges), jnp.float32),
            pltpu.VMEM((32, edges), jnp.float32),
            pltpu.VMEM((channels, pairs * lanes), jnp.float32),
            pltpu.VMEM((channels, pairs * lanes), jnp.float32),
            pltpu.VMEM((channels, lanes), jnp.float32),
            pltpu.VMEM((basis, basis, lanes), jnp.float32),
        ],
        scalars=1,
        flops=1 << 31,
    )
    part_m, part_0, part_o, partial, cext, pext, index, ef, ee, e8, pmat, rmat = first(
        sides, wide, mate2, other2, dm, valid, rad, vec, mix, rad_t, vec_t, mix_t, out_t
    )

    back_m = fetch(part_m, "gx", mate_x)
    back_o = fetch(part_o, "gx", other_x)
    local = vmem_call(
        functools.partial(sums_kernel, vectors=vectors, atoms=atoms), f32(vectors, lanes), flops=1 << 25
    )(cext, pext, partial)
    local = local + fetch(local, "gx", mate_x)
    folded = part_0 + back_m + back_o
    f_m, f_0, f_o = folded[:half3], folded[half3 : 2 * half3], folded[2 * half3 :]

    far_m = [other_y[m] for m in mate_y]
    far_o = [mate_y[o] for o in other_y]
    got_m = fetch(jnp.concatenate([f_0, f_m, local]), "gy", mate_y)
    got_o = fetch(jnp.concatenate([f_0, f_o, local]), "gy", other_y)
    if far_m == far_o:
        got_2 = fetch(jnp.concatenate([f_m, f_o, local]), "gy", far_m)
        far_mate, far_other = got_2[half3 : 2 * half3], got_2[:half3]
        sums = (local + got_m[2 * half3 :]) + (got_o[2 * half3 :] + got_2[2 * half3 :])
    else:
        far_mate = fetch(f_o, "gy", far_m)
        far_other = fetch(f_m, "gy", far_o)
        terms = [local] + [
            fetch(local, "gy", [(i + d) % n_y for i in range(n_y)]) for d in range(1, n_y)
        ]
        sums = jnp.sum(jnp.roll(jnp.stack(terms), at_y, axis=0), axis=0)
    w_m = got_m[:half3] + f_m + far_mate
    w_0 = f_0 + got_m[half3 : 2 * half3] + got_o[half3 : 2 * half3]
    w_o = got_o[:half3] + far_other + f_o
    column = jnp.concatenate([w_m, w_0, w_o, sums])

    col_m = fetch(column, "gx", mate_x)
    col_o = fetch(column, "gx", other_x)
    pairs_x = n_x // 2
    steps = [d for d in range(1, pairs_x - 1)]
    far = [
        fetch(sums, "gx", [(i + 2 * d) % n_x if i % 2 == 0 else (i - 2 * d) % n_x for i in range(n_x)])
        for d in steps
    ]
    chip, way = at_x // 2, 1 - 2 * (at_x % 2)
    order = jnp.stack([(chip + d * way) % pairs_x for d in [0, -1] + steps]).astype(jnp.int32)

    second = vmem_call(
        functools.partial(second_kernel, vectors=vectors, atoms=atoms, total_rows=total_rows, chips=pairs_x),
        [
            f32(3 * half3, lanes),
            f32(3 * half3, lanes),
            f32(3 * half3, lanes),
            f32(2 * vectors, lanes),
            f32(half3, lanes),
            f32(vec3, extended),
            f32(vec3, extended),
        ],
        work_scratch
        + [pltpu.VMEM((vec3, 9 * atoms), jnp.float32), pltpu.VMEM((pairs_x, vectors, lanes), jnp.float32)],
        scalars=1,
        flops=1 << 30,
    )
    part_m, part_0, part_o, shared, rown, rext, partial = second(
        order, column, col_m, col_o, *far, cext, pext, index, dm, ef, ee, e8, pmat, rmat
    )
    back_m = fetch(part_m, "gx", mate_x)
    back_o = fetch(part_o, "gx", other_x)
    sent_rows = 2 * vectors * vectors // lanes
    pairs_rr = vmem_call(
        functools.partial(pair_kernel, vectors=vectors, atoms=atoms), f32(sent_rows, lanes), flops=1 << 25
    )(rext, partial)
    folded = part_0 + back_m + back_o
    if far_m == far_o:
        share = jnp.concatenate([folded, pairs_rr])
        got_m = fetch(share, "gy", mate_y)
        got_o = fetch(share, "gy", other_y)
        got_2 = fetch(share, "gy", far_m)
        order = jnp.stack([at_y, at_y ^ 1, (at_y - 1 + 2 * (at_y % 2)) % 4, (at_y + 2) % 4])
        spread_sums, yown = vmem_call(
            functools.partial(column_gram_kernel, vectors=vectors, atoms=atoms),
            [f32(n_x, sent_rows, lanes), f32(half3, lanes)],
            [pltpu.VMEM((4, half3, lanes), jnp.float32)],
            scalars=1,
        )(order.astype(jnp.int32), share, got_m, got_o, got_2)
        got = lax.all_to_all(spread_sums, "gx", 0, 0)
    else:
        y_m = fetch(folded[:half3], "gy", mate_y)
        y_o = fetch(folded[2 * half3 :], "gy", other_y)
        spread_sums, yown = vmem_call(
            functools.partial(gram_kernel, vectors=vectors, atoms=atoms),
            [f32(n_x * n_y, sent_rows, lanes), f32(half3, lanes)],
        )(pairs_rr, folded[half3 : 2 * half3], y_m, y_o)
        got = lax.all_to_all(spread_sums, ("gx", "gy"), 0, 0)
    blocks, factors = vmem_call(
        functools.partial(final_kernel, vectors=vectors, atoms=atoms, total_rows=total_rows),
        [f32(2, 3, vectors, atoms), f32(2, vectors, vectors)],
    )(got, shared, rown, yown, table)
    return blocks.transpose(0, 2, 1, 3), factors


def solution(mesh):
    placed = (
        P(None, ("gx", "gy")),
        P(None, None, ("gx", "gy")),
        P(None, None, ("gx", "gy")),
        P(None, ("gx", "gy")),
        P(("gx", "gy")),
        P(("gx", "gy"), None, None),
        P(("gx", "gy"), None, None),
        P(),
        P(),
        P(),
        P(),
    )
    return jax.shard_map(
        shards,
        mesh=mesh,
        in_specs=placed,
        out_specs=(P(None, None, None, ("gx", "gy")), P()),
        check_vma=False,
    )
```

```python
import functools

import jax
import jax.numpy as jnp
from jax import lax
from jax.experimental import pallas as pl
from jax.experimental.pallas import tpu as pltpu
from jax.sharding import PartitionSpec as P

SOFTEN = 0.25
CUTOFF = 5.0
GAUSS_WIDTH = 2.0
EXACT = lax.Precision.HIGHEST
VMEM_BYTES = 48 * 1024 * 1024
NN = (((1,), (0,)), ((), ()))
NT = (((1,), (1,)), ((), ()))
TN = (((0,), (0,)), ((), ()))


def dot16(left, right, dims=NN):
    return lax.dot_general(left, right, dims, preferred_element_type=jnp.float32)


def dot32(left, right, dims=NN):
    return lax.dot_general(
        left, right, dims, precision=EXACT, preferred_element_type=jnp.float32
    )


def split(values, parts):
    pieces = []
    for _ in range(parts):
        piece = values.astype(jnp.bfloat16)
        pieces.append(piece)
        values = values - piece.astype(jnp.float32)
    return jnp.concatenate(pieces, axis=0)


def dot_split(left, right, dims=NN):
    if dims == TN:
        left = left.T
        dims = NN
    rows = left.shape[0]
    both = split(left, 2)
    high = right.astype(jnp.bfloat16)
    low = (right - high.astype(jnp.float32)).astype(jnp.bfloat16)
    first = dot16(both, high, dims)
    return first[:rows] + first[rows:] + dot16(both[:rows], low, dims)


def component(block, comp, vectors):
    return block[comp * vectors : (comp + 1) * vectors]


def unpack(packed, atoms):
    return jnp.concatenate([packed[:, :atoms], packed[:, atoms:]], axis=0)


def pack(rows):
    half = rows.shape[0] // 2
    return jnp.concatenate([rows[:half], rows[half:]], axis=1)


def pick_matrix(index_row, patch_rows):
    extended = index_row.shape[1]
    rows = lax.broadcasted_iota(jnp.int32, (patch_rows, extended), 0)
    return (rows == index_row).astype(jnp.float32).astype(jnp.bfloat16)


def select(rows, *names):
    picks = jnp.concatenate(names, axis=1)
    hits = lax.broadcasted_iota(jnp.int32, (rows.shape[1], picks.shape[1]), 0) == picks
    got = dot16(split(rows, 3), hits.astype(jnp.float32).astype(jnp.bfloat16))
    count = rows.shape[0]
    return got[:count] + (got[count : 2 * count] + got[2 * count :])


def rows_and_cols(size):
    return (
        lax.broadcasted_iota(jnp.int32, (size, size), 0),
        lax.broadcasted_iota(jnp.int32, (size, size), 1),
    )


def join_triangles(lower, upper):
    rows, cols = rows_and_cols(lower.shape[0])
    return jnp.where(rows >= cols, lower, upper)


def with_diagonal(lower, source):
    size = lower.shape[0]
    rows, cols = rows_and_cols(size)
    line = jnp.sum(jnp.where(rows == cols, source, 0.0), axis=0, keepdims=True)
    upper = jnp.where(rows == 0, line, jnp.where((rows == 1) & (cols == size - 1), source[0:1, 0:1], 0.0))
    return jnp.where(rows >= cols, lower, upper)


def from_lower(joined):
    rows, cols = rows_and_cols(joined.shape[0])
    strict = jnp.where(rows > cols, joined, 0.0)
    return jnp.where(rows >= cols, joined, 0.0) + strict.T


def from_upper(joined, holder):
    size = joined.shape[0]
    rows, cols = rows_and_cols(size)
    strict = jnp.where(rows < cols, joined, 0.0)
    line = jnp.where(cols[0:1] >= 1, holder[0:1], holder[1:2, size - 1 : size])
    return strict + strict.T + jnp.where(rows == cols, line, 0.0)


def flatten(square, lanes):
    size = square.shape[0]
    rows = size * size // lanes
    return jnp.concatenate([square[i * rows : (i + 1) * rows] for i in range(lanes // size)], axis=1)


def unflatten(flat, size):
    return jnp.concatenate(
        [flat[:, i * size : (i + 1) * size] for i in range(flat.shape[1] // size)], axis=0
    )


def rows_of(tile, comp, vectors):
    return slice(comp * vectors + tile * 8, comp * vectors + tile * 8 + 8)


def contract(mv_ref, ef_ref, ee_ref, head_of, xs_ref, sx_ref, atoms):
    lanes = 2 * atoms
    basis, edges = ef_ref.shape
    vectors = mv_ref.shape[0] // 3
    pairs = 2 * basis
    lower = lax.broadcasted_iota(jnp.int32, (8, lanes), 1) < atoms
    for tile in range(vectors // 8):
        acc = [jnp.zeros((8, lanes), jnp.float32)] * (4 * basis)
        for j in range(edges // lanes):
            at = slice(j * lanes, (j + 1) * lanes)
            m = [mv_ref[rows_of(tile, c, vectors), at] for c in range(3)]
            head = [head_of(c, at) for c in range(3)]
            u = head[0] * m[0] + head[1] * m[1] + head[2] * m[2]
            along = [head[c] * u for c in range(3)]
            across = [m[c] - along[c] for c in range(3)]
            for k in range(basis):
                slope = ef_ref[k : k + 1, at]
                even = ee_ref[k : k + 1, at]
                acc[k] = acc[k] + slope * u
                for c in range(3):
                    i = (c + 1) * basis + k
                    acc[i] = acc[i] + (slope * along[c] + even * across[c])
        for i in range(pairs):
            a, b = acc[i], acc[i + pairs]
            x = jnp.where(lower, a, b) + pltpu.roll(jnp.where(lower, b, a), atoms, 1)
            xs_ref[i, tile * 8 : tile * 8 + 8, :] = x
            sx_ref[i, tile * 8 : tile * 8 + 8, :] = pltpu.roll(x, atoms, 1)


def spread(dm_ref, ef_ref, ee_ref, e8_ref, p_ref, r_ref, mv_ref, eo_ref, xs_ref, sx_ref, cs_ref, atoms):
    lanes = 2 * atoms
    basis, edges = ef_ref.shape
    groups = edges // lanes
    vec3 = mv_ref.shape[0]
    vectors = vec3 // 3
    pairs = 2 * basis
    tiles = vectors // 8
    wide_lower = lax.broadcasted_iota(jnp.int32, (8 * tiles, lanes), 1) < atoms

    def mix_step(kappa, carry):
        at = pl.ds(pl.multiple_of(kappa * pairs, pairs), pairs)
        straight = p_ref[at, :]
        crossed = r_ref[at, :]
        y = jnp.zeros((8 * tiles, lanes), jnp.float32)
        for i in range(pairs):
            y = y + straight[i : i + 1, :] * xs_ref[i] + crossed[i : i + 1, :] * sx_ref[i]
        turned = pltpu.roll(y, atoms, 1)
        cs_ref[kappa] = jnp.where(wide_lower, y, turned)
        cs_ref[kappa + pairs] = jnp.where(wide_lower, turned, y)
        return carry

    lax.fori_loop(0, pairs, mix_step, 0, unroll=8)

    total = None
    step = max(groups // 4, 1)
    for first in range(0, groups, step):
        for tile in range(tiles):
            coeff = [cs_ref[i, tile * 8 : tile * 8 + 8, :] for i in range(4 * basis)]
            for j in range(first, first + step):
                at = slice(j * lanes, (j + 1) * lanes)
                m = [mv_ref[rows_of(tile, c, vectors), at] for c in range(3)]
                row = [e8_ref[i : i + 1, at] for i in range(8)]
                head, turn = row[0:3], row[5:8]
                u = head[0] * m[0] + head[1] * m[1] + head[2] * m[2]
                radial = row[4] * u + (turn[0] * m[0] + turn[1] * m[1] + turn[2] * m[2])
                sums, evens = [None] * 3, [None] * 3
                for k in range(basis):
                    slope = ef_ref[k : k + 1, at]
                    even = ee_ref[k : k + 1, at]
                    radial = radial + slope * coeff[k]
                    for c in range(3):
                        i = (c + 1) * basis + k
                        more, plus = slope * coeff[i], even * coeff[i]
                        sums[c] = more if k == 0 else sums[c] + more
                        evens[c] = plus if k == 0 else evens[c] + plus
                for c in range(3):
                    radial = radial + head[c] * (sums[c] - evens[c])
                for c in range(3):
                    eo_ref[rows_of(tile, c, vectors), at] = (
                        evens[c] + head[c] * radial + (row[3] * m[c] + turn[c] * u)
                    )
        at = slice(first * lanes, (first + step) * lanes)
        both = dot16(split(eo_ref[:, at], 2), dm_ref[:, at], NT)
        part = both[:vec3] + both[vec3:]
        total = part if total is None else total + part
    return total


def stacked_sums(parts):
    row = lax.broadcasted_iota(jnp.int32, parts[0].shape, 0)

    def moved(values, by):
        return values + pltpu.roll(values, by % 8, 0)

    upper = row < 4
    fours = [
        jnp.where(upper, parts[i], parts[i + 4]) + pltpu.roll(jnp.where(upper, parts[i + 4], parts[i]), 4, 0)
        for i in range(4)
    ]
    twos = [jnp.where(row % 4 < 2, moved(fours[i], -2), moved(fours[i + 2], 2)) for i in range(2)]
    return jnp.where(row % 2 < 1, moved(twos[0], -1), moved(twos[1], 1))


def store_patch(outs, extended_rows, pick, atoms):
    vec3 = extended_rows.shape[0]
    half3 = vec3 // 2
    both = dot16(split(extended_rows, 2), pick, NT)
    patch = both[:vec3] + both[vec3:]
    for x in range(3):
        for y in range(3):
            at = (3 * y + x) * atoms
            tile = patch[:, at : at + atoms]
            outs[x][y * half3 : (y + 1) * half3, 0:atoms] = tile[:half3]
            outs[x][y * half3 : (y + 1) * half3, atoms : 2 * atoms] = tile[half3:]


def emit(even, rows, lists, to_mate, to_other):
    low, high = lists
    got = select(rows, jnp.where(even, low, high), jnp.where(even, high, low))
    halo = low.shape[1]
    vec3 = (rows.shape[0] - 8) // 2
    for which, out in enumerate((to_mate, to_other)):
        part = got[:, which * halo : (which + 1) * halo]
        out[0:vec3, :] = jnp.concatenate([part[0:vec3], part[vec3 : 2 * vec3]], axis=1)
        out[vec3:, :] = jnp.concatenate([part[2 * vec3 :], jnp.zeros_like(part[2 * vec3 :])], axis=1)


def unpack_rows(block, width):
    vec3 = block.shape[0] - 8
    return jnp.concatenate([block[:vec3, 0:width], block[:vec3, width : 2 * width], block[vec3:, 0:width]], axis=0)


def table_rows(table, atoms):
    rows = unpack_rows(table, atoms)
    count = rows.shape[0]
    number = lax.broadcasted_iota(jnp.int32, (8, atoms), 1).astype(jnp.float32)
    line = lax.broadcasted_iota(jnp.int32, (8, atoms), 0)
    last = jnp.where(line < 3, rows[count - 8 :], jnp.where(line == 3, number, 0.0))
    return jnp.concatenate([rows[: count - 8], last], axis=0)


def table_lists(table, line, halo):
    base = table.shape[0] - 8 + line
    rows = table[base : base + 2, 0:halo].astype(jnp.int32)
    return rows[0:1], rows[1:2]


def beside(rows, mate, other, even, step):
    line = rows.shape[0] - 5
    at = (lax.broadcasted_iota(jnp.int32, (rows.shape[0], 1), 0) == line).astype(jnp.float32) * step
    other = other + 2.0 * at
    return jnp.concatenate(
        [rows + at, jnp.where(even, other, mate), jnp.where(even, mate, other)], axis=1
    )


def select_kernel(sides, table, from_mate, from_other, to_mate, to_other, wide, *, atoms, halo):
    even = sides[0] == 0
    picked = []
    for ref, flip in ((from_mate[...], False), (from_other[...], True)):
        low, high = table_lists(ref, 3, halo)
        names = jnp.where(even, low, high) if flip else jnp.where(even, high, low)
        picked.append(select(table_rows(ref, atoms), names))
    got = beside(table_rows(table[...], atoms), *picked, even, float(atoms))
    wide[...] = got
    emit(sides[1] == 0, got, table_lists(table[...], 5, halo), to_mate, to_other)


def prepare_kernel(table, dm, valid, rad, vec, mix, rad_t, vec_t, mix_t, out_t, *, slots, atoms):
    lanes = 2 * atoms
    basis, channels = rad.shape
    starts = [0, channels, channels + basis, channels + 2 * basis, channels + 2 * basis + 8]
    w_mix, w_rad, w_vec = (table[starts[i] : starts[i + 1], :] for i in range(3))
    w_out = table[starts[3] : starts[4], :]
    ints = table[starts[4] :, 0:atoms].astype(jnp.int32)
    nb, count = ints[:slots], ints[slots : slots + 1]
    difference_matrix(dm, nb, dm.shape[0], atoms)
    lane = lax.broadcasted_iota(jnp.int32, (8, lanes), 1)
    first = jnp.where(lane < atoms, 0, slots // 2)
    limit = jnp.concatenate([count, count], axis=1)
    for j in range(slots // 2):
        valid[:, j * lanes : (j + 1) * lanes] = (first + j < limit).astype(jnp.float32)
    rad[...] = w_rad
    vec[...] = w_vec
    mix[...] = w_mix
    rad_t[...] = w_rad.T
    vec_t[...] = w_vec.T
    mix_t[...] = w_mix.T
    out_t[...] = w_out.T


def difference_matrix(dm_ref, nb, extended, atoms):
    half = nb.shape[0] // 2
    lanes = 2 * atoms
    paired = jnp.concatenate([nb[:half], nb[half:]], axis=1)
    rows = lax.broadcasted_iota(jnp.int32, (extended, lanes), 0)
    lane = lax.broadcasted_iota(jnp.int32, (extended, lanes), 1)
    own = (rows == jnp.where(lane < atoms, lane, lane - atoms)).astype(jnp.float32)
    for j in range(half):
        hit = (rows == paired[j : j + 1, :]).astype(jnp.float32)
        dm_ref[:, j * lanes : (j + 1) * lanes] = (hit - own).astype(jnp.bfloat16)


def gather_edges(parts16, dm, valid, mv, ef, ee, f2s, hs, vec3, lanes):
    basis, edges = ef.shape
    wide = 2 * lanes
    cut = 1.0 / (CUTOFF * CUTOFF)
    centre = (lax.broadcasted_iota(jnp.int32, (basis, wide), 0).astype(jnp.float32) + 0.5) * (CUTOFF / basis)
    totals = [jnp.zeros((basis, lanes), jnp.float32) for _ in range(4)]
    for j in range(edges // wide):
        at = slice(j * wide, (j + 1) * wide)
        got = dot16(parts16, dm[:, at])
        mv[:, at] = got[:vec3] + got[vec3 : 2 * vec3]
        third = 2 * vec3
        delta = got[third : third + 8] + got[third + 16 : third + 24] + got[third + 32 : third + 40]
        d = [jnp.broadcast_to(delta[c : c + 1], delta.shape) for c in range(3)]
        squared = d[0] * d[0] + d[1] * d[1] + d[2] * d[2] + SOFTEN
        radius = jnp.sqrt(squared)
        inverse = 1.0 / radius
        head = [d[c] * inverse for c in range(3)]
        tau = jnp.maximum(1.0 - squared * cut, 0.0)
        env = tau * tau * tau
        env1 = (-6.0 * cut) * radius * tau * tau
        env2 = (24.0 * cut * cut) * squared * tau - (6.0 * cut) * tau * tau
        off = radius - centre
        gauss = jnp.exp(-GAUSS_WIDTH * off * off) * valid[:, at]
        gauss1 = (-2.0 * GAUSS_WIDTH) * off * gauss
        gauss2 = (4.0 * GAUSS_WIDTH * GAUSS_WIDTH * off * off - 2.0 * GAUSS_WIDTH) * gauss
        value = gauss * env
        ef[:, at] = gauss1 * env + gauss * env1
        ee[:, at] = value * inverse
        f2s[:, at] = gauss2 * env + 2.0 * gauss1 * env1 + gauss * env2
        for c in range(3):
            hs[8 * c : 8 * c + 8, at] = head[c]
        hs[24:32, at] = inverse
        terms = [value, value * head[0], value * head[1], value * head[2]]
        totals = [t + v[:, :lanes] + v[:, lanes:] for t, v in zip(totals, terms)]
    return [t + pltpu.roll(t, lanes // 2, 1) for t in totals]


def edge_rows(alpha, beta, ef, ee, f2s, hs, e8, lanes):
    for j in range(ef.shape[1] // lanes):
        at = slice(j * lanes, (j + 1) * lanes)
        head = [hs[8 * c : 8 * c + 8, at] for c in range(3)]
        inverse = hs[24:32, at]
        slope_k, even_k, second = ef[:, at], ee[:, at], f2s[:, at]
        even1 = (slope_k - even_k) * inverse
        even2 = (second - 2.0 * even1) * inverse

        sums = stacked_sums(
            [alpha * slope_k, alpha * second]
            + [beta[c] * even1 for c in range(3)]
            + [beta[c] * even2 for c in range(3)]
        )
        first, bend_r = sums[0:1], sums[1:2]
        turn = [sums[2 + c : 3 + c] for c in range(3)]
        twist = [sums[5 + c : 6 + c] for c in range(3)]
        inv1 = inverse[0:1]
        h1 = [head[c][0:1] for c in range(3)]
        radius = 1.0 / inv1
        line = h1[0] * turn[0] + h1[1] * turn[1] + h1[2] * turn[2]
        isotropic = first * inv1 + line
        radial = bend_r + (h1[0] * twist[0] + h1[1] * twist[1] + h1[2] * twist[2]) * radius - isotropic
        e8[:, at] = jnp.concatenate(h1 + [isotropic, radial] + turn, axis=0)


def channel_lift(flow, rad_t, vec_t, mix_t, qs, qr, lanes, atoms):
    channels, basis = rad_t.shape
    lower = lax.broadcasted_iota(jnp.int32, (channels, lanes), 1) < atoms
    lift0 = 2.0 * jnp.where(lower, flow[0], flow[2])
    lift1 = 2.0 * flow[1]
    for i in range(2 * basis):
        k = i % basis
        if i < basis:
            side = jnp.where(lower, jnp.broadcast_to(rad_t[:, k : k + 1], lower.shape), lift1 * vec_t[:, k : k + 1])
        else:
            side = lift0 * vec_t[:, k : k + 1]
        lifted = dot_split(mix_t, side)
        qs[:, i * lanes : (i + 1) * lanes] = lifted
        qr[:, i * lanes : (i + 1) * lanes] = pltpu.roll(lifted, atoms, 1)


def descriptor_curvature(vec, u, bend, qs, qr, bd, both, pmat, rmat, lanes, atoms):
    basis = vec.shape[0]
    pairs = 2 * basis
    channels = bend.shape[0]
    bd[...] = bend
    low_row = lax.broadcasted_iota(jnp.int32, (basis, lanes), 1) < atoms
    for k in range(basis):
        both[k] = 2.0 * dot32(vec * vec[k : k + 1, :], u)

    def block(i, column):
        accs = None
        for tile in range(channels // 8):
            rows = slice(8 * tile, 8 * tile + 8)
            weight = bd[rows, :]
            left = [
                qs[rows, pl.ds(pl.multiple_of((i + d) * lanes, lanes), lanes)] * weight for d in range(2)
            ]
            columns = [slice((column + k) * lanes, (column + k + 1) * lanes) for k in range(basis)]
            right = [ref[rows, at] for ref in (qs, qr) for at in columns]
            terms = [l * r for l in left for r in right]
            accs = terms if accs is None else [a + t for a, t in zip(accs, terms)]
        return [stacked_sums(accs[q * basis : (q + 1) * basis]) for q in range(4)]

    def put(i, column, tiles):
        for d in range(2):
            at = pl.ds(pl.multiple_of((i + d) * pairs + column, basis), basis)
            pmat[at, :] = tiles[2 * d]
            rmat[at, :] = tiles[2 * d + 1]

    def upper_step(step, carry):
        i = 2 * step
        tiles = block(i, 0)
        for d in range(2):
            tiles[2 * d] = tiles[2 * d] + jnp.where(low_row, 0.0, both[i + d])
        put(i, 0, tiles)
        return carry

    def lower_step(step, carry):
        i = 2 * step + basis
        tiles = block(i, 0)
        put(i, 0, tiles)
        for d in range(2):
            pmat[pl.ds(i + d, basis, pairs), :] = tiles[2 * d]
            rmat[pl.ds(i + d, basis, pairs), :] = pltpu.roll(tiles[2 * d + 1], atoms, 1)
        tiles = block(i, basis)
        for d in range(2):
            tiles[2 * d] = tiles[2 * d] + both[i + d - basis]
        put(i, basis, tiles)
        return carry

    lax.fori_loop(0, basis // 2, upper_step, 0, unroll=True)
    lax.fori_loop(0, basis // 2, lower_step, 0, unroll=True)


def first_kernel(
    sides, wide, from_mate, from_other, dm, valid, w_rad, w_vec, w_mix, rad_t, vec_t, mix_t, out_t,
    out_m, out_o, out_x, partial, cext, pext, index, ef, ee, e8, pmat, rmat,
    mv, eo, xs, sx, cs, f2s, hs, qs, qr, bd, both,
    *, vectors, atoms, halo,
):
    half3 = 3 * vectors // 2
    vec3 = 2 * half3
    lanes = 2 * atoms
    rows = beside(
        wide[...],
        unpack_rows(from_mate[...], halo),
        unpack_rows(from_other[...], halo),
        sides[1] == 0,
        3.0 * atoms,
    )
    cext[...] = rows[:vec3]
    pext[...] = rows[vec3 : 2 * vec3]
    base = 2 * vec3
    places = jnp.round(rows[base + 3 : base + 4]).astype(jnp.int32)
    index[...] = jnp.broadcast_to(places, index.shape)
    shape = (8, rows.shape[1])
    place = jnp.concatenate([rows[base : base + 8], jnp.zeros(shape, jnp.float32)], axis=0)
    parts16 = jnp.concatenate([split(rows[:vec3], 2), split(place, 3)], axis=0)
    descr = gather_edges(parts16, dm, valid, mv, ef, ee, f2s, hs, vec3, lanes)
    contract(mv, ef, ee, lambda c, at: hs[8 * c : 8 * c + 8, at], xs, sx, atoms)

    rad, vec, mix = w_rad[...], w_vec[...], w_mix[...]
    radt, vect, mixt, outt = rad_t[...], vec_t[...], mix_t[...], out_t[:, 0:1]
    flow = [dot32(vect, descr[c + 1]) for c in range(3)]
    mixed = dot32(radt, descr[0]) + flow[0] * flow[0] + flow[1] * flow[1] + flow[2] * flow[2]
    hidden = dot_split(mixt, mixed)
    gate = 1.0 / (1.0 + jnp.exp(-hidden))
    slope = gate * (1.0 + hidden * (1.0 - gate)) * outt
    bend = gate * (1.0 - gate) * (2.0 + hidden * (1.0 - 2.0 * gate)) * outt
    u = dot_split(mix, slope)
    alpha = dot32(rad, u)
    beta = [2.0 * dot32(vec, flow[c] * u) for c in range(3)]
    edge_rows(alpha, beta, ef, ee, f2s, hs, e8, lanes)
    channel_lift(flow, radt, vect, mixt, qs, qr, lanes, atoms)
    descriptor_curvature(vec, u, bend, qs, qr, bd, both, pmat, rmat, lanes, atoms)

    result = spread(dm, ef, ee, e8, pmat, rmat, mv, eo, xs, sx, cs, atoms)
    partial[...] = result
    store_patch((out_m, out_o, out_x), result, pick_matrix(places, 9 * atoms), atoms)


def product(left, right, vectors):
    total = jnp.zeros((vectors, vectors), jnp.float32)
    for c in range(3):
        total = total + dot_split(component(left, c, vectors), component(right, c, vectors), NT)
    return total


def sums_kernel(cext, pext, partial, out, *, vectors, atoms):
    old_c, old_p, new = cext[...], pext[...], partial[...]
    cw, pw = product(old_c, new, vectors), product(old_p, new, vectors)
    own_c, own_p = old_c[:, :atoms], old_p[:, :atoms]
    cc, cp, pp = (product(*pair, vectors) for pair in ((own_c, own_c), (own_c, own_p), (own_p, own_p)))
    out[...] = jnp.concatenate([with_diagonal(cw, pp), pw, cp, join_triangles(cc, pp)], axis=1)


def pair_kernel(resid, partial, out, *, vectors, atoms):
    r = resid[...]
    own = r[:, :atoms]
    lanes = out.shape[1]
    rr, ry = product(own, own, vectors), product(r, partial[...], vectors)
    out[...] = jnp.concatenate([flatten(rr, lanes), flatten(ry, lanes)], axis=0)


def second_kernel(order, own, mate, other, *rest, vectors, atoms, total_rows, chips):
    far, rest = rest[: chips - 2], rest[chips - 2 :]
    cext, pext, index, dm, ef, ee, e8, pmat, rmat, out_m, out_o, out_x, shared, rown, rext, partial = rest[:16]
    mv, eo, xs, sx, cs, patch, ring = rest[16:]
    half3 = 3 * vectors // 2
    vec3 = 2 * half3
    tail = 3 * half3
    pick = pick_matrix(index[0:1, :], 9 * atoms)
    ring[order[0]] = own[tail:, :]
    ring[order[1]] = other[tail:, :]
    for i, part in enumerate(far):
        ring[order[2 + i]] = part[...]
    total = ring[0]
    for i in range(1, chips):
        total = total + ring[i]
    total = total * (1.0 / total_rows)
    v = vectors
    held, pw, cp, joined = (total[:, i * v : (i + 1) * v] for i in range(4))
    coef = jnp.concatenate([from_lower(held), pw], axis=0)
    cc, pp = from_lower(joined), from_upper(joined, held)
    gram_old = jnp.concatenate(
        [jnp.concatenate([cc, cp], axis=1), jnp.concatenate([cp.T, pp], axis=1)], axis=0
    )
    shared[...] = jnp.concatenate([gram_old, coef, jnp.zeros_like(coef)], axis=1)

    for x, ref in enumerate((mate, own, other)):
        for y in range(3):
            at = (3 * y + x) * atoms
            patch[:, at : at + atoms] = unpack(ref[y * half3 : (y + 1) * half3, :], atoms)
    both = dot16(split(patch[...], 2), pick)
    work = both[:vec3] + both[vec3:]
    turned = coef.T
    resid = work - jnp.concatenate(
        [
            dot_split(
                turned,
                jnp.concatenate(
                    [component(cext[...], c, vectors), component(pext[...], c, vectors)], axis=0
                ),
            )
            for c in range(3)
        ],
        axis=0,
    )
    rown[...] = pack(resid[:, :atoms])
    rext[...] = resid
    parts16 = split(resid, 2)
    wide = 4 * atoms
    for j in range(dm.shape[1] // wide):
        at = slice(j * wide, (j + 1) * wide)
        got = dot16(parts16, dm[:, at])
        mv[:, at] = got[:vec3] + got[vec3:]
    contract(mv, ef, ee, lambda c, at: e8[c : c + 1, at], xs, sx, atoms)
    rows = spread(dm, ef, ee, e8, pmat, rmat, mv, eo, xs, sx, cs, atoms)
    partial[...] = rows
    store_patch((out_m, out_o, out_x), rows, pick, atoms)


def send_sums(pairs, yy, out):
    count, lanes = pairs.shape[0] // 2, pairs.shape[1]
    size = yy.shape[0]
    rr, ry = unflatten(pairs[:count], size), unflatten(pairs[count:], size)
    sent = jnp.concatenate(
        [flatten(join_triangles(rr, yy), lanes), flatten(with_diagonal(ry, yy), lanes)], axis=0
    )
    out[...] = jnp.broadcast_to(sent[None], out.shape)


def gram_kernel(pairs, y0, ym, yo, out, yown, *, vectors, atoms):
    work = y0[...] + ym[...] + yo[...]
    yown[...] = work
    y = unpack(work, atoms)
    send_sums(pairs[...], product(y, y, vectors), out)


def column_gram_kernel(order, own, mate, other, far, out, yown, held, *, vectors, atoms):
    half3 = 3 * vectors // 2

    def part(ref, which):
        return ref[which * half3 : (which + 1) * half3, :]

    m, zero, o = 0, 1, 2
    mine = part(own, zero) + part(mate, m) + part(other, o)
    yown[...] = mine
    held[order[0]] = mine
    held[order[1]] = part(mate, zero) + part(own, m) + part(far, o)
    held[order[2]] = part(other, zero) + part(far, m) + part(own, o)
    held[order[3]] = part(far, zero) + part(other, m) + part(mate, o)
    y = jnp.concatenate([unpack(held[i], atoms) for i in range(4)], axis=1)
    tail = 3 * half3
    pairs = (own[tail:, :] + mate[tail:, :]) + (other[tail:, :] + far[tail:, :])
    send_sums(pairs, product(y, y, vectors), out)


def cholesky(matrix, lower, *extra):
    size = matrix.shape[0]
    rows, cols = rows_and_cols(size)
    unit = (rows == cols).astype(jnp.float32)
    work = jnp.concatenate([matrix, unit, *extra], axis=1)
    columns = [jnp.broadcast_to(lower[:, k : k + 1], work.shape) for k in range(size)]
    lines = []
    for j in range(0, size, 2):
        first, second = columns[j], columns[j + 1]
        a, b, d = first[j : j + 1], first[j + 1 : j + 2], second[j + 1 : j + 2]
        det = a * d - b * b
        inverse = 1.0 / det
        ai, bi, di = a * inverse, b * inverse, d * inverse
        keep = (j + 2) // 8 * 8
        for k in range(j + 2, size):
            x0, x1 = first[k : k + 1], second[k : k + 1]
            low = columns[k][keep:] - (first[keep:] * (di * x0 - bi * x1) + second[keep:] * (ai * x1 - bi * x0))
            columns[k] = jnp.concatenate([columns[k][:keep], low], axis=0) if keep else low
        r0, r1 = work[j : j + 1], work[j + 1 : j + 2]
        work = work - (first * (di * r0 - bi * r1) + second * (ai * r1 - bi * r0))
        lines += [r0 * root_inverse(a), (r1 - (b / a) * r0) * root_inverse(det / a)]
    done = jnp.concatenate(lines, axis=0)
    upper = jnp.where(cols >= rows, done[:, :size], 0.0)
    return [upper] + [done[:, i * size : (i + 1) * size] for i in range(1, 2 + len(extra))]


def root_inverse(value):
    guess = lax.rsqrt(value)
    return guess * (1.5 - 0.5 * value * guess * guess)


def final_kernel(got, sums, rown, yown, cown, blocks, factors, *, vectors, atoms, total_rows):
    devices = got.shape[0]
    v = vectors
    total = got[0]
    for i in range(1, devices):
        total = total + got[i]
    total = total * (1.0 / total_rows)
    count = total.shape[0] // 2
    joined, held = unflatten(total[:count], v), unflatten(total[count:], v)
    rr, ry, yy = from_lower(joined), from_lower(held), from_upper(joined, held)
    shared = sums[...]
    gram_old, coef1 = shared[:, : 2 * v], shared[:, 2 * v : 3 * v]
    rows, cols = rows_and_cols(v)
    unit = (rows == cols).astype(jnp.float32)
    left = coef1 - dot32(gram_old, coef1)
    wr = rr + dot32(coef1, left, TN)
    fixed = yy + dot32(wr, dot32(gram_old[:v, :v] - 2.0 * unit, wr), TN)

    upper1, inv1, along, cross = cholesky(rr, joined, ry, left[:v].T)
    mixed = dot32(cross, wr)
    gram2 = fixed + dot32(
        jnp.concatenate([along, mixed], axis=0), jnp.concatenate([mixed - along, along], axis=0), TN
    )
    upper2, inv2 = cholesky(gram2, gram2)
    factors[0] = upper1.T
    factors[1] = jnp.where(rows >= cols, dot32(inv1, upper2, NT), 0.0)
    r, y, old = unpack(rown[...], atoms), unpack(yown[...], atoms), cown[0 : 3 * vectors, 0:atoms]
    back = dot32(along, inv1, TN)
    weights = jnp.concatenate([-back, -wr.T], axis=1)
    for c in range(3):
        parts = [component(part, c, vectors) for part in (r, old)]
        blocks[0, c] = dot32(inv1, parts[0])
        rest = component(y, c, vectors) + dot32(weights, jnp.concatenate(parts, axis=0))
        blocks[1, c] = dot32(inv2, rest)


def mates(count):
    mate = [i ^ 1 for i in range(count)]
    other = [(i - 1) % count if i % 2 == 0 else (i + 1) % count for i in range(count)]
    return mate, other


def fetch(values, axis, sources):
    return lax.ppermute(values, axis, [(s, i) for i, s in enumerate(sources)])


def vmem_call(kernel, outs, scratch=(), scalars=0, flops=1 << 20):
    def call(*operands):
        spaces = [pltpu.SMEM] * scalars + [pltpu.VMEM] * (len(operands) - scalars)
        return pl.pallas_call(
            kernel,
            out_shape=outs,
            in_specs=[pl.BlockSpec(memory_space=s) for s in spaces],
            out_specs=jax.tree.map(lambda _: pl.BlockSpec(memory_space=pltpu.VMEM), outs),
            scratch_shapes=list(scratch),
            compiler_params=pltpu.CompilerParams(vmem_limit_bytes=VMEM_BYTES),
            cost_estimate=pl.CostEstimate(flops=flops, bytes_accessed=1 << 16, transcendentals=0),
        )(*operands)

    return call


def laid(shape, pieces):
    total = None
    for row, lane, piece in pieces:
        rows, lanes = piece.shape
        edges = ((row, shape[0] - row - rows), (lane, shape[1] - lane - lanes))
        placed = jnp.pad(piece, edges).astype(jnp.float32)
        total = placed if total is None else total + placed
    return total


def f32(*shape):
    return jax.ShapeDtypeStruct(shape, jnp.float32)


def shards(positions, block_prev, block_cur, neighbours, counts, x_lists, y_lists, w_radial, w_vector, w_mix, w_out):
    vectors, _, atoms = block_cur.shape
    halo = x_lists.shape[2]
    slots = neighbours.shape[0]
    basis, channels = w_radial.shape
    n_x, n_y = lax.axis_size("gx"), lax.axis_size("gy")
    total_rows = 3.0 * atoms * n_x * n_y
    half3 = 3 * vectors // 2
    vec3 = 3 * vectors
    lanes = 2 * atoms
    edges = slots * atoms
    extended = atoms + 4 * halo
    pairs = 2 * basis
    mate_x, other_x = mates(n_x)
    mate_y, other_y = mates(n_y)
    at_x, at_y = lax.axis_index("gx"), lax.axis_index("gy")
    sides = jnp.stack([at_x % 2, at_y % 2]).astype(jnp.int32)
    own_rows = vec3 + 8

    cur = block_cur.transpose(1, 0, 2).reshape(vec3, atoms)
    prev = block_prev.transpose(1, 0, 2).reshape(vec3, atoms)
    slab = f32(own_rows, lanes)
    all_rows = 2 * vec3 + 8

    table = laid(
        (own_rows, lanes),
        [
            (0, 0, cur),
            (0, atoms, prev),
            (vec3, 0, positions),
            (vec3 + 3, 0, x_lists[0]),
            (vec3 + 5, 0, y_lists[0]),
        ],
    )
    mate1 = fetch(table, "gx", mate_x)
    other1 = fetch(table, "gx", other_x)
    after = channels + 2 * basis + 8
    fixed = laid(
        (after + slots + 8, channels),
        [
            (0, 0, w_mix),
            (channels, 0, w_radial),
            (channels + basis, 0, w_vector),
            (channels + 2 * basis, 0, w_out[None]),
            (after, 0, neighbours),
            (after + slots, 0, counts[None]),
        ],
    )
    rad_shape, mix_shape, turned_shape = f32(basis, channels), f32(channels, channels), f32(channels, basis)
    dm, valid, rad, vec, mix, rad_t, vec_t, mix_t, out_t = vmem_call(
        functools.partial(prepare_kernel, slots=slots, atoms=atoms),
        [
            jax.ShapeDtypeStruct((extended, edges), jnp.bfloat16),
            f32(8, edges),
            rad_shape,
            rad_shape,
            mix_shape,
            turned_shape,
            turned_shape,
            mix_shape,
            f32(channels, 8),
        ],
        flops=1 << 24,
    )(fixed)
    to_mate, to_other, wide = vmem_call(
        functools.partial(select_kernel, atoms=atoms, halo=halo),
        [slab, slab, f32(all_rows, atoms + 2 * halo)],
        scalars=1,
    )(sides, table, mate1, other1)
    mate2 = fetch(to_mate, "gy", mate_y)
    other2 = fetch(to_other, "gy", other_y)

    work_scratch = [
        pltpu.VMEM((vec3, edges), jnp.float32),
        pltpu.VMEM((vec3, edges), jnp.float32),
        pltpu.VMEM((pairs, vectors, lanes), jnp.float32),
        pltpu.VMEM((pairs, vectors, lanes), jnp.float32),
        pltpu.VMEM((2 * pairs, vectors, lanes), jnp.float32),
    ]
    first = vmem_call(
        functools.partial(first_kernel, vectors=vectors, atoms=atoms, halo=halo),
        [
            f32(3 * half3, lanes),
            f32(3 * half3, lanes),
            f32(3 * half3, lanes),
            f32(vec3, extended),
            f32(vec3, extended),
            f32(vec3, extended),
            jax.ShapeDtypeStruct((8, extended), jnp.int32),
            f32(basis, edges),
            f32(basis, edges),
            f32(8, edges),
            f32(pairs * pairs, lanes),
            f32(pairs * pairs, lanes),
        ],
        work_scratch
        + [
            pltpu.VMEM((basis, edges), jnp.float32),
            pltpu.VMEM((32, edges), jnp.float32),
            pltpu.VMEM((channels, pairs * lanes), jnp.float32),
            pltpu.VMEM((channels, pairs * lanes), jnp.float32),
            pltpu.VMEM((channels, lanes), jnp.float32),
            pltpu.VMEM((basis, basis, lanes), jnp.float32),
        ],
        scalars=1,
        flops=1 << 31,
    )
    part_m, part_0, part_o, partial, cext, pext, index, ef, ee, e8, pmat, rmat = first(
        sides, wide, mate2, other2, dm, valid, rad, vec, mix, rad_t, vec_t, mix_t, out_t
    )

    back_m = fetch(part_m, "gx", mate_x)
    back_o = fetch(part_o, "gx", other_x)
    local = vmem_call(
        functools.partial(sums_kernel, vectors=vectors, atoms=atoms), f32(vectors, lanes), flops=1 << 25
    )(cext, pext, partial)
    local = local + fetch(local, "gx", mate_x)
    folded = part_0 + back_m + back_o
    f_m, f_0, f_o = folded[:half3], folded[half3 : 2 * half3], folded[2 * half3 :]

    far_m = [other_y[m] for m in mate_y]
    far_o = [mate_y[o] for o in other_y]
    got_m = fetch(jnp.concatenate([f_0, f_m, local]), "gy", mate_y)
    got_o = fetch(jnp.concatenate([f_0, f_o, local]), "gy", other_y)
    if far_m == far_o:
        got_2 = fetch(jnp.concatenate([f_m, f_o, local]), "gy", far_m)
        far_mate, far_other = got_2[half3 : 2 * half3], got_2[:half3]
        sums = (local + got_m[2 * half3 :]) + (got_o[2 * half3 :] + got_2[2 * half3 :])
    else:
        far_mate = fetch(f_o, "gy", far_m)
        far_other = fetch(f_m, "gy", far_o)
        terms = [local] + [
            fetch(local, "gy", [(i + d) % n_y for i in range(n_y)]) for d in range(1, n_y)
        ]
        sums = jnp.sum(jnp.roll(jnp.stack(terms), at_y, axis=0), axis=0)
    w_m = got_m[:half3] + f_m + far_mate
    w_0 = f_0 + got_m[half3 : 2 * half3] + got_o[half3 : 2 * half3]
    w_o = got_o[:half3] + far_other + f_o
    column = jnp.concatenate([w_m, w_0, w_o, sums])

    col_m = fetch(column, "gx", mate_x)
    col_o = fetch(column, "gx", other_x)
    pairs_x = n_x // 2
    steps = [d for d in range(1, pairs_x - 1)]
    far = [
        fetch(sums, "gx", [(i + 2 * d) % n_x if i % 2 == 0 else (i - 2 * d) % n_x for i in range(n_x)])
        for d in steps
    ]
    chip, way = at_x // 2, 1 - 2 * (at_x % 2)
    order = jnp.stack([(chip + d * way) % pairs_x for d in [0, -1] + steps]).astype(jnp.int32)

    second = vmem_call(
        functools.partial(second_kernel, vectors=vectors, atoms=atoms, total_rows=total_rows, chips=pairs_x),
        [
            f32(3 * half3, lanes),
            f32(3 * half3, lanes),
            f32(3 * half3, lanes),
            f32(2 * vectors, lanes),
            f32(half3, lanes),
            f32(vec3, extended),
            f32(vec3, extended),
        ],
        work_scratch
        + [pltpu.VMEM((vec3, 9 * atoms), jnp.float32), pltpu.VMEM((pairs_x, vectors, lanes), jnp.float32)],
        scalars=1,
        flops=1 << 30,
    )
    part_m, part_0, part_o, shared, rown, rext, partial = second(
        order, column, col_m, col_o, *far, cext, pext, index, dm, ef, ee, e8, pmat, rmat
    )
    back_m = fetch(part_m, "gx", mate_x)
    back_o = fetch(part_o, "gx", other_x)
    sent_rows = 2 * vectors * vectors // lanes
    pairs_rr = vmem_call(
        functools.partial(pair_kernel, vectors=vectors, atoms=atoms), f32(sent_rows, lanes), flops=1 << 25
    )(rext, partial)
    folded = part_0 + back_m + back_o
    if far_m == far_o:
        share = jnp.concatenate([folded, pairs_rr])
        got_m = fetch(share, "gy", mate_y)
        got_o = fetch(share, "gy", other_y)
        got_2 = fetch(share, "gy", far_m)
        order = jnp.stack([at_y, at_y ^ 1, (at_y - 1 + 2 * (at_y % 2)) % 4, (at_y + 2) % 4])
        spread_sums, yown = vmem_call(
            functools.partial(column_gram_kernel, vectors=vectors, atoms=atoms),
            [f32(n_x, sent_rows, lanes), f32(half3, lanes)],
            [pltpu.VMEM((4, half3, lanes), jnp.float32)],
            scalars=1,
        )(order.astype(jnp.int32), share, got_m, got_o, got_2)
        got = lax.all_to_all(spread_sums, "gx", 0, 0)
    else:
        y_m = fetch(folded[:half3], "gy", mate_y)
        y_o = fetch(folded[2 * half3 :], "gy", other_y)
        spread_sums, yown = vmem_call(
            functools.partial(gram_kernel, vectors=vectors, atoms=atoms),
            [f32(n_x * n_y, sent_rows, lanes), f32(half3, lanes)],
        )(pairs_rr, folded[half3 : 2 * half3], y_m, y_o)
        got = lax.all_to_all(spread_sums, ("gx", "gy"), 0, 0)
    blocks, factors = vmem_call(
        functools.partial(final_kernel, vectors=vectors, atoms=atoms, total_rows=total_rows),
        [f32(2, 3, vectors, atoms), f32(2, vectors, vectors)],
    )(got, shared, rown, yown, table)
    return blocks.transpose(0, 2, 1, 3), factors


def solution(mesh):
    placed = (
        P(None, ("gx", "gy")),
        P(None, None, ("gx", "gy")),
        P(None, None, ("gx", "gy")),
        P(None, ("gx", "gy")),
        P(("gx", "gy")),
        P(("gx", "gy"), None, None),
        P(("gx", "gy"), None, None),
        P(),
        P(),
        P(),
        P(),
    )
    return jax.shard_map(
        shards,
        mesh=mesh,
        in_specs=placed,
        out_specs=(P(None, None, None, ("gx", "gy")), P()),
        check_vma=False,
    )
```

```python
import functools

import jax
import jax.numpy as jnp
from jax import lax
from jax.experimental import pallas as pl
from jax.experimental.pallas import tpu as pltpu
from jax.sharding import PartitionSpec as P

SOFTEN = 0.25
CUTOFF = 5.0
GAUSS_WIDTH = 2.0
EXACT = lax.Precision.HIGHEST
VMEM_BYTES = 48 * 1024 * 1024
NN = (((1,), (0,)), ((), ()))
NT = (((1,), (1,)), ((), ()))
TN = (((0,), (0,)), ((), ()))


def dot16(left, right, dims=NN):
    return lax.dot_general(left, right, dims, preferred_element_type=jnp.float32)


def dot32(left, right, dims=NN):
    return lax.dot_general(
        left, right, dims, precision=EXACT, preferred_element_type=jnp.float32
    )


def split(values, parts):
    pieces = []
    for _ in range(parts):
        piece = values.astype(jnp.bfloat16)
        pieces.append(piece)
        values = values - piece.astype(jnp.float32)
    return jnp.concatenate(pieces, axis=0)


def dot_split(left, right, dims=NN):
    if dims == TN:
        left = left.T
        dims = NN
    rows = left.shape[0]
    both = split(left, 2)
    high = right.astype(jnp.bfloat16)
    low = (right - high.astype(jnp.float32)).astype(jnp.bfloat16)
    first = dot16(both, high, dims)
    return first[:rows] + first[rows:] + dot16(both[:rows], low, dims)


def component(block, comp, vectors):
    return block[comp * vectors : (comp + 1) * vectors]


def unpack(packed, atoms):
    return jnp.concatenate([packed[:, :atoms], packed[:, atoms:]], axis=0)


def pack(rows):
    half = rows.shape[0] // 2
    return jnp.concatenate([rows[:half], rows[half:]], axis=1)


def pick_matrix(index_row, patch_rows):
    extended = index_row.shape[1]
    rows = lax.broadcasted_iota(jnp.int32, (patch_rows, extended), 0)
    return (rows == index_row).astype(jnp.float32).astype(jnp.bfloat16)


def select(rows, *names):
    picks = jnp.concatenate(names, axis=1)
    hits = lax.broadcasted_iota(jnp.int32, (rows.shape[1], picks.shape[1]), 0) == picks
    tail = 16
    count = rows.shape[0] - tail
    parts = jnp.concatenate([split(rows[:count], 2), split(rows[count:], 3)], axis=0)
    got = dot16(parts, hits.astype(jnp.float32).astype(jnp.bfloat16))
    last = got[2 * count :]
    return jnp.concatenate(
        [
            got[:count] + got[count : 2 * count],
            last[:tail] + (last[tail : 2 * tail] + last[2 * tail :]),
        ],
        axis=0,
    )


def rows_and_cols(size):
    return (
        lax.broadcasted_iota(jnp.int32, (size, size), 0),
        lax.broadcasted_iota(jnp.int32, (size, size), 1),
    )


def join_triangles(lower, upper):
    rows, cols = rows_and_cols(lower.shape[0])
    return jnp.where(rows >= cols, lower, upper)


def with_diagonal(lower, source):
    size = lower.shape[0]
    rows, cols = rows_and_cols(size)
    line = jnp.sum(jnp.where(rows == cols, source, 0.0), axis=0, keepdims=True)
    upper = jnp.where(rows == 0, line, jnp.where((rows == 1) & (cols == size - 1), source[0:1, 0:1], 0.0))
    return jnp.where(rows >= cols, lower, upper)


def from_lower(joined):
    rows, cols = rows_and_cols(joined.shape[0])
    strict = jnp.where(rows > cols, joined, 0.0)
    return jnp.where(rows >= cols, joined, 0.0) + strict.T


def from_upper(joined, holder):
    size = joined.shape[0]
    rows, cols = rows_and_cols(size)
    strict = jnp.where(rows < cols, joined, 0.0)
    line = jnp.where(cols[0:1] >= 1, holder[0:1], holder[1:2, size - 1 : size])
    return strict + strict.T + jnp.where(rows == cols, line, 0.0)


def flatten(square, lanes):
    size = square.shape[0]
    rows = size * size // lanes
    return jnp.concatenate([square[i * rows : (i + 1) * rows] for i in range(lanes // size)], axis=1)


def unflatten(flat, size):
    return jnp.concatenate(
        [flat[:, i * size : (i + 1) * size] for i in range(flat.shape[1] // size)], axis=0
    )


def rows_of(tile, comp, vectors):
    return slice(comp * vectors + tile * 8, comp * vectors + tile * 8 + 8)


def contract(mv_ref, ef_ref, ee_ref, head_of, xs_ref, sx_ref, atoms):
    lanes = 2 * atoms
    basis, edges = ef_ref.shape
    vectors = mv_ref.shape[0] // 3
    pairs = 2 * basis
    lower = lax.broadcasted_iota(jnp.int32, (8, lanes), 1) < atoms
    for tile in range(vectors // 8):
        acc = [jnp.zeros((8, lanes), jnp.float32)] * (4 * basis)
        for j in range(edges // lanes):
            at = slice(j * lanes, (j + 1) * lanes)
            m = [mv_ref[rows_of(tile, c, vectors), at] for c in range(3)]
            head = [head_of(c, at) for c in range(3)]
            u = head[0] * m[0] + head[1] * m[1] + head[2] * m[2]
            along = [head[c] * u for c in range(3)]
            across = [m[c] - along[c] for c in range(3)]
            for k in range(basis):
                slope = ef_ref[k : k + 1, at]
                even = ee_ref[k : k + 1, at]
                acc[k] = acc[k] + slope * u
                for c in range(3):
                    i = (c + 1) * basis + k
                    acc[i] = acc[i] + (slope * along[c] + even * across[c])
        for i in range(pairs):
            a, b = acc[i], acc[i + pairs]
            x = jnp.where(lower, a, b) + pltpu.roll(jnp.where(lower, b, a), atoms, 1)
            xs_ref[i, tile * 8 : tile * 8 + 8, :] = x
            sx_ref[i, tile * 8 : tile * 8 + 8, :] = pltpu.roll(x, atoms, 1)


def spread(dm_ref, ef_ref, ee_ref, e8_ref, p_ref, r_ref, mv_ref, eo_ref, xs_ref, sx_ref, cs_ref, atoms):
    lanes = 2 * atoms
    basis, edges = ef_ref.shape
    groups = edges // lanes
    vec3 = mv_ref.shape[0]
    vectors = vec3 // 3
    pairs = 2 * basis
    tiles = vectors // 8
    wide_lower = lax.broadcasted_iota(jnp.int32, (8 * tiles, lanes), 1) < atoms

    def mix_step(kappa, carry):
        at = pl.ds(pl.multiple_of(kappa * pairs, pairs), pairs)
        straight = p_ref[at, :]
        crossed = r_ref[at, :]
        y = jnp.zeros((8 * tiles, lanes), jnp.float32)
        for i in range(pairs):
            y = y + straight[i : i + 1, :] * xs_ref[i] + crossed[i : i + 1, :] * sx_ref[i]
        turned = pltpu.roll(y, atoms, 1)
        cs_ref[kappa] = jnp.where(wide_lower, y, turned)
        cs_ref[kappa + pairs] = jnp.where(wide_lower, turned, y)
        return carry

    lax.fori_loop(0, pairs, mix_step, 0, unroll=8)

    total = None
    step = max(groups // 4, 1)
    for first in range(0, groups, step):
        for tile in range(tiles):
            coeff = [cs_ref[i, tile * 8 : tile * 8 + 8, :] for i in range(4 * basis)]
            for j in range(first, first + step):
                at = slice(j * lanes, (j + 1) * lanes)
                m = [mv_ref[rows_of(tile, c, vectors), at] for c in range(3)]
                row = [e8_ref[i : i + 1, at] for i in range(8)]
                head, turn = row[0:3], row[5:8]
                u = head[0] * m[0] + head[1] * m[1] + head[2] * m[2]
                radial = row[4] * u + (turn[0] * m[0] + turn[1] * m[1] + turn[2] * m[2])
                sums, evens = [None] * 3, [None] * 3
                for k in range(basis):
                    slope = ef_ref[k : k + 1, at]
                    even = ee_ref[k : k + 1, at]
                    radial = radial + slope * coeff[k]
                    for c in range(3):
                        i = (c + 1) * basis + k
                        more, plus = slope * coeff[i], even * coeff[i]
                        sums[c] = more if k == 0 else sums[c] + more
                        evens[c] = plus if k == 0 else evens[c] + plus
                for c in range(3):
                    radial = radial + head[c] * (sums[c] - evens[c])
                for c in range(3):
                    eo_ref[rows_of(tile, c, vectors), at] = (
                        evens[c] + head[c] * radial + (row[3] * m[c] + turn[c] * u)
                    )
        at = slice(first * lanes, (first + step) * lanes)
        both = dot16(split(eo_ref[:, at], 2), dm_ref[:, at], NT)
        part = both[:vec3] + both[vec3:]
        total = part if total is None else total + part
    return total


def stacked_sums(parts):
    row = lax.broadcasted_iota(jnp.int32, parts[0].shape, 0)

    def moved(values, by):
        return values + pltpu.roll(values, by % 8, 0)

    upper = row < 4
    fours = [
        jnp.where(upper, parts[i], parts[i + 4]) + pltpu.roll(jnp.where(upper, parts[i + 4], parts[i]), 4, 0)
        for i in range(4)
    ]
    twos = [jnp.where(row % 4 < 2, moved(fours[i], -2), moved(fours[i + 2], 2)) for i in range(2)]
    return jnp.where(row % 2 < 1, moved(twos[0], -1), moved(twos[1], 1))


def store_patch(outs, extended_rows, pick, atoms):
    vec3 = extended_rows.shape[0]
    half3 = vec3 // 2
    both = dot16(split(extended_rows, 2), pick, NT)
    patch = both[:vec3] + both[vec3:]
    for x in range(3):
        for y in range(3):
            at = (3 * y + x) * atoms
            tile = patch[:, at : at + atoms]
            outs[x][y * half3 : (y + 1) * half3, 0:atoms] = tile[:half3]
            outs[x][y * half3 : (y + 1) * half3, atoms : 2 * atoms] = tile[half3:]


def emit(even, rows, lists, to_mate, to_other):
    low, high = lists
    got = select(rows, jnp.where(even, low, high), jnp.where(even, high, low))
    halo = low.shape[1]
    vec3 = (rows.shape[0] - 8) // 2
    for which, out in enumerate((to_mate, to_other)):
        part = got[:, which * halo : (which + 1) * halo]
        out[0:vec3, :] = jnp.concatenate([part[0:vec3], part[vec3 : 2 * vec3]], axis=1)
        out[vec3:, :] = jnp.concatenate([part[2 * vec3 :], jnp.zeros_like(part[2 * vec3 :])], axis=1)


def unpack_rows(block, width):
    vec3 = block.shape[0] - 8
    return jnp.concatenate([block[:vec3, 0:width], block[:vec3, width : 2 * width], block[vec3:, 0:width]], axis=0)


def table_rows(table, atoms):
    rows = unpack_rows(table, atoms)
    count = rows.shape[0]
    number = lax.broadcasted_iota(jnp.int32, (8, atoms), 1).astype(jnp.float32)
    line = lax.broadcasted_iota(jnp.int32, (8, atoms), 0)
    last = jnp.where(line < 3, rows[count - 8 :], jnp.where(line == 3, number, 0.0))
    return jnp.concatenate([rows[: count - 8], last], axis=0)


def table_lists(table, line, halo):
    base = table.shape[0] - 8 + line
    rows = table[base : base + 2, 0:halo].astype(jnp.int32)
    return rows[0:1], rows[1:2]


def beside(rows, mate, other, even, step):
    line = rows.shape[0] - 5
    at = (lax.broadcasted_iota(jnp.int32, (rows.shape[0], 1), 0) == line).astype(jnp.float32) * step
    other = other + 2.0 * at
    return jnp.concatenate(
        [rows + at, jnp.where(even, other, mate), jnp.where(even, mate, other)], axis=1
    )


def select_kernel(sides, table, from_mate, from_other, to_mate, to_other, wide, *, atoms, halo):
    even = sides[0] == 0
    picked = []
    for ref, flip in ((from_mate[...], False), (from_other[...], True)):
        low, high = table_lists(ref, 3, halo)
        names = jnp.where(even, low, high) if flip else jnp.where(even, high, low)
        picked.append(select(table_rows(ref, atoms), names))
    got = beside(table_rows(table[...], atoms), *picked, even, float(atoms))
    wide[...] = got
    emit(sides[1] == 0, got, table_lists(table[...], 5, halo), to_mate, to_other)


def prepare_kernel(table, dm, valid, rad, vec, mix, rad_t, vec_t, mix_t, out_t, *, slots, atoms):
    lanes = 2 * atoms
    basis, channels = rad.shape
    starts = [0, channels, channels + basis, channels + 2 * basis, channels + 2 * basis + 8]
    w_mix, w_rad, w_vec = (table[starts[i] : starts[i + 1], :] for i in range(3))
    w_out = table[starts[3] : starts[4], :]
    ints = table[starts[4] :, 0:atoms].astype(jnp.int32)
    nb, count = ints[:slots], ints[slots : slots + 1]
    difference_matrix(dm, nb, dm.shape[0], atoms)
    lane = lax.broadcasted_iota(jnp.int32, (8, lanes), 1)
    first = jnp.where(lane < atoms, 0, slots // 2)
    limit = jnp.concatenate([count, count], axis=1)
    for j in range(slots // 2):
        valid[:, j * lanes : (j + 1) * lanes] = (first + j < limit).astype(jnp.float32)
    rad[...] = w_rad
    vec[...] = w_vec
    mix[...] = w_mix
    rad_t[...] = w_rad.T
    vec_t[...] = w_vec.T
    mix_t[...] = w_mix.T
    out_t[...] = w_out.T


def difference_matrix(dm_ref, nb, extended, atoms):
    half = nb.shape[0] // 2
    lanes = 2 * atoms
    paired = jnp.concatenate([nb[:half], nb[half:]], axis=1)
    rows = lax.broadcasted_iota(jnp.int32, (extended, lanes), 0)
    lane = lax.broadcasted_iota(jnp.int32, (extended, lanes), 1)
    own = (rows == jnp.where(lane < atoms, lane, lane - atoms)).astype(jnp.float32)
    for j in range(half):
        hit = (rows == paired[j : j + 1, :]).astype(jnp.float32)
        dm_ref[:, j * lanes : (j + 1) * lanes] = (hit - own).astype(jnp.bfloat16)


def gather_edges(parts16, dm, valid, mv, ef, ee, f2s, hs, vec3, lanes):
    basis, edges = ef.shape
    wide = 2 * lanes
    cut = 1.0 / (CUTOFF * CUTOFF)
    centre = (lax.broadcasted_iota(jnp.int32, (basis, wide), 0).astype(jnp.float32) + 0.5) * (CUTOFF / basis)
    totals = [jnp.zeros((basis, lanes), jnp.float32) for _ in range(4)]
    for j in range(edges // wide):
        at = slice(j * wide, (j + 1) * wide)
        got = dot16(parts16, dm[:, at])
        mv[:, at] = got[:vec3] + got[vec3 : 2 * vec3]
        third = 2 * vec3
        delta = got[third : third + 8] + got[third + 16 : third + 24] + got[third + 32 : third + 40]
        d = [jnp.broadcast_to(delta[c : c + 1], delta.shape) for c in range(3)]
        squared = d[0] * d[0] + d[1] * d[1] + d[2] * d[2] + SOFTEN
        radius = jnp.sqrt(squared)
        inverse = 1.0 / radius
        head = [d[c] * inverse for c in range(3)]
        tau = jnp.maximum(1.0 - squared * cut, 0.0)
        env = tau * tau * tau
        env1 = (-6.0 * cut) * radius * tau * tau
        env2 = (24.0 * cut * cut) * squared * tau - (6.0 * cut) * tau * tau
        off = radius - centre
        gauss = jnp.exp(-GAUSS_WIDTH * off * off) * valid[:, at]
        gauss1 = (-2.0 * GAUSS_WIDTH) * off * gauss
        gauss2 = (4.0 * GAUSS_WIDTH * GAUSS_WIDTH * off * off - 2.0 * GAUSS_WIDTH) * gauss
        value = gauss * env
        ef[:, at] = gauss1 * env + gauss * env1
        ee[:, at] = value * inverse
        f2s[:, at] = gauss2 * env + 2.0 * gauss1 * env1 + gauss * env2
        for c in range(3):
            hs[8 * c : 8 * c + 8, at] = head[c]
        hs[24:32, at] = inverse
        terms = [value, value * head[0], value * head[1], value * head[2]]
        totals = [t + v[:, :lanes] + v[:, lanes:] for t, v in zip(totals, terms)]
    return [t + pltpu.roll(t, lanes // 2, 1) for t in totals]


def edge_rows(alpha, beta, ef, ee, f2s, hs, e8, lanes):
    for j in range(ef.shape[1] // lanes):
        at = slice(j * lanes, (j + 1) * lanes)
        head = [hs[8 * c : 8 * c + 8, at] for c in range(3)]
        inverse = hs[24:32, at]
        slope_k, even_k, second = ef[:, at], ee[:, at], f2s[:, at]
        even1 = (slope_k - even_k) * inverse
        even2 = (second - 2.0 * even1) * inverse

        sums = stacked_sums(
            [alpha * slope_k, alpha * second]
            + [beta[c] * even1 for c in range(3)]
            + [beta[c] * even2 for c in range(3)]
        )
        first, bend_r = sums[0:1], sums[1:2]
        turn = [sums[2 + c : 3 + c] for c in range(3)]
        twist = [sums[5 + c : 6 + c] for c in range(3)]
        inv1 = inverse[0:1]
        h1 = [head[c][0:1] for c in range(3)]
        radius = 1.0 / inv1
        line = h1[0] * turn[0] + h1[1] * turn[1] + h1[2] * turn[2]
        isotropic = first * inv1 + line
        radial = bend_r + (h1[0] * twist[0] + h1[1] * twist[1] + h1[2] * twist[2]) * radius - isotropic
        e8[:, at] = jnp.concatenate(h1 + [isotropic, radial] + turn, axis=0)


def channel_lift(flow, rad_t, vec_t, mix_t, qs, qr, lanes, atoms):
    channels, basis = rad_t.shape
    lower = lax.broadcasted_iota(jnp.int32, (channels, lanes), 1) < atoms
    lift0 = 2.0 * jnp.where(lower, flow[0], flow[2])
    lift1 = 2.0 * flow[1]
    for i in range(2 * basis):
        k = i % basis
        if i < basis:
            side = jnp.where(lower, jnp.broadcast_to(rad_t[:, k : k + 1], lower.shape), lift1 * vec_t[:, k : k + 1])
        else:
            side = lift0 * vec_t[:, k : k + 1]
        lifted = dot_split(mix_t, side)
        qs[:, i * lanes : (i + 1) * lanes] = lifted
        qr[:, i * lanes : (i + 1) * lanes] = pltpu.roll(lifted, atoms, 1)


def descriptor_curvature(vec, u, bend, qs, qr, bd, both, pmat, rmat, lanes, atoms):
    basis = vec.shape[0]
    pairs = 2 * basis
    channels = bend.shape[0]
    bd[...] = bend
    low_row = lax.broadcasted_iota(jnp.int32, (basis, lanes), 1) < atoms
    for k in range(basis):
        both[k] = 2.0 * dot_split(vec * vec[k : k + 1, :], u)

    def block(i, column):
        accs = None
        for tile in range(channels // 8):
            rows = slice(8 * tile, 8 * tile + 8)
            weight = bd[rows, :]
            left = [
                qs[rows, pl.ds(pl.multiple_of((i + d) * lanes, lanes), lanes)] * weight for d in range(2)
            ]
            columns = [slice((column + k) * lanes, (column + k + 1) * lanes) for k in range(basis)]
            right = [ref[rows, at] for ref in (qs, qr) for at in columns]
            terms = [l * r for l in left for r in right]
            accs = terms if accs is None else [a + t for a, t in zip(accs, terms)]
        return [stacked_sums(accs[q * basis : (q + 1) * basis]) for q in range(4)]

    def put(i, column, tiles):
        for d in range(2):
            at = pl.ds(pl.multiple_of((i + d) * pairs + column, basis), basis)
            pmat[at, :] = tiles[2 * d]
            rmat[at, :] = tiles[2 * d + 1]

    def upper_step(step, carry):
        i = 2 * step
        tiles = block(i, 0)
        for d in range(2):
            tiles[2 * d] = tiles[2 * d] + jnp.where(low_row, 0.0, both[i + d])
        put(i, 0, tiles)
        return carry

    def lower_step(step, carry):
        i = 2 * step + basis
        tiles = block(i, 0)
        put(i, 0, tiles)
        for d in range(2):
            pmat[pl.ds(i + d, basis, pairs), :] = tiles[2 * d]
            rmat[pl.ds(i + d, basis, pairs), :] = pltpu.roll(tiles[2 * d + 1], atoms, 1)
        tiles = block(i, basis)
        for d in range(2):
            tiles[2 * d] = tiles[2 * d] + both[i + d - basis]
        put(i, basis, tiles)
        return carry

    lax.fori_loop(0, basis // 2, upper_step, 0, unroll=True)
    lax.fori_loop(0, basis // 2, lower_step, 0, unroll=True)


def first_kernel(
    sides, wide, from_mate, from_other, dm, valid, w_rad, w_vec, w_mix, rad_t, vec_t, mix_t, out_t,
    out_m, out_o, out_x, partial, cext, pext, index, ef, ee, e8, pmat, rmat,
    mv, eo, xs, sx, cs, f2s, hs, qs, qr, bd, both,
    *, vectors, atoms, halo,
):
    half3 = 3 * vectors // 2
    vec3 = 2 * half3
    lanes = 2 * atoms
    rows = beside(
        wide[...],
        unpack_rows(from_mate[...], halo),
        unpack_rows(from_other[...], halo),
        sides[1] == 0,
        3.0 * atoms,
    )
    cext[...] = rows[:vec3]
    pext[...] = rows[vec3 : 2 * vec3]
    base = 2 * vec3
    places = jnp.round(rows[base + 3 : base + 4]).astype(jnp.int32)
    index[...] = jnp.broadcast_to(places, index.shape)
    shape = (8, rows.shape[1])
    place = jnp.concatenate([rows[base : base + 8], jnp.zeros(shape, jnp.float32)], axis=0)
    parts16 = jnp.concatenate([split(rows[:vec3], 2), split(place, 3)], axis=0)
    descr = gather_edges(parts16, dm, valid, mv, ef, ee, f2s, hs, vec3, lanes)
    contract(mv, ef, ee, lambda c, at: hs[8 * c : 8 * c + 8, at], xs, sx, atoms)

    rad, vec, mix = w_rad[...], w_vec[...], w_mix[...]
    radt, vect, mixt, outt = rad_t[...], vec_t[...], mix_t[...], out_t[:, 0:1]
    flow = [dot_split(vect, descr[c + 1]) for c in range(3)]
    mixed = dot_split(radt, descr[0]) + flow[0] * flow[0] + flow[1] * flow[1] + flow[2] * flow[2]
    hidden = dot_split(mixt, mixed)
    gate = 1.0 / (1.0 + jnp.exp(-hidden))
    slope = gate * (1.0 + hidden * (1.0 - gate)) * outt
    bend = gate * (1.0 - gate) * (2.0 + hidden * (1.0 - 2.0 * gate)) * outt
    u = dot_split(mix, slope)
    alpha = dot_split(rad, u)
    beta = [2.0 * dot_split(vec, flow[c] * u) for c in range(3)]
    edge_rows(alpha, beta, ef, ee, f2s, hs, e8, lanes)
    channel_lift(flow, radt, vect, mixt, qs, qr, lanes, atoms)
    descriptor_curvature(vec, u, bend, qs, qr, bd, both, pmat, rmat, lanes, atoms)

    result = spread(dm, ef, ee, e8, pmat, rmat, mv, eo, xs, sx, cs, atoms)
    partial[...] = result
    store_patch((out_m, out_o, out_x), result, pick_matrix(places, 9 * atoms), atoms)


def product(left, right, vectors):
    total = jnp.zeros((vectors, vectors), jnp.float32)
    for c in range(3):
        total = total + dot_split(component(left, c, vectors), component(right, c, vectors), NT)
    return total


def sums_kernel(cext, pext, partial, out, *, vectors, atoms):
    old_c, old_p, new = cext[...], pext[...], partial[...]
    cw, pw = product(old_c, new, vectors), product(old_p, new, vectors)
    own_c, own_p = old_c[:, :atoms], old_p[:, :atoms]
    cc, cp, pp = (product(*pair, vectors) for pair in ((own_c, own_c), (own_c, own_p), (own_p, own_p)))
    out[...] = jnp.concatenate([with_diagonal(cw, pp), pw, cp, join_triangles(cc, pp)], axis=1)


def pair_kernel(resid, partial, out, *, vectors, atoms):
    r = resid[...]
    own = r[:, :atoms]
    lanes = out.shape[1]
    rr, ry = product(own, own, vectors), product(r, partial[...], vectors)
    out[...] = jnp.concatenate([flatten(rr, lanes), flatten(ry, lanes)], axis=0)


def second_kernel(order, own, mate, other, *rest, vectors, atoms, total_rows, chips):
    far, rest = rest[: chips - 2], rest[chips - 2 :]
    cext, pext, index, dm, ef, ee, e8, pmat, rmat, out_m, out_o, out_x, shared, rown, rext, partial = rest[:16]
    mv, eo, xs, sx, cs, patch, ring = rest[16:]
    half3 = 3 * vectors // 2
    vec3 = 2 * half3
    tail = 3 * half3
    pick = pick_matrix(index[0:1, :], 9 * atoms)
    ring[order[0]] = own[tail:, :]
    ring[order[1]] = other[tail:, :]
    for i, part in enumerate(far):
        ring[order[2 + i]] = part[...]
    total = ring[0]
    for i in range(1, chips):
        total = total + ring[i]
    total = total * (1.0 / total_rows)
    v = vectors
    held, pw, cp, joined = (total[:, i * v : (i + 1) * v] for i in range(4))
    coef = jnp.concatenate([from_lower(held), pw], axis=0)
    cc, pp = from_lower(joined), from_upper(joined, held)
    gram_old = jnp.concatenate(
        [jnp.concatenate([cc, cp], axis=1), jnp.concatenate([cp.T, pp], axis=1)], axis=0
    )
    shared[...] = jnp.concatenate([gram_old, coef, jnp.zeros_like(coef)], axis=1)

    for x, ref in enumerate((mate, own, other)):
        for y in range(3):
            at = (3 * y + x) * atoms
            patch[:, at : at + atoms] = unpack(ref[y * half3 : (y + 1) * half3, :], atoms)
    both = dot16(split(patch[...], 2), pick)
    work = both[:vec3] + both[vec3:]
    turned = coef.T
    resid = work - jnp.concatenate(
        [
            dot_split(
                turned,
                jnp.concatenate(
                    [component(cext[...], c, vectors), component(pext[...], c, vectors)], axis=0
                ),
            )
            for c in range(3)
        ],
        axis=0,
    )
    rown[...] = pack(resid[:, :atoms])
    rext[...] = resid
    parts16 = split(resid, 2)
    wide = 4 * atoms
    for j in range(dm.shape[1] // wide):
        at = slice(j * wide, (j + 1) * wide)
        got = dot16(parts16, dm[:, at])
        mv[:, at] = got[:vec3] + got[vec3:]
    contract(mv, ef, ee, lambda c, at: e8[c : c + 1, at], xs, sx, atoms)
    rows = spread(dm, ef, ee, e8, pmat, rmat, mv, eo, xs, sx, cs, atoms)
    partial[...] = rows
    store_patch((out_m, out_o, out_x), rows, pick, atoms)


def send_sums(pairs, yy, out):
    count, lanes = pairs.shape[0] // 2, pairs.shape[1]
    size = yy.shape[0]
    rr, ry = unflatten(pairs[:count], size), unflatten(pairs[count:], size)
    sent = jnp.concatenate(
        [flatten(join_triangles(rr, yy), lanes), flatten(with_diagonal(ry, yy), lanes)], axis=0
    )
    out[...] = jnp.broadcast_to(sent[None], out.shape)


def gram_kernel(pairs, y0, ym, yo, out, yown, *, vectors, atoms):
    work = y0[...] + ym[...] + yo[...]
    yown[...] = work
    y = unpack(work, atoms)
    send_sums(pairs[...], product(y, y, vectors), out)


def column_gram_kernel(order, own, mate, other, far, out, yown, held, *, vectors, atoms):
    half3 = 3 * vectors // 2

    def part(ref, which):
        return ref[which * half3 : (which + 1) * half3, :]

    m, zero, o = 0, 1, 2
    mine = part(own, zero) + part(mate, m) + part(other, o)
    yown[...] = mine
    held[order[0]] = mine
    held[order[1]] = part(mate, zero) + part(own, m) + part(far, o)
    held[order[2]] = part(other, zero) + part(far, m) + part(own, o)
    held[order[3]] = part(far, zero) + part(other, m) + part(mate, o)
    y = jnp.concatenate([unpack(held[i], atoms) for i in range(4)], axis=1)
    tail = 3 * half3
    pairs = (own[tail:, :] + mate[tail:, :]) + (other[tail:, :] + far[tail:, :])
    send_sums(pairs, product(y, y, vectors), out)


def cholesky(matrix, lower, *extra):
    size = matrix.shape[0]
    rows, cols = rows_and_cols(size)
    unit = (rows == cols).astype(jnp.float32)
    work = jnp.concatenate([matrix, unit, *extra], axis=1)
    columns = [jnp.broadcast_to(lower[:, k : k + 1], work.shape) for k in range(size)]
    lines = []
    for j in range(0, size, 2):
        first, second = columns[j], columns[j + 1]
        a, b, d = first[j : j + 1], first[j + 1 : j + 2], second[j + 1 : j + 2]
        det = a * d - b * b
        inverse = 1.0 / det
        ai, bi, di = a * inverse, b * inverse, d * inverse
        keep = (j + 2) // 8 * 8
        for k in range(j + 2, size):
            x0, x1 = first[k : k + 1], second[k : k + 1]
            low = columns[k][keep:] - (first[keep:] * (di * x0 - bi * x1) + second[keep:] * (ai * x1 - bi * x0))
            columns[k] = jnp.concatenate([columns[k][:keep], low], axis=0) if keep else low
        r0, r1 = work[j : j + 1], work[j + 1 : j + 2]
        work = work - (first * (di * r0 - bi * r1) + second * (ai * r1 - bi * r0))
        lines += [r0 * root_inverse(a), (r1 - (b / a) * r0) * root_inverse(det / a)]
    done = jnp.concatenate(lines, axis=0)
    upper = jnp.where(cols >= rows, done[:, :size], 0.0)
    return [upper] + [done[:, i * size : (i + 1) * size] for i in range(1, 2 + len(extra))]


def root_inverse(value):
    guess = lax.rsqrt(value)
    return guess * (1.5 - 0.5 * value * guess * guess)


def final_kernel(got, sums, rown, yown, cown, blocks, factors, *, vectors, atoms, total_rows):
    devices = got.shape[0]
    v = vectors
    total = got[0]
    for i in range(1, devices):
        total = total + got[i]
    total = total * (1.0 / total_rows)
    count = total.shape[0] // 2
    joined, held = unflatten(total[:count], v), unflatten(total[count:], v)
    rr, ry, yy = from_lower(joined), from_lower(held), from_upper(joined, held)
    shared = sums[...]
    gram_old, coef1 = shared[:, : 2 * v], shared[:, 2 * v : 3 * v]
    rows, cols = rows_and_cols(v)
    unit = (rows == cols).astype(jnp.float32)
    left = coef1 - dot32(gram_old, coef1)
    wr = rr + dot32(coef1, left, TN)
    fixed = yy + dot32(wr, dot32(gram_old[:v, :v] - 2.0 * unit, wr), TN)

    upper1, inv1, along, cross = cholesky(rr, joined, ry, left[:v].T)
    mixed = dot32(cross, wr)
    gram2 = fixed + dot32(
        jnp.concatenate([along, mixed], axis=0), jnp.concatenate([mixed - along, along], axis=0), TN
    )
    upper2, inv2 = cholesky(gram2, gram2)
    factors[0] = upper1.T
    factors[1] = jnp.where(rows >= cols, dot32(inv1, upper2, NT), 0.0)
    r, y, old = unpack(rown[...], atoms), unpack(yown[...], atoms), cown[0 : 3 * vectors, 0:atoms]
    back = dot32(along, inv1, TN)
    weights = jnp.concatenate([-back, -wr.T], axis=1)
    for c in range(3):
        parts = [component(part, c, vectors) for part in (r, old)]
        blocks[0, c] = dot32(inv1, parts[0])
        rest = component(y, c, vectors) + dot32(weights, jnp.concatenate(parts, axis=0))
        blocks[1, c] = dot32(inv2, rest)


def mates(count):
    mate = [i ^ 1 for i in range(count)]
    other = [(i - 1) % count if i % 2 == 0 else (i + 1) % count for i in range(count)]
    return mate, other


def fetch(values, axis, sources):
    return lax.ppermute(values, axis, [(s, i) for i, s in enumerate(sources)])


def vmem_call(kernel, outs, scratch=(), scalars=0, flops=1 << 20):
    def call(*operands):
        spaces = [pltpu.SMEM] * scalars + [pltpu.VMEM] * (len(operands) - scalars)
        return pl.pallas_call(
            kernel,
            out_shape=outs,
            in_specs=[pl.BlockSpec(memory_space=s) for s in spaces],
            out_specs=jax.tree.map(lambda _: pl.BlockSpec(memory_space=pltpu.VMEM), outs),
            scratch_shapes=list(scratch),
            compiler_params=pltpu.CompilerParams(vmem_limit_bytes=VMEM_BYTES),
            cost_estimate=pl.CostEstimate(flops=flops, bytes_accessed=1 << 16, transcendentals=0),
        )(*operands)

    return call


def laid(shape, pieces):
    total = None
    for row, lane, piece in pieces:
        rows, lanes = piece.shape
        edges = ((row, shape[0] - row - rows), (lane, shape[1] - lane - lanes))
        placed = jnp.pad(piece, edges).astype(jnp.float32)
        total = placed if total is None else total + placed
    return total


def f32(*shape):
    return jax.ShapeDtypeStruct(shape, jnp.float32)


def shards(positions, block_prev, block_cur, neighbours, counts, x_lists, y_lists, w_radial, w_vector, w_mix, w_out):
    vectors, _, atoms = block_cur.shape
    halo = x_lists.shape[2]
    slots = neighbours.shape[0]
    basis, channels = w_radial.shape
    n_x, n_y = lax.axis_size("gx"), lax.axis_size("gy")
    total_rows = 3.0 * atoms * n_x * n_y
    half3 = 3 * vectors // 2
    vec3 = 3 * vectors
    lanes = 2 * atoms
    edges = slots * atoms
    extended = atoms + 4 * halo
    pairs = 2 * basis
    mate_x, other_x = mates(n_x)
    mate_y, other_y = mates(n_y)
    at_x, at_y = lax.axis_index("gx"), lax.axis_index("gy")
    sides = jnp.stack([at_x % 2, at_y % 2]).astype(jnp.int32)
    own_rows = vec3 + 8

    cur = block_cur.transpose(1, 0, 2).reshape(vec3, atoms)
    prev = block_prev.transpose(1, 0, 2).reshape(vec3, atoms)
    slab = f32(own_rows, lanes)
    all_rows = 2 * vec3 + 8

    table = laid(
        (own_rows, lanes),
        [
            (0, 0, cur),
            (0, atoms, prev),
            (vec3, 0, positions),
            (vec3 + 3, 0, x_lists[0]),
            (vec3 + 5, 0, y_lists[0]),
        ],
    )
    mate1 = fetch(table, "gx", mate_x)
    other1 = fetch(table, "gx", other_x)
    after = channels + 2 * basis + 8
    fixed = laid(
        (after + slots + 8, channels),
        [
            (0, 0, w_mix),
            (channels, 0, w_radial),
            (channels + basis, 0, w_vector),
            (channels + 2 * basis, 0, w_out[None]),
            (after, 0, neighbours),
            (after + slots, 0, counts[None]),
        ],
    )
    rad_shape, mix_shape, turned_shape = f32(basis, channels), f32(channels, channels), f32(channels, basis)
    dm, valid, rad, vec, mix, rad_t, vec_t, mix_t, out_t = vmem_call(
        functools.partial(prepare_kernel, slots=slots, atoms=atoms),
        [
            jax.ShapeDtypeStruct((extended, edges), jnp.bfloat16),
            f32(8, edges),
            rad_shape,
            rad_shape,
            mix_shape,
            turned_shape,
            turned_shape,
            mix_shape,
            f32(channels, 8),
        ],
        flops=1 << 24,
    )(fixed)
    to_mate, to_other, wide = vmem_call(
        functools.partial(select_kernel, atoms=atoms, halo=halo),
        [slab, slab, f32(all_rows, atoms + 2 * halo)],
        scalars=1,
    )(sides, table, mate1, other1)
    mate2 = fetch(to_mate, "gy", mate_y)
    other2 = fetch(to_other, "gy", other_y)

    work_scratch = [
        pltpu.VMEM((vec3, edges), jnp.float32),
        pltpu.VMEM((vec3, edges), jnp.float32),
        pltpu.VMEM((pairs, vectors, lanes), jnp.float32),
        pltpu.VMEM((pairs, vectors, lanes), jnp.float32),
        pltpu.VMEM((2 * pairs, vectors, lanes), jnp.float32),
    ]
    first = vmem_call(
        functools.partial(first_kernel, vectors=vectors, atoms=atoms, halo=halo),
        [
            f32(3 * half3, lanes),
            f32(3 * half3, lanes),
            f32(3 * half3, lanes),
            f32(vec3, extended),
            f32(vec3, extended),
            f32(vec3, extended),
            jax.ShapeDtypeStruct((8, extended), jnp.int32),
            f32(basis, edges),
            f32(basis, edges),
            f32(8, edges),
            f32(pairs * pairs, lanes),
            f32(pairs * pairs, lanes),
        ],
        work_scratch
        + [
            pltpu.VMEM((basis, edges), jnp.float32),
            pltpu.VMEM((32, edges), jnp.float32),
            pltpu.VMEM((channels, pairs * lanes), jnp.float32),
            pltpu.VMEM((channels, pairs * lanes), jnp.float32),
            pltpu.VMEM((channels, lanes), jnp.float32),
            pltpu.VMEM((basis, basis, lanes), jnp.float32),
        ],
        scalars=1,
        flops=1 << 31,
    )
    part_m, part_0, part_o, partial, cext, pext, index, ef, ee, e8, pmat, rmat = first(
        sides, wide, mate2, other2, dm, valid, rad, vec, mix, rad_t, vec_t, mix_t, out_t
    )

    back_m = fetch(part_m, "gx", mate_x)
    back_o = fetch(part_o, "gx", other_x)
    local = vmem_call(
        functools.partial(sums_kernel, vectors=vectors, atoms=atoms), f32(vectors, lanes), flops=1 << 25
    )(cext, pext, partial)
    local = local + fetch(local, "gx", mate_x)
    folded = part_0 + back_m + back_o
    f_m, f_0, f_o = folded[:half3], folded[half3 : 2 * half3], folded[2 * half3 :]

    far_m = [other_y[m] for m in mate_y]
    far_o = [mate_y[o] for o in other_y]
    got_m = fetch(jnp.concatenate([f_0, f_m, local]), "gy", mate_y)
    got_o = fetch(jnp.concatenate([f_0, f_o, local]), "gy", other_y)
    if far_m == far_o:
        got_2 = fetch(jnp.concatenate([f_m, f_o, local]), "gy", far_m)
        far_mate, far_other = got_2[half3 : 2 * half3], got_2[:half3]
        sums = (local + got_m[2 * half3 :]) + (got_o[2 * half3 :] + got_2[2 * half3 :])
    else:
        far_mate = fetch(f_o, "gy", far_m)
        far_other = fetch(f_m, "gy", far_o)
        terms = [local] + [
            fetch(local, "gy", [(i + d) % n_y for i in range(n_y)]) for d in range(1, n_y)
        ]
        sums = jnp.sum(jnp.roll(jnp.stack(terms), at_y, axis=0), axis=0)
    w_m = got_m[:half3] + f_m + far_mate
    w_0 = f_0 + got_m[half3 : 2 * half3] + got_o[half3 : 2 * half3]
    w_o = got_o[:half3] + far_other + f_o
    column = jnp.concatenate([w_m, w_0, w_o, sums])

    col_m = fetch(column, "gx", mate_x)
    col_o = fetch(column, "gx", other_x)
    pairs_x = n_x // 2
    steps = [d for d in range(1, pairs_x - 1)]
    far = [
        fetch(sums, "gx", [(i + 2 * d) % n_x if i % 2 == 0 else (i - 2 * d) % n_x for i in range(n_x)])
        for d in steps
    ]
    chip, way = at_x // 2, 1 - 2 * (at_x % 2)
    order = jnp.stack([(chip + d * way) % pairs_x for d in [0, -1] + steps]).astype(jnp.int32)

    second = vmem_call(
        functools.partial(second_kernel, vectors=vectors, atoms=atoms, total_rows=total_rows, chips=pairs_x),
        [
            f32(3 * half3, lanes),
            f32(3 * half3, lanes),
            f32(3 * half3, lanes),
            f32(2 * vectors, lanes),
            f32(half3, lanes),
            f32(vec3, extended),
            f32(vec3, extended),
        ],
        work_scratch
        + [pltpu.VMEM((vec3, 9 * atoms), jnp.float32), pltpu.VMEM((pairs_x, vectors, lanes), jnp.float32)],
        scalars=1,
        flops=1 << 30,
    )
    part_m, part_0, part_o, shared, rown, rext, partial = second(
        order, column, col_m, col_o, *far, cext, pext, index, dm, ef, ee, e8, pmat, rmat
    )
    back_m = fetch(part_m, "gx", mate_x)
    back_o = fetch(part_o, "gx", other_x)
    sent_rows = 2 * vectors * vectors // lanes
    pairs_rr = vmem_call(
        functools.partial(pair_kernel, vectors=vectors, atoms=atoms), f32(sent_rows, lanes), flops=1 << 25
    )(rext, partial)
    folded = part_0 + back_m + back_o
    if far_m == far_o:
        share = jnp.concatenate([folded, pairs_rr])
        got_m = fetch(share, "gy", mate_y)
        got_o = fetch(share, "gy", other_y)
        got_2 = fetch(share, "gy", far_m)
        order = jnp.stack([at_y, at_y ^ 1, (at_y - 1 + 2 * (at_y % 2)) % 4, (at_y + 2) % 4])
        spread_sums, yown = vmem_call(
            functools.partial(column_gram_kernel, vectors=vectors, atoms=atoms),
            [f32(n_x, sent_rows, lanes), f32(half3, lanes)],
            [pltpu.VMEM((4, half3, lanes), jnp.float32)],
            scalars=1,
        )(order.astype(jnp.int32), share, got_m, got_o, got_2)
        got = lax.all_to_all(spread_sums, "gx", 0, 0)
    else:
        y_m = fetch(folded[:half3], "gy", mate_y)
        y_o = fetch(folded[2 * half3 :], "gy", other_y)
        spread_sums, yown = vmem_call(
            functools.partial(gram_kernel, vectors=vectors, atoms=atoms),
            [f32(n_x * n_y, sent_rows, lanes), f32(half3, lanes)],
        )(pairs_rr, folded[half3 : 2 * half3], y_m, y_o)
        got = lax.all_to_all(spread_sums, ("gx", "gy"), 0, 0)
    blocks, factors = vmem_call(
        functools.partial(final_kernel, vectors=vectors, atoms=atoms, total_rows=total_rows),
        [f32(2, 3, vectors, atoms), f32(2, vectors, vectors)],
    )(got, shared, rown, yown, table)
    return blocks.transpose(0, 2, 1, 3), factors


def solution(mesh):
    placed = (
        P(None, ("gx", "gy")),
        P(None, None, ("gx", "gy")),
        P(None, None, ("gx", "gy")),
        P(None, ("gx", "gy")),
        P(("gx", "gy")),
        P(("gx", "gy"), None, None),
        P(("gx", "gy"), None, None),
        P(),
        P(),
        P(),
        P(),
    )
    return jax.shard_map(
        shards,
        mesh=mesh,
        in_specs=placed,
        out_specs=(P(None, None, None, ("gx", "gy")), P()),
        check_vma=False,
    )
```
